32 devices in a mesh: seq: 4 (over y, x), exp: 4 (over z), fsdp: 2 (over core).
Axes of the slice: x: 2, y: 2, z: 4, core: 2. Of those that a mesh axis runs over, the one named last changes fastest.
Arguments:
- tokens: bfloat16 [8, 1024, 2048], P(('exp', 'fsdp'), 'seq')
- cotangent: bfloat16 [8, 1024, 2048], P(('exp', 'fsdp'), 'seq'), may hold values from -6 to 6
- expert_ids: int32 [8, 1024, 8], P(('exp', 'fsdp'), 'seq'), may hold values from 0 to 15, all different within a row; in each aligned block of 256 rows (0 to 255, 256 to 511, ..., all dimensions but the last counted through in order) at most 144 rows name the same one
- segment_ids: int32 [8, 1024], P(('exp', 'fsdp')), may hold values from 0 to 6, as said below
- norm_gains: bfloat16 [2048, 4], P(('seq', 'exp', 'fsdp')), may hold values from 0.099609375 to 1.8984375
- w_qkv: bfloat16 [2048, 6144], P(('seq', 'exp', 'fsdp')), may hold values from -0.125 to 0.125
- w_out: bfloat16 [2048, 2048], P(('seq', 'exp', 'fsdp')), may hold values from -1 to 1
- router: bfloat16 [2048, 16], P(('seq', 'exp', 'fsdp')), may hold values from -0.0625 to 0.0625
- expert_in: bfloat16 [2048, 16, 2048], P(('seq', 'fsdp'), 'exp'), may hold values from -0.125 to 0.125
- expert_out: bfloat16 [2048, 16, 1024], P(('seq', 'fsdp'), 'exp'), may hold values from -1.5 to 1.5
Outputs:
- output: bfloat16 [8, 1024, 2048], P(('exp', 'fsdp'), 'seq')
- grad_tokens: float32 [8, 1024, 2048], P(('exp', 'fsdp'), 'seq')
- grad_norm_gains: float32 [2048, 4], P(('seq', 'exp', 'fsdp'))
- grad_w_qkv: float32 [2048, 6144], P(('seq', 'exp', 'fsdp'))
- grad_w_out: float32 [2048, 2048], P(('seq', 'exp', 'fsdp'))
- grad_router: float32 [2048, 16], P(('seq', 'exp', 'fsdp'))
- grad_expert_in: float32 [2048, 16, 2048], P(('seq', 'fsdp'), 'exp')
- grad_expert_out: float32 [2048, 16, 1024], P(('seq', 'fsdp'), 'exp')
The draws below stay inside these ranges and needn't reach their ends.
Inputs may be any that keep to these rules, and one draw needn't show every extreme that they name: `expert_ids`: each token's 8 ids differ. Among the tokens of one device (aligned blocks of 256 positions) no id appears more than 144 times, and in some blocks one appears exactly 144 times. `segment_ids`: Non-decreasing along each sequence, starting at 0; every sequence holds exactly seven documents.
All inputs are finite; a program needn't handle non-finite values.
Results may differ from the reference program's by a relative error of at most 0.018.
Values may be sent and summed in bfloat16 or wider, within the bound.
No kernel may reach another device: no remote copies, remote signals or barrier semaphores. Data moves between devices by JAX's collectives and lax.ppermute only.
A program may use at most 448 MiB of HBM per device.

```python
import math
import jax
import jax.numpy as jnp
import numpy as np
from jax import lax

D = 2048
HEADS = 16
HEAD_DIM = 128
FF = 1024
TOP = 8
ATT_BLOCK = 256
TOK_DEV = 256
EXPERTS = 16
CAP = 144
LEN = 1024
SEQS = 8
N_SEQ = 4


def draw_tokens(key, part):
    key = jax.random.fold_in(key, 17)
    base_key, column_key, row_key = jax.random.split(key, 3)
    columns = jnp.exp(jax.random.uniform(column_key, (D,), jnp.float32, -1.15, 1.15))
    row_scales = jnp.exp(jax.random.uniform(row_key, (SEQS, LEN, 1), jnp.float32, -0.7, 0.7))
    values = jax.random.truncated_normal(base_key, -4.0, 4.0, (SEQS, LEN, D), jnp.float32)
    return (0.6 * values * columns * row_scales).astype(jnp.bfloat16)


def pick_two(key, valid, position):
    scores = jax.random.randint(key, valid.shape, 0, 65536).astype(jnp.int32) * LEN + position
    scores = jnp.where(valid, scores, jnp.int32(2 ** 30))
    chosen = jnp.sort(scores, axis=1)[:, :2] % LEN
    return jnp.any(position[:, :, None] == chosen[:, None, :], axis=-1)


def draw_segment_ids(key, part):
    key = jax.random.fold_in(key, 29)
    start_key, finish_key, head_key, tail_key = jax.random.split(key, 4)
    margin = LEN // 8
    starts = jax.random.randint(start_key, (SEQS, 1), margin // 2, margin).astype(jnp.int32)
    finish = jax.random.randint(finish_key, (SEQS, 1), LEN - margin, LEN - margin // 2).astype(jnp.int32)
    position = jnp.broadcast_to(jnp.arange(LEN, dtype=jnp.int32)[None, :], (SEQS, LEN))
    head_cuts = pick_two(head_key, (position >= 1) & (position < starts), position)
    tail_cuts = pick_two(tail_key, position > finish + 1, position)
    boundary = (position == starts) | (position == finish + 1) | head_cuts | tail_cuts
    return jnp.cumsum(boundary.astype(jnp.int32), axis=1).astype(jnp.int32)


def levels(rng, shape, pieces, least, top_value):
    gain = 1.0
    for axis_at, blocks in pieces:
        heights = jax.random.uniform(jax.random.fold_in(jax.random.fold_in(rng, 6), axis_at), (blocks,), jnp.float32, least / len(pieces), top_value / len(pieces))
        gain = gain * jnp.repeat(jnp.exp(heights), shape[axis_at] // blocks).reshape((-1,) + (1,) * (len(shape) - 1 - axis_at))
    return gain


def assign_block(stream_key, own, number, rows, number_of, top, limit, skew):
    ranking = jax.random.permutation(stream_key, number_of)
    crowded, usual = load_shares(number_of, rows * top, limit, skew, True), load_shares(number_of, rows * top, limit, skew, False)
    places = jnp.arange(number_of)

    def named(tallies, offset_by):
        used = int((tallies > 0).sum())
        fixed = max(1, used // 4)
        moved = fixed + (places - fixed + offset_by * (used - fixed)) % max(1, number_of - fixed)
        return jnp.zeros((number_of,), jnp.int32).at[ranking[jnp.where(places < fixed, places, moved)]].set(jnp.asarray(tallies, jnp.int32))

    tallies = jnp.where(number % 4 == 0, named(crowded, number // 4), named(usual, number - number // 4 - 1))
    mixed = jax.random.permutation(jax.random.fold_in(own, 3), number_of)
    giver, taker = mixed[0:number_of // 2 * 2:2], mixed[1:number_of // 2 * 2:2]
    slack = jnp.minimum(tallies[giver] - 1, limit - tallies[taker]) // 2
    slack = jnp.where((giver == ranking[0]) | (taker == ranking[0]) | (tallies[taker] == 0), 0, jnp.maximum(slack, 0))
    moved = jax.random.randint(jax.random.fold_in(own, 4), (number_of // 2,), 0, 1 << 20) % (slack + 1)
    tallies = tallies.at[giver].add(-moved).at[taker].add(moved)
    members = jnp.searchsorted(jnp.cumsum(tallies), jnp.arange(rows * top), side="right").astype(jnp.int32)
    grid = members.reshape(top, rows).T
    grid = grid[jax.random.permutation(jax.random.fold_in(own, 1), rows)]
    offset_by = jax.random.randint(jax.random.fold_in(own, 2), (rows, 1), 0, top)
    return jnp.take_along_axis(grid, (jnp.arange(top)[None, :] + offset_by) % top, axis=1)


def load_shares(count, total, most, skew, full):
    weights = [(1 << 20) // math.isqrt(rank ** skew) + 1 for rank in range(1, count + 1)]
    largest = most if full else min(most, max(-(-total // count), total * weights[0] // sum(weights)))
    least = 1 if total - largest >= count - 1 else 0
    counts, spare = [largest] + [least] * (count - 1), total - largest - least * (count - 1)
    while spare > 0:
        free = [i for i in range(1, count) if counts[i] < largest] or [i for i in range(1, count) if counts[i] < most]
        pool, budget = sum([weights[i] for i in free]), spare
        for i in free:
            more = min(most - counts[i], max(1, budget * weights[i] // pool), spare)
            counts[i] = counts[i] + more
            spare = spare - more
    return np.array(counts)


def bell_draw(stream_key, extent, deviation, most, cuts=(), kind=jnp.bfloat16):
    array = deviation * jax.random.normal(stream_key, extent, jnp.float32)
    if cuts:
        array = array * levels(stream_key, extent, cuts, -0.22, 0.18)
    return jnp.clip(array, -most, most).astype(kind)


def setup_inputs(seed: int = 0) -> dict:
    splits = jax.random.split(jax.random.key(seed), 11)
    tokens = draw_tokens(jax.random.fold_in(splits[10], 71), 0)
    cotangent = bell_draw(splits[1], (SEQS, LEN, D), 1.0, 6.0, ((0, 8), (1, 4)))
    expert_ids_keys = jax.random.split(jax.random.fold_in(splits[2], 1), SEQS * LEN // TOK_DEV)
    expert_ids_turns = jax.random.permutation(jax.random.fold_in(splits[2], 3), SEQS * LEN // TOK_DEV)
    expert_ids = jax.vmap(lambda own, number: assign_block(jax.random.fold_in(splits[2], 2), own, number, TOK_DEV, EXPERTS, TOP, CAP, 2))(expert_ids_keys, expert_ids_turns).reshape((SEQS, LEN, TOP))
    segment_ids = draw_segment_ids(jax.random.fold_in(splits[10], 71), 0)
    norm_gains = jnp.clip(1.0 + 0.18 * jax.random.normal(splits[4], (D, 4), jnp.float32), 0.099609375, 1.8984375).astype(jnp.bfloat16)
    w_qkv = bell_draw(splits[5], (D, 3 * D), D ** -0.5, 0.125, ((0, 32),))
    w_out = bell_draw(splits[6], (D, D), (max(1, D // 64)) ** -0.5, 1.0, ((0, 32),))
    router = bell_draw(splits[7], (D, EXPERTS), (4 * D) ** -0.5, 0.0625, ((0, 32),))
    expert_in = bell_draw(splits[8], (D, EXPERTS, 2 * FF), D ** -0.5, 0.125, ((0, 8), (1, 4)))
    expert_out = bell_draw(splits[9], (D, EXPERTS, FF), (max(1, FF // 64)) ** -0.5, 1.5, ((0, 8), (1, 4)))
    return {"tokens": tokens, "cotangent": cotangent, "expert_ids": expert_ids, "segment_ids": segment_ids, "norm_gains": norm_gains, "w_qkv": w_qkv, "w_out": w_out, "router": router, "expert_in": expert_in, "expert_out": expert_out}


epsilon = 1e-05
rotary_base = 10000.0
highest = lax.Precision.HIGHEST

@jax.custom_vjp
def low(v):
    return lax.optimization_barrier(v.astype(jnp.bfloat16)).astype(jnp.float32)

@jax.custom_vjp
def low_back(v):
    return v

def low_keep(v):
    return (low(v), None)

def low_pass(kept, grad):
    return (grad,)

def back_keep(v):
    return (v, None)

def back_low(kept, grad):
    return (low(grad),)
low.defvjp(low_keep, low_pass)
low_back.defvjp(back_keep, back_low)

def rms_scale(values, gain_vector):
    return values * lax.rsqrt(lax.optimization_barrier(jnp.mean(values * values, axis=-1, keepdims=True)) + epsilon) * gain_vector

def rotary(values, position):
    half_dim = values.shape[-1] // 2
    exponent = jnp.arange(half_dim, dtype=jnp.float32) * (2.0 / values.shape[-1])
    angles = position.astype(jnp.float32)[:, None] * (rotary_base ** (-exponent))[None, :]
    cosine = jnp.cos(angles)[:, None, :]
    sine_part = jnp.sin(angles)[:, None, :]
    first_half = values[..., :half_dim]
    second_half = values[..., half_dim:]
    return jnp.concatenate([first_half * cosine - second_half * sine_part, second_half * cosine + first_half * sine_part], axis=-1)

def attention(q_low, k_low, v_low, segment):
    length = q_low.shape[0]
    block_rows = min(512, length)
    key_block = jnp.arange(length, dtype=jnp.int32) // ATT_BLOCK
    scale_factor = q_low.shape[-1] ** (-0.5)

    def one_block(offset):
        query_rows = lax.dynamic_slice_in_dim(q_low, offset, block_rows, 0)
        query_pos = offset + jnp.arange(block_rows, dtype=jnp.int32)
        query_seg = lax.dynamic_slice_in_dim(segment, offset, block_rows, 0)
        scores = low_back(jnp.einsum('qhd,khd->hqk', query_rows, k_low, precision=highest) * scale_factor)
        allowed = (query_seg[:, None] == segment[None, :]) & (key_block[None, :] <= (query_pos // ATT_BLOCK)[:, None])
        masked = jnp.where(allowed[None], scores, -jnp.inf)
        weights = low(jax.nn.softmax(masked, axis=-1))
        return low_back(low(jnp.einsum('hqk,khd->qhd', weights, v_low, precision=highest)))
    starts = jnp.arange(length // block_rows, dtype=jnp.int32) * block_rows
    blocks = lax.map(jax.checkpoint(one_block), starts)
    return blocks.reshape(length, q_low.shape[1], q_low.shape[2])

def experts(mlp_low, router_probs, routed_ids, expert_in, expert_out):
    capacity = CAP * N_SEQ

    def one_expert(running, expert):
        chosen = jnp.any(routed_ids == expert, axis=-1)
        row_order = jnp.argsort(jnp.where(chosen, 0, 1).astype(jnp.int32), stable=True)[:capacity].astype(jnp.int32)
        weight = lax.dynamic_index_in_dim(router_probs, expert, 1, keepdims=False)[row_order] * chosen[row_order].astype(jnp.float32)
        copies = low_back(mlp_low[row_order])
        in_weight = lax.dynamic_index_in_dim(expert_in, expert, 1, keepdims=False)
        gate_up = low_back(jnp.dot(copies, in_weight, precision=highest))
        activated = low(jax.nn.silu(gate_up[:, :FF]) * gate_up[:, FF:])
        out_weight = lax.dynamic_index_in_dim(expert_out, expert, 1, keepdims=False)
        result = low_back(low(jnp.dot(activated, out_weight.T, precision=highest)))
        return (running.at[row_order].add(result * weight[:, None]), None)
    running, unused = lax.scan(jax.checkpoint(one_expert), jnp.zeros_like(mlp_low), jnp.arange(EXPERTS, dtype=jnp.int32))
    return running

def one_sequence(inputs, params):
    token_values, routed_ids, segment = inputs
    gains, w_qkv, w_out, router, expert_in, expert_out = params
    attn_in = low(rms_scale(token_values, gains[:, 0]))
    qkv = low_back(jnp.dot(attn_in, w_qkv, precision=highest))
    q_norm = rms_scale(qkv[:, :D], gains[:, 1])
    k_norm = rms_scale(qkv[:, D:2 * D], gains[:, 2])
    position = jnp.arange(LEN, dtype=jnp.int32)
    head_shape = (LEN, HEADS, HEAD_DIM)
    q_low = low_back(low(rotary(q_norm.reshape(head_shape), position)))
    k_low = low_back(low(rotary(k_norm.reshape(head_shape), position)))
    v_low = low_back(low(qkv[:, 2 * D:].reshape(head_shape)))
    att_low = attention(q_low, k_low, v_low, segment).reshape(LEN, D)
    branch = low_back(jnp.dot(att_low, w_out.T, precision=highest))
    hidden_one = token_values + branch
    mlp_low = low(rms_scale(hidden_one, gains[:, 3]))
    router_probs = jax.nn.softmax(jnp.dot(mlp_low, router, precision=highest), axis=-1)
    return hidden_one + experts(mlp_low, router_probs, routed_ids, expert_in, expert_out)

def reference(tokens, cotangent, expert_ids, segment_ids, norm_gains, w_qkv, w_out, router, expert_in, expert_out):
    params = (norm_gains.astype(jnp.float32), w_qkv.astype(jnp.float32), w_out.astype(jnp.float32), router.astype(jnp.float32), expert_in.astype(jnp.float32), expert_out.astype(jnp.float32))
    token_values = tokens.astype(jnp.float32)

    def forward(values_all, weights_all):

        def advance(carried, inputs):
            return (carried, jax.checkpoint(one_sequence)(inputs, weights_all))
        unused, outputs = lax.scan(advance, jnp.float32(0.0), (values_all, expert_ids, segment_ids))
        return outputs
    result, pullback = jax.vjp(forward, token_values, params)
    token_grad, param_grads = pullback(cotangent.astype(jnp.float32))
    return (result.astype(jnp.bfloat16), token_grad, param_grads[0], param_grads[1], param_grads[2], param_grads[3], param_grads[4], param_grads[5])
```

```python
import jax
import jax.numpy as jnp
from jax import lax
from jax.sharding import PartitionSpec as P

HEADS = 16
HEAD_DIM = 128
FF = 1024
TOP = 8
ATT_BLOCK = 256


epsilon = 1e-05
rotary_base = 10000.0
highest = lax.Precision.HIGHEST
f32 = jnp.float32
bf16 = jnp.bfloat16


def swap_pairs(count, mask):
    return [(i, i ^ mask) for i in range(count)]


def put_block(buffer, block, index, axis):
    return lax.dynamic_update_index_in_dim(buffer, block, index, axis)


def is_square(axis):
    return lax.axis_size(axis) == 4


def gather_square(block, axis, out_axis):
    if not is_square(axis):
        return lax.all_gather(block, axis, axis=out_axis)
    own = lax.axis_index(axis)
    half = block.shape[0] // 2
    first, second = block[:half], block[half:]
    first_near = lax.ppermute(first, axis, swap_pairs(4, 1))
    second_near = lax.ppermute(second, axis, swap_pairs(4, 2))
    first_pair = lax.ppermute(jnp.stack([first, first_near]), axis, swap_pairs(4, 2))
    second_pair = lax.ppermute(jnp.stack([second, second_near]), axis, swap_pairs(4, 1))
    parts = [
        (block[:half], block[half:]),
        (first_near, second_pair[0]),
        (first_pair[0], second_near),
        (first_pair[1], second_pair[1]),
    ]
    shape = block.shape[:out_axis] + (4,) + block.shape[out_axis:]
    out = jnp.zeros(shape, block.dtype)
    for mask, (low_part, high_part) in enumerate(parts):
        whole = jnp.concatenate([low_part, high_part], axis=0)
        out = put_block(out, whole, own ^ mask, out_axis)
    return out


def scatter_square(blocks, axis):
    if not is_square(axis):
        return lax.psum_scatter(blocks, axis, scatter_dimension=0, tiled=False)
    own = lax.axis_index(axis)
    kind = blocks.dtype
    half = blocks.shape[1] // 2
    rel = [lax.dynamic_index_in_dim(blocks, own ^ mask, 0, keepdims=False) for mask in range(4)]

    def add(one, other):
        return (one.astype(f32) + other.astype(f32)).astype(kind)

    first = [block[:half] for block in rel]
    second = [block[half:] for block in rel]
    first_in = lax.ppermute(jnp.stack([first[2], first[3]]), axis, swap_pairs(4, 2))
    second_in = lax.ppermute(jnp.stack([second[1], second[3]]), axis, swap_pairs(4, 1))
    first_far = lax.ppermute(add(first[1], first_in[1]), axis, swap_pairs(4, 1))
    second_far = lax.ppermute(add(second[2], second_in[1]), axis, swap_pairs(4, 2))
    first_sum = first[0].astype(f32) + first_in[0].astype(f32) + first_far.astype(f32)
    second_sum = second[0].astype(f32) + second_in[0].astype(f32) + second_far.astype(f32)
    return jnp.concatenate([first_sum, second_sum], axis=0)


def sum_square(value, axis):
    count = lax.axis_size(axis)
    if count & (count - 1):
        return lax.psum(value, axis)
    mask = 1
    while mask < count:
        value = value + lax.ppermute(value, axis, swap_pairs(count, mask))
        mask *= 2
    return value


def gather_line(block, axis):
    count = lax.axis_size(axis)
    own = lax.axis_index(axis)
    up, down = block, block
    ups, downs = [block], [block]
    for step in range(1, count):
        up = lax.ppermute(up, axis, [(j, j + 1) for j in range(step - 1, count - 1)])
        down = lax.ppermute(down, axis, [(j, j - 1) for j in range(1, count - step + 1)])
        ups.append(up)
        downs.append(down)
    return [block] + [
        jnp.where(own >= k, ups[k], downs[count - k]) for k in range(1, count)
    ]


def scatter_line(blocks, axis):
    count = lax.axis_size(axis)
    kind = blocks[0].dtype
    up = down = None

    def add(one, other):
        return one if other is None else (one.astype(f32) + other.astype(f32)).astype(kind)

    for step in range(1, count):
        up = lax.ppermute(
            add(blocks[step], up), axis, [(j, j + 1) for j in range(min(step, count - 1))]
        )
        down = lax.ppermute(
            add(blocks[count - step], down),
            axis,
            [(j, j - 1) for j in range(max(count - step, 1), count)],
        )
    return blocks[0].astype(f32) + up.astype(f32) + down.astype(f32)


def order_line(blocks, axis, out_axis):
    count = lax.axis_size(axis)
    own = lax.axis_index(axis)
    shape = blocks[0].shape[:out_axis] + (count,) + blocks[0].shape[out_axis:]
    out = jnp.zeros(shape, blocks[0].dtype)
    for k, block in enumerate(blocks):
        out = put_block(out, block, lax.rem(own - k + count, count), out_axis)
    return out


def split_line(stacked, axis, in_axis):
    count = lax.axis_size(axis)
    own = lax.axis_index(axis)
    return [
        lax.dynamic_index_in_dim(
            stacked, lax.rem(own - k + count, count), in_axis, keepdims=False
        )
        for k in range(count)
    ]


def gather_core(block, axis, out_axis):
    if lax.axis_size(axis) != 2:
        return lax.all_gather(block, axis, axis=out_axis)
    other = lax.ppermute(block, axis, swap_pairs(2, 1))
    is_first = lax.axis_index(axis) == 0
    return jnp.stack(
        [jnp.where(is_first, block, other), jnp.where(is_first, other, block)], axis=out_axis
    )


def scatter_core(stacked, axis, in_axis):
    if lax.axis_size(axis) != 2:
        return lax.psum_scatter(stacked, axis, scatter_dimension=in_axis, tiled=False)
    own = lax.axis_index(axis)
    kept = lax.dynamic_index_in_dim(stacked, own, in_axis, keepdims=False)
    given = lax.dynamic_index_in_dim(stacked, 1 - own, in_axis, keepdims=False)
    received = lax.ppermute(given, axis, swap_pairs(2, 1))
    return (kept.astype(f32) + received.astype(f32)).astype(stacked.dtype)


def rms_inverse(values):
    return lax.rsqrt(jnp.mean(values * values, axis=-1, keepdims=True) + epsilon)


def rms_back(gradient, values, inverse, gain_vector):
    scaled = gradient * gain_vector
    gain_grad = jnp.sum(gradient * values * inverse, axis=0)
    value_grad = inverse * scaled - values * inverse**3 * jnp.mean(
        scaled * values, axis=-1, keepdims=True
    )
    return (value_grad, gain_grad)


def rotary_tables(position, head_dim):
    half_dim = head_dim // 2
    exponent = jnp.arange(half_dim, dtype=f32) * (2.0 / head_dim)
    angles = position.astype(f32)[:, None] * (rotary_base ** (-exponent))[None, :]
    return (jnp.cos(angles)[:, None, :], jnp.sin(angles)[:, None, :])


def rotate(values, cosine, sine_part):
    half_dim = values.shape[-1] // 2
    first_half = values[..., :half_dim]
    second_half = values[..., half_dim:]
    return jnp.concatenate(
        [
            first_half * cosine - second_half * sine_part,
            second_half * cosine + first_half * sine_part,
        ],
        axis=-1,
    )


def rotate_back(gradient, cosine, sine_part):
    return rotate(gradient, cosine, -sine_part)


def block_scores(query_rows, keys, query_segment, key_segment, block_index):
    scores = jnp.einsum("qhd,khd->hqk", query_rows, keys, preferred_element_type=f32)
    scores = scores * (query_rows.shape[-1] ** (-0.5))
    allowed = query_segment[:, None] == key_segment[None, :]
    return jnp.where(allowed[None], scores, -jnp.inf)


def attend(queries, keys, values, segment):
    length = queries.shape[0]
    outputs, log_totals = [], []
    for start in range(0, length, ATT_BLOCK):
        stop = start + ATT_BLOCK
        scores = block_scores(
            queries[start:stop], keys[:stop], segment[start:stop], segment[:stop], start
        )
        highest_score = jnp.max(scores, axis=-1, keepdims=True)
        exponent_terms = jnp.exp(scores - highest_score)
        totals = jnp.sum(exponent_terms, axis=-1, keepdims=True)
        weights = (exponent_terms / totals).astype(bf16)
        output = jnp.einsum("hqk,khd->qhd", weights, values[:stop], preferred_element_type=f32)
        outputs.append(output.astype(bf16))
        log_totals.append(highest_score + jnp.log(totals))
    return jnp.concatenate(outputs, axis=0), log_totals


def attend_back(queries, keys, values, log_totals, grads, segment):
    length = queries.shape[0]
    scale_factor = queries.shape[-1] ** (-0.5)
    query_grads = []
    key_grads = [[] for _ in range(0, length, ATT_BLOCK)]
    value_grads = [[] for _ in range(0, length, ATT_BLOCK)]
    for number, start in enumerate(range(0, length, ATT_BLOCK)):
        stop = start + ATT_BLOCK
        query_rows, grad_rows = queries[start:stop], grads[start:stop]
        scores = block_scores(query_rows, keys[:stop], segment[start:stop], segment[:stop], start)
        prob_rows = jnp.exp(scores - log_totals[number])
        value_grad = jnp.einsum(
            "hqk,qhd->khd", prob_rows.astype(bf16), grad_rows, preferred_element_type=f32
        )
        prob_grad = jnp.einsum(
            "qhd,khd->hqk", grad_rows, values[:stop], preferred_element_type=f32
        )
        inner_sum = jnp.sum(prob_rows * prob_grad, axis=-1, keepdims=True)
        score_grad = (prob_rows * (prob_grad - inner_sum)).astype(bf16)
        query_grad = jnp.einsum("hqk,khd->qhd", score_grad, keys[:stop], preferred_element_type=f32)
        key_grad = jnp.einsum("hqk,qhd->khd", score_grad, query_rows, preferred_element_type=f32)
        query_grads.append((query_grad * scale_factor).astype(bf16))
        for earlier in range(number + 1):
            rows = slice(earlier * ATT_BLOCK, (earlier + 1) * ATT_BLOCK)
            key_grads[earlier].append(key_grad[rows])
            value_grads[earlier].append(value_grad[rows])
    key_grad = jnp.concatenate([sum(parts) for parts in key_grads], axis=0) * scale_factor
    value_grad = jnp.concatenate([sum(parts) for parts in value_grads], axis=0)
    return jnp.concatenate(query_grads, axis=0), key_grad.astype(bf16), value_grad.astype(bf16)


def on_device(
    tokens,
    cotangent,
    expert_ids,
    segment_ids,
    norm_gains,
    w_qkv,
    w_out,
    router,
    expert_in,
    expert_out,
):
    own_low = tokens[0]
    inputs = own_low.astype(f32)
    tok_count, model_width = inputs.shape
    segment = segment_ids[0]
    length = segment.shape[0]
    seq_count = lax.axis_size("seq")
    exp_count = lax.axis_size("exp")
    core_count = lax.axis_size("fsdp")
    own_seq = lax.axis_index("seq")
    own_exp = lax.axis_index("exp")
    rows_dev = w_qkv.shape[0]
    heads_dev = HEADS // seq_count
    head_cols = heads_dev * HEAD_DIM
    experts_total = router.shape[1]
    exp_dev = expert_in.shape[1]

    small = jnp.concatenate([norm_gains, router], axis=1).T
    small = gather_square(small, "seq", 1)
    small = order_line(gather_line(small, "exp"), "exp", 2)
    small = gather_core(small, "fsdp", 3).reshape(-1, model_width)
    gains = small[:4].astype(f32)
    router_rows = small[4:]

    all_tokens = gather_square(own_low, "seq", 0).reshape(length, model_width)
    heads_weight = lax.all_to_all(
        w_qkv.reshape(rows_dev, 3, seq_count, head_cols), "seq", split_axis=2, concat_axis=0, tiled=True
    ).reshape(seq_count, rows_dev, 3 * head_cols)
    heads_weight = order_line(gather_line(heads_weight, "exp"), "exp", 1)
    heads_weight = gather_core(heads_weight, "fsdp", 2).reshape(model_width, 3 * head_cols)

    out_weight = gather_square(w_out, "seq", 0)
    out_weight = order_line(gather_line(out_weight, "exp"), "exp", 1)
    out_weight = gather_core(out_weight, "fsdp", 2).reshape(model_width, model_width)

    in_weight = lax.all_gather(
        jnp.transpose(expert_in, (1, 0, 2)), ("seq", "fsdp"), axis=1, tiled=True
    )
    down_weight = lax.all_gather(
        jnp.transpose(expert_out, (1, 0, 2)), ("seq", "fsdp"), axis=1, tiled=True
    )
    cot_group = jnp.stack(gather_line(cotangent[0], "exp"))

    capacity = tok_count * TOP // experts_total * 9 // 8
    chosen = jnp.any(
        expert_ids[0][:, :, None] == jnp.arange(experts_total, dtype=jnp.int32)[None, None, :], axis=1
    )
    earlier = (
        jnp.arange(tok_count)[:, None] > jnp.arange(tok_count)[None, :]
    ).astype(bf16)
    rank = jnp.dot(earlier, chosen.astype(bf16), preferred_element_type=f32)
    rank = jnp.where(chosen, rank, -1.0).T
    rank_group = jnp.stack(gather_line(rank, "exp"))
    rank_group = lax.dynamic_slice_in_dim(rank_group, own_exp * exp_dev, exp_dev, 1)
    rank_group = jnp.transpose(rank_group, (1, 0, 2))
    pick = rank_group[:, :, None, :] == jnp.arange(capacity, dtype=f32)[None, None, :, None]
    pick_low = pick.astype(bf16)

    all_inputs = all_tokens.astype(f32)
    first_inverse = rms_inverse(all_inputs)
    attn_low = (all_inputs * first_inverse * gains[0]).astype(bf16)
    projected = jnp.dot(attn_low, heads_weight, preferred_element_type=f32)
    own_gains = lax.dynamic_slice_in_dim(gains, own_seq * head_cols, head_cols, 1)
    query_pre, key_pre = projected[:, :head_cols], projected[:, head_cols : 2 * head_cols]
    squares = jnp.stack([jnp.sum(query_pre * query_pre, axis=-1), jnp.sum(key_pre * key_pre, axis=-1)])
    squares = sum_square(squares, "seq")
    inverses = lax.rsqrt(squares / model_width + epsilon)
    query_inverse, key_inverse = inverses[0][:, None], inverses[1][:, None]
    cosine, sine_part = rotary_tables(jnp.arange(length, dtype=jnp.int32), HEAD_DIM)
    head_shape = (length, heads_dev, HEAD_DIM)
    queries = rotate(
        (query_pre * query_inverse * own_gains[1]).reshape(head_shape), cosine, sine_part
    ).astype(bf16)
    keys = rotate(
        (key_pre * key_inverse * own_gains[2]).reshape(head_shape), cosine, sine_part
    ).astype(bf16)
    values = projected[:, 2 * head_cols :].astype(bf16).reshape(head_shape)
    attended, log_totals = attend(queries, keys, values, segment)
    merged = lax.all_to_all(
        attended.reshape(length, head_cols), "seq", split_axis=0, concat_axis=1, tiled=True
    )
    branch = jnp.einsum("tc,dc->td", merged, out_weight, preferred_element_type=f32)
    residual = inputs + branch
    mlp_inverse = rms_inverse(residual)
    mlp_low = (residual * mlp_inverse * gains[3]).astype(bf16)

    mlp_group = jnp.stack(gather_line(mlp_low, "exp"))
    logits = jnp.einsum("std,ed->ste", mlp_group, router_rows, preferred_element_type=f32)
    group_probs = jax.nn.softmax(logits, axis=-1)
    router_probs = group_probs[0]
    near_probs = lax.dynamic_slice_in_dim(group_probs, own_exp * exp_dev, exp_dev, 2)
    near_probs = jnp.transpose(near_probs, (2, 0, 1))
    gate_rows = jnp.sum(jnp.where(pick, near_probs[:, :, None, :], 0.0), axis=-1)
    rows_shape = (exp_dev, exp_count * capacity)
    gate_rows = gate_rows.reshape(rows_shape + (1,))
    expert_rows = jnp.einsum("esrt,std->esrd", pick_low, mlp_group, preferred_element_type=f32)
    expert_rows = expert_rows.astype(bf16).reshape(rows_shape + (model_width,))
    cot_rows = jnp.einsum("esrt,std->esrd", pick_low, cot_group, preferred_element_type=f32)
    cot_rows = cot_rows.astype(bf16).reshape(rows_shape + (model_width,))
    gate_up = jnp.einsum("erd,edf->erf", expert_rows, in_weight, preferred_element_type=f32)
    gate_part, up_part = gate_up[..., :FF], gate_up[..., FF:]
    sigmoid_gate = jax.nn.sigmoid(gate_part)
    silu_gate = gate_part * sigmoid_gate
    activated = silu_gate * up_part
    gated = (activated * gate_rows).astype(bf16)
    expert_result = jnp.einsum("erf,edf->erd", gated, down_weight, preferred_element_type=f32)
    expert_result = expert_result.astype(bf16).reshape(exp_dev, exp_count, capacity, model_width)
    mix_parts = jnp.einsum(
        "esrt,esrd->std", pick_low, expert_result, preferred_element_type=f32
    ).astype(bf16)

    result_grad = jnp.einsum("erd,edf->erf", cot_rows, down_weight, preferred_element_type=f32)
    gate_grad = jnp.sum(result_grad * activated, axis=-1)
    act_grad = result_grad * gate_rows
    gate_up_grad = jnp.concatenate(
        [
            act_grad * up_part * sigmoid_gate * (1.0 + gate_part * (1.0 - sigmoid_gate)),
            act_grad * silu_gate,
        ],
        axis=-1,
    ).astype(bf16)
    down_grad = jnp.einsum("erd,erf->edf", cot_rows, gated, preferred_element_type=f32)
    grad_expert_out = lax.psum_scatter(
        down_grad.astype(bf16), ("seq", "fsdp"), scatter_dimension=1, tiled=True
    )
    row_grad = jnp.einsum("erf,edf->erd", gate_up_grad, in_weight, preferred_element_type=f32)
    row_grad = row_grad.astype(bf16).reshape(exp_dev, exp_count, capacity, model_width)
    copy_parts = jnp.einsum(
        "esrt,esrd->std", pick_low, row_grad, preferred_element_type=f32
    ).astype(bf16)
    in_grad = jnp.einsum("erd,erf->edf", expert_rows, gate_up_grad, preferred_element_type=f32)
    grad_expert_in = lax.psum_scatter(
        in_grad.astype(bf16), ("seq", "fsdp"), scatter_dimension=1, tiled=True
    )
    gate_grad = gate_grad.reshape(exp_dev, exp_count, capacity)
    prob_parts = jnp.sum(jnp.where(pick, gate_grad[..., None], 0.0), axis=2)
    prob_parts = jnp.transpose(prob_parts, (1, 0, 2))
    prob_parts = lax.dynamic_update_slice_in_dim(
        jnp.zeros((exp_count, experts_total, tok_count), f32), prob_parts, own_exp * exp_dev, 1
    )
    prob_grad = scatter_line([prob_parts[k] for k in range(exp_count)], "exp").T
    mlp_grad_experts = scatter_line([copy_parts[k] for k in range(exp_count)], "exp")
    expert_mix = scatter_line([mix_parts[k] for k in range(exp_count)], "exp")
    output = (residual + expert_mix).astype(bf16)

    logit_grad = router_probs * (
        prob_grad - jnp.sum(router_probs * prob_grad, axis=-1, keepdims=True)
    )
    router_grad = jnp.dot(logit_grad.T, mlp_low.astype(f32), precision=highest)
    mlp_grad = mlp_grad_experts + jnp.dot(
        logit_grad, router_rows.astype(f32), precision=highest
    )
    residual_norm_grad, mlp_gain_grad = rms_back(mlp_grad, residual, mlp_inverse, gains[3])
    residual_grad = cotangent[0].astype(f32) + residual_norm_grad
    branch_grad = residual_grad.astype(bf16)

    merged_grad = jnp.einsum("td,dc->tc", branch_grad, out_weight, preferred_element_type=f32)
    heads_grad = lax.all_to_all(
        merged_grad.astype(bf16), "seq", split_axis=1, concat_axis=0, tiled=True
    ).reshape(head_shape)
    out_weight_grad = jnp.einsum("td,tc->dc", branch_grad, merged, preferred_element_type=f32)
    query_grad, key_grad, value_grad = attend_back(
        queries, keys, values, log_totals, heads_grad, segment
    )
    query_grad = rotate_back(query_grad.astype(f32), cosine, sine_part).reshape(length, head_cols)
    key_grad = rotate_back(key_grad.astype(f32), cosine, sine_part).reshape(length, head_cols)
    query_scaled, key_scaled = query_grad * own_gains[1], key_grad * own_gains[2]
    means = jnp.stack(
        [jnp.sum(query_scaled * query_pre, axis=-1), jnp.sum(key_scaled * key_pre, axis=-1)]
    )
    means = sum_square(means, "seq") / model_width
    query_gain_grad = jnp.sum(query_grad * query_pre * query_inverse, axis=0)
    key_gain_grad = jnp.sum(key_grad * key_pre * key_inverse, axis=0)
    query_pre_grad = query_inverse * query_scaled - query_pre * query_inverse**3 * means[0][:, None]
    key_pre_grad = key_inverse * key_scaled - key_pre * key_inverse**3 * means[1][:, None]
    qkv_grad = jnp.concatenate(
        [query_pre_grad.astype(bf16), key_pre_grad.astype(bf16), value_grad.reshape(length, head_cols)],
        axis=1,
    )
    attn_in_part = jnp.einsum("tc,dc->td", qkv_grad, heads_weight, preferred_element_type=f32)
    first_gain_grad = jnp.sum(attn_in_part * all_inputs * first_inverse, axis=0)
    attn_in_grad = scatter_square(
        attn_in_part.astype(bf16).reshape(seq_count, tok_count, model_width), "seq"
    )
    heads_weight_grad = jnp.einsum("td,tc->dc", attn_low, qkv_grad, preferred_element_type=f32)

    own_inverse = lax.dynamic_slice_in_dim(first_inverse, own_seq * tok_count, tok_count, 0)
    input_norm_grad, _ = rms_back(attn_in_grad, inputs, own_inverse, gains[0])
    input_grad = residual_grad + input_norm_grad

    rows_split = (seq_count, exp_count, core_count, rows_dev)
    heads_terms = heads_weight_grad.astype(bf16).reshape(rows_split + (3 * head_cols,))
    heads_terms = scatter_core(heads_terms, "fsdp", 2)
    heads_terms = scatter_line(split_line(heads_terms, "exp", 1), "exp").astype(bf16)
    grad_w_qkv = lax.all_to_all(
        heads_terms.reshape(seq_count, rows_dev, 3, 1, head_cols), "seq", split_axis=0, concat_axis=3, tiled=True
    ).reshape(rows_dev, 3 * model_width).astype(f32)

    out_terms = out_weight_grad.astype(bf16).reshape(rows_split + (model_width,))
    out_terms = scatter_core(out_terms, "fsdp", 2)
    out_terms = scatter_line(split_line(out_terms, "exp", 1), "exp").astype(bf16)
    grad_w_out = scatter_square(out_terms, "seq")

    zero_row = jnp.zeros((model_width,), f32)
    small_terms = jnp.concatenate(
        [
            jnp.stack(
                [
                    first_gain_grad,
                    lax.dynamic_update_slice_in_dim(zero_row, query_gain_grad, own_seq * head_cols, 0),
                    lax.dynamic_update_slice_in_dim(zero_row, key_gain_grad, own_seq * head_cols, 0),
                    mlp_gain_grad,
                ]
            ),
            router_grad,
        ],
        axis=0,
    ).reshape((-1,) + rows_split)
    small_terms = jnp.transpose(small_terms, (1, 0, 2, 3, 4))
    small_terms = scatter_core(small_terms, "fsdp", 3)
    small_terms = scatter_line(split_line(small_terms, "exp", 2), "exp")
    small_grad = scatter_square(small_terms, "seq").T
    return (
        output[None],
        input_grad[None],
        small_grad[:, :4],
        grad_w_qkv,
        grad_w_out,
        small_grad[:, 4:],
        jnp.transpose(grad_expert_in, (1, 0, 2)).astype(f32),
        jnp.transpose(grad_expert_out, (1, 0, 2)).astype(f32),
    )


def solution(mesh):
    in_specs = (
        P(("exp", "fsdp"), "seq", None),
        P(("exp", "fsdp"), "seq", None),
        P(("exp", "fsdp"), "seq", None),
        P(("exp", "fsdp"), None),
        P(("seq", "exp", "fsdp"), None),
        P(("seq", "exp", "fsdp"), None),
        P(("seq", "exp", "fsdp"), None),
        P(("seq", "exp", "fsdp"), None),
        P(("seq", "fsdp"), "exp", None),
        P(("seq", "fsdp"), "exp", None),
    )
    out_specs = (
        P(("exp", "fsdp"), "seq", None),
        P(("exp", "fsdp"), "seq", None),
        P(("seq", "exp", "fsdp"), None),
        P(("seq", "exp", "fsdp"), None),
        P(("seq", "exp", "fsdp"), None),
        P(("seq", "exp", "fsdp"), None),
        P(("seq", "fsdp"), "exp", None),
        P(("seq", "fsdp"), "exp", None),
    )
    return jax.shard_map(
        on_device, mesh=mesh, in_specs=in_specs, out_specs=out_specs, check_vma=False
    )
```

```python
import functools

import jax
import jax.numpy as jnp
from jax import lax
from jax.experimental import pallas as pl
from jax.experimental.pallas import tpu as pltpu
from jax.sharding import PartitionSpec as P

HEADS = 16
HEAD_DIM = 128
FF = 1024
TOP = 8
ATT_BLOCK = 256


epsilon = 1e-05
rotary_base = 10000.0
highest = lax.Precision.HIGHEST
f32 = jnp.float32
bf16 = jnp.bfloat16
VMEM_BYTES = 63 * 1024 * 1024
KERNEL_PARAMS = pltpu.CompilerParams(vmem_limit_bytes=VMEM_BYTES)
SMALL_COST = pl.CostEstimate(flops=1, bytes_accessed=1, transcendentals=0)
DOWN_GRAD_COST = pl.CostEstimate(flops=10**11, bytes_accessed=1, transcendentals=0)
ATTEND_BACK_COST = pl.CostEstimate(flops=345 * 10**9, bytes_accessed=1, transcendentals=0)


def after(value, other):
    first = lax.slice(other, (0,) * other.ndim, (1,) * other.ndim).reshape(())
    return value + (0.0 * first.astype(f32)).astype(value.dtype)


def swap_pairs(count, mask):
    return [(i, i ^ mask) for i in range(count)]


def shift_pairs(count, step):
    return [(i, (i + step) % count) for i in range(count)]


def ring_place(index, count):
    return index & (count - 1) if count & (count - 1) == 0 else lax.rem(index + count, count)


def exchange(stacked, axis, split_axis=0):
    return lax.all_to_all(stacked, axis, split_axis=split_axis, concat_axis=split_axis, tiled=True)


def gather_near(block, axis):
    count = lax.axis_size(axis)
    return [block] + [
        lax.ppermute(block, axis, shift_pairs(count, k)) for k in range(1, count)
    ]


def send_near(blocks, axis):
    count = lax.axis_size(axis)
    return [blocks[0]] + [
        lax.ppermute(blocks[k], axis, shift_pairs(count, -k)) for k in range(1, count)
    ]


def add_up(blocks):
    return sum(block.astype(f32) for block in blocks)


def order(blocks, axis, out_axis=0, sign=-1):
    count = lax.axis_size(axis)
    own = lax.axis_index(axis)
    shape = blocks[0].shape[:out_axis] + (count,) + blocks[0].shape[out_axis:]
    out = jnp.zeros(shape, blocks[0].dtype)
    for k, block in enumerate(blocks):
        place = ring_place(own + sign * k, count)
        out = lax.dynamic_update_index_in_dim(out, block, place, out_axis)
    return out


def split(stacked, axis, in_axis=0, sign=-1):
    count = lax.axis_size(axis)
    own = lax.axis_index(axis)
    return [
        lax.dynamic_index_in_dim(
            stacked, ring_place(own + sign * k, count), in_axis, keepdims=False
        )
        for k in range(count)
    ]


def gather(block, axis, out_axis=0):
    return order(gather_near(block, axis), axis, out_axis)


def scatter(stacked, axis, split_axis=0):
    return add_up(send_near(split(stacked, axis, split_axis), axis))


def sum_all(value, axis):
    return add_up(gather_near(value, axis))


def assemble_kernel(groups, parts, place_ref, *refs):
    sources, out_ref, sems = refs[: len(refs) - 2], refs[-2], refs[-1]
    rows = sources[0].shape[0] // groups
    copies = []
    for k, source in enumerate(sources):
        for group in range(groups):
            target = pl.multiple_of((group * parts + place_ref[k]) * rows, rows)
            copies.append(
                pltpu.make_async_copy(
                    source.at[pl.ds(group * rows, rows)],
                    out_ref.at[pl.ds(target, rows)],
                    sems.at[k, group],
                )
            )
    for copy in copies:
        copy.start()
    for copy in copies:
        copy.wait()


def assemble(blocks, places, groups):
    parts = len(blocks)
    return pl.pallas_call(
        functools.partial(assemble_kernel, groups, parts),
        in_specs=[pl.BlockSpec(memory_space=pltpu.SMEM)]
        + [pl.BlockSpec(memory_space=pltpu.VMEM)] * parts,
        out_specs=pl.BlockSpec(memory_space=pl.ANY),
        out_shape=jax.ShapeDtypeStruct(
            (parts * blocks[0].shape[0], blocks[0].shape[1]), blocks[0].dtype
        ),
        scratch_shapes=[pltpu.SemaphoreType.DMA((parts, groups))],
        compiler_params=KERNEL_PARAMS,
        cost_estimate=SMALL_COST,
        name="assemble",
    )(places, *blocks)


def order_cores(blocks, groups, axis, core_axis):
    count, cores = lax.axis_size(axis), lax.axis_size(core_axis)
    own, own_core = lax.axis_index(axis), lax.axis_index(core_axis)
    if cores == 2:
        blocks = blocks + [lax.ppermute(block, core_axis, swap_pairs(2, 1)) for block in blocks]
        core_places = [own_core, 1 - own_core]
    else:
        every = lax.all_gather(jnp.stack(blocks), core_axis, axis=0)
        blocks = [every[core, k] for core in range(cores) for k in range(count)]
        core_places = list(range(cores))
    places = [
        ring_place(own - k, count) * cores + core for core in core_places for k in range(count)
    ]
    places = jnp.stack([jnp.asarray(place, jnp.int32) for place in places])
    return assemble(blocks, places, groups)


def scatter_core(stacked, axis):
    if lax.axis_size(axis) != 2:
        return lax.psum_scatter(stacked, axis, scatter_dimension=0, tiled=False)
    own = lax.axis_index(axis)
    kept = lax.dynamic_index_in_dim(stacked, own, 0, keepdims=False)
    given = lax.dynamic_index_in_dim(stacked, 1 - own, 0, keepdims=False)
    received = lax.ppermute(given, axis, swap_pairs(2, 1))
    return (kept.astype(f32) + received.astype(f32)).astype(stacked.dtype)


def rms_inverse(values):
    return lax.rsqrt(jnp.mean(values * values, axis=-1, keepdims=True) + epsilon)


def rms_back(gradient, values, inverse, gain_vector):
    scaled = gradient * gain_vector
    gain_grad = jnp.sum(gradient * values * inverse, axis=0)
    value_grad = inverse * scaled - values * inverse**3 * jnp.mean(
        scaled * values, axis=-1, keepdims=True
    )
    return (value_grad, gain_grad)


def rotary_tables(position, head_dim):
    half_dim = head_dim // 2
    exponent = jnp.arange(half_dim, dtype=f32) * (2.0 / head_dim)
    angles = position.astype(f32)[:, None] * (rotary_base ** (-exponent))[None, :]
    cosine, sine_part = jnp.cos(angles), jnp.sin(angles)
    return jnp.stack(
        [
            jnp.concatenate([cosine, cosine], axis=1),
            jnp.concatenate([-sine_part, sine_part], axis=1),
        ]
    )


def dot(one, other, one_axis, other_axis):
    return lax.dot_general(
        one, other, (((one_axis,), (other_axis,)), ((), ())), preferred_element_type=f32
    )


def turn(values, cosines, sines):
    return values * cosines + pltpu.roll(values, HEAD_DIM // 2, 1) * sines


def block_probs(query_rows, keys, query_segment, key_segment, scale):
    scores = dot(query_rows, keys, 1, 1) * scale
    scores = jnp.where(query_segment == key_segment, scores, -jnp.inf)
    terms = jnp.exp(scores - jnp.max(scores, axis=1, keepdims=True))
    return terms / jnp.sum(terms, axis=1, keepdims=True)


def attend_kernel(
    query_ref, key_ref, value_ref, scale_ref, gain_ref, turn_ref, row_seg_ref, col_seg_ref,
    out_ref, query_low_ref, key_low_ref, value_low_ref,
):
    length = query_ref.shape[0]
    cosines, sines = turn_ref[0], turn_ref[1]
    query = query_ref[...] * scale_ref[:, 0:1] * gain_ref[0:1, :]
    key = key_ref[...] * scale_ref[:, 1:2] * gain_ref[1:2, :]
    query_low_ref[...] = turn(query, cosines, sines).astype(bf16)
    key_low_ref[...] = turn(key, cosines, sines).astype(bf16)
    value_low_ref[...] = value_ref[...].astype(bf16)
    for start in range(0, length, ATT_BLOCK):
        stop = start + ATT_BLOCK
        probs = block_probs(
            query_low_ref[start:stop],
            key_low_ref[:stop],
            row_seg_ref[start:stop, 0:1],
            col_seg_ref[0:1, :stop],
            HEAD_DIM ** (-0.5),
        )
        out = dot(probs.astype(bf16), value_low_ref[:stop], 1, 0)
        out_ref[start:stop] = out.astype(bf16)


def attend(projected, scales, gains, turns, row_segment, col_segment, heads):
    length = projected.shape[0]
    column = lambda part: pl.BlockSpec((length, HEAD_DIM), lambda h: (0, part * heads + h))
    whole = lambda shape: pl.BlockSpec(shape, lambda h: (0,) * len(shape))
    out = pl.BlockSpec((length, HEAD_DIM), lambda h: (0, h))
    return pl.pallas_call(
        attend_kernel,
        grid=(heads,),
        in_specs=[
            column(0), column(1), column(2), whole(scales.shape),
            pl.BlockSpec((2, HEAD_DIM), lambda h: (0, h)),
            whole(turns.shape), whole(row_segment.shape), whole(col_segment.shape),
        ],
        out_specs=[out] * 4,
        out_shape=[jax.ShapeDtypeStruct((length, heads * HEAD_DIM), bf16)] * 4,
        compiler_params=KERNEL_PARAMS,
        cost_estimate=SMALL_COST,
        name="attend",
    )(projected, projected, projected, scales, gains, turns, row_segment, col_segment)


def attend_back_kernel(
    query_ref, key_ref, value_ref, grad_ref, turn_ref, row_seg_ref, col_seg_ref,
    query_out_ref, key_out_ref, value_out_ref, key_sum_ref, value_sum_ref,
):
    length = query_ref.shape[0]
    scale = HEAD_DIM ** (-0.5)
    cosines, sines = turn_ref[0], -turn_ref[1]
    for start in reversed(range(0, length, ATT_BLOCK)):
        stop = start + ATT_BLOCK
        query_rows, grad_rows, keys = query_ref[start:stop], grad_ref[start:stop], key_ref[:stop]
        probs = block_probs(
            query_rows, keys, row_seg_ref[start:stop, 0:1], col_seg_ref[0:1, :stop], scale
        )
        value_terms = dot(probs.astype(bf16), grad_rows, 0, 0)
        prob_grad = dot(grad_rows, value_ref[:stop], 1, 1)
        inner = jnp.sum(probs * prob_grad, axis=1, keepdims=True)
        score_grad = (probs * (prob_grad - inner)).astype(bf16)
        query_grad = (dot(score_grad, keys, 1, 0) * scale).astype(bf16).astype(f32)
        query_out_ref[start:stop] = turn(query_grad, cosines[start:stop], sines[start:stop])
        key_terms = dot(score_grad, query_rows, 0, 0)
        if stop == length:
            key_sum_ref[...] = key_terms
            value_sum_ref[...] = value_terms
        else:
            key_sum_ref[:stop] += key_terms
            value_sum_ref[:stop] += value_terms
    key_grad = (key_sum_ref[...] * scale).astype(bf16).astype(f32)
    key_out_ref[...] = turn(key_grad, cosines, sines)
    value_out_ref[...] = value_sum_ref[...].astype(bf16)


def attend_back(queries, keys, values, grads, turns, row_segment, col_segment, heads):
    length = queries.shape[0]
    column = pl.BlockSpec((length, HEAD_DIM), lambda h: (0, h))
    whole = lambda shape: pl.BlockSpec(shape, lambda h: (0,) * len(shape))
    shape = (length, heads * HEAD_DIM)
    return pl.pallas_call(
        attend_back_kernel,
        grid=(heads,),
        in_specs=[column] * 4 + [whole(turns.shape), whole(row_segment.shape), whole(col_segment.shape)],
        out_specs=[column] * 3,
        out_shape=[
            jax.ShapeDtypeStruct(shape, f32),
            jax.ShapeDtypeStruct(shape, f32),
            jax.ShapeDtypeStruct(shape, bf16),
        ],
        scratch_shapes=[pltpu.VMEM((length, HEAD_DIM), f32)] * 2,
        compiler_params=KERNEL_PARAMS,
        cost_estimate=ATTEND_BACK_COST,
        name="attend_back",
    )(queries, keys, values, grads, turns, row_segment, col_segment)


def chunk_of(width, most):
    return most if width % most == 0 else width


def forward_kernel(count, kept, pick_ref, gate_ref, in_ref, down_ref, *refs):
    near_refs, refs = refs[:count], refs[count:]
    earlier_refs, refs = refs[4:kept], refs[kept:]
    rows_ref, gate_out_ref, up_out_ref, gated_ref = refs[:4]
    mix_refs = refs[4 : count + 4]
    result_ref, sums_ref = refs[count + 4 :]
    step_number, steps = pl.program_id(0), pl.num_programs(0)
    capacity, width = pick_ref.shape[2], rows_ref.shape[2]
    hidden = gated_ref.shape[2]
    for k in range(count):
        rows_ref[0, k * capacity : (k + 1) * capacity] = dot(
            pick_ref[0, k], near_refs[k][...], 1, 0
        ).astype(bf16)
    step = chunk_of(hidden, 512)

    @pl.loop(0, hidden // step)
    def _(j):
        low = pl.ds(pl.multiple_of(j * step, step), step)
        high = pl.ds(pl.multiple_of(hidden + j * step, step), step)
        gate = dot(rows_ref[0], in_ref[0, :, low], 1, 0)
        up = dot(rows_ref[0], in_ref[0, :, high], 1, 0)
        gate_out_ref[0, :, low] = gate.astype(bf16)
        up_out_ref[0, :, low] = up.astype(bf16)
        gated_ref[0, :, low] = (gate * jax.nn.sigmoid(gate) * up * gate_ref[0]).astype(bf16)

    wide = chunk_of(width, 1024)

    @pl.loop(0, width // wide)
    def _(j):
        cols = pl.ds(pl.multiple_of(j * wide, wide), wide)
        result_ref[...] = dot(gated_ref[0], down_ref[0, cols, :], 1, 1).astype(bf16)
        for k in range(count):
            part = dot(pick_ref[0, k], result_ref[k * capacity : (k + 1) * capacity], 0, 0)

            @pl.when(step_number == 0)
            def _():
                sums_ref[k, :, cols] = part

            @pl.when(step_number > 0)
            def _():
                sums_ref[k, :, cols] += part

    @pl.when(step_number == steps - 1)
    def _():
        for k in range(count):
            mix = sums_ref[k]
            if earlier_refs:
                mix = mix + earlier_refs[k][...].astype(f32)
            mix_refs[k][...] = mix.astype(bf16)


def experts_forward(first, kept, pick, gates, in_weight, down_weight, near):
    experts, count, capacity, tokens = pick.shape
    here, width, hidden = in_weight.shape[0], in_weight.shape[1], down_weight.shape[2]
    rows = count * capacity
    each = lambda shape: pl.BlockSpec((1,) + shape, lambda e: (first + e,) + (0,) * len(shape))
    near_each = lambda shape: pl.BlockSpec((1,) + shape, lambda e: (e,) + (0,) * len(shape))
    whole = pl.BlockSpec((tokens, width), lambda e: (0, 0), pipeline_mode=pl.Buffered(1))
    return pl.pallas_call(
        functools.partial(forward_kernel, count, len(kept)),
        grid=(here,),
        in_specs=[
            each((count, capacity, tokens)), each((rows, 1)),
            near_each((width, 2 * hidden)), near_each((width, hidden)),
        ] + [whole] * count + [pl.BlockSpec(memory_space=pl.ANY)] * len(kept[:4]) + [whole] * len(kept[4:]),
        out_specs=[each((rows, width))] + [each((rows, hidden))] * 3 + [whole] * count,
        out_shape=[jax.ShapeDtypeStruct((experts, rows, width), bf16)]
        + [jax.ShapeDtypeStruct((experts, rows, hidden), bf16)] * 3
        + [jax.ShapeDtypeStruct((tokens, width), bf16)] * count,
        scratch_shapes=[
            pltpu.VMEM((rows, chunk_of(width, 1024)), bf16),
            pltpu.VMEM((count, tokens, width), f32),
        ],
        input_output_aliases={4 + count + i: i for i in range(len(kept[:4]))},
        compiler_params=KERNEL_PARAMS,
        cost_estimate=SMALL_COST,
        name="experts_forward",
    )(pick, gates, in_weight, down_weight, *near, *kept)


def down_grad_kernel(count, pick_ref, gated_ref, *refs):
    near_refs = refs[:count]
    rows_ref, grad_ref = refs[count:]
    capacity, width = pick_ref.shape[2], rows_ref.shape[2]
    for k in range(count):
        rows_ref[0, k * capacity : (k + 1) * capacity] = dot(
            pick_ref[0, k], near_refs[k][...], 1, 0
        ).astype(bf16)
    step = chunk_of(width, 2048)

    @pl.loop(0, width // step)
    def _(j):
        cols = pl.ds(pl.multiple_of(j * step, step), step)
        grad_ref[0, cols, :] = dot(rows_ref[0, :, cols], gated_ref[0], 0, 0).astype(bf16)


def experts_down_grad(pick, gated, near):
    experts, count, capacity, tokens = pick.shape
    width, hidden = near[0].shape[1], gated.shape[2]
    rows = count * capacity
    each = lambda shape: pl.BlockSpec((1,) + shape, lambda e: (e,) + (0,) * len(shape))
    whole = pl.BlockSpec((tokens, width), lambda e: (0, 0), pipeline_mode=pl.Buffered(1))
    return pl.pallas_call(
        functools.partial(down_grad_kernel, count),
        grid=(experts,),
        in_specs=[each((count, capacity, tokens)), each((rows, hidden))] + [whole] * count,
        out_specs=[each((rows, width)), each((width, hidden))],
        out_shape=[
            jax.ShapeDtypeStruct((experts, rows, width), bf16),
            jax.ShapeDtypeStruct((experts, width, hidden), bf16),
        ],
        compiler_params=KERNEL_PARAMS,
        cost_estimate=DOWN_GRAD_COST,
        name="experts_down_grad",
    )(pick, gated, *near)


def backward_kernel(
    first, count, kept, pick_ref, gate_rows_ref, cot_ref, gate_ref, up_ref, in_ref, down_ref, *refs
):
    earlier_refs, refs = refs[1:kept], refs[kept:]
    both_ref = refs[0]
    copy_refs = refs[1 : 1 + count]
    result_ref, inner_ref, sums_ref, inner_sums_ref = refs[1 + count :]
    step_number, steps = pl.program_id(0), pl.num_programs(0)
    capacity, width = pick_ref.shape[2], cot_ref.shape[2]
    hidden = gate_ref.shape[2]
    lanes = inner_sums_ref.shape[2]
    step = chunk_of(hidden, 512)
    inner_ref[...] = jnp.zeros_like(inner_ref)

    @pl.when(step_number == 0)
    def _():
        inner_sums_ref[...] = jnp.zeros_like(inner_sums_ref)

    @pl.loop(0, hidden // step)
    def _(j):
        low = pl.ds(pl.multiple_of(j * step, step), step)
        high = pl.ds(pl.multiple_of(hidden + j * step, step), step)
        result_grad = dot(cot_ref[0], down_ref[0, :, low], 1, 0)
        gate, up = gate_ref[0, :, low].astype(f32), up_ref[0, :, low].astype(f32)
        sigmoid = jax.nn.sigmoid(gate)
        silu = gate * sigmoid
        inner_ref[...] += jnp.sum(result_grad * silu * up, axis=1, keepdims=True)
        act_grad = result_grad * gate_rows_ref[0]
        both_ref[0, :, low] = (act_grad * up * (sigmoid + silu * (1.0 - sigmoid))).astype(bf16)
        both_ref[0, :, high] = (act_grad * silu).astype(bf16)

    inner_high = inner_ref[...].astype(bf16).astype(f32)
    lane = lax.broadcasted_iota(jnp.int32, (count * capacity, lanes), 1)
    place = 2 * (first + step_number)
    inner_wide = jnp.where(lane == place, inner_high, 0.0)
    inner_wide = jnp.where(lane == place + 1, inner_ref[...] - inner_high, inner_wide)
    inner_wide = inner_wide.astype(bf16)
    for k in range(count):
        inner_sums_ref[k] += dot(pick_ref[0, k], inner_wide[k * capacity : (k + 1) * capacity], 0, 0)
    wide = chunk_of(width, 1024)

    @pl.loop(0, width // wide)
    def _(j):
        cols = pl.ds(pl.multiple_of(j * wide, wide), wide)
        result_ref[...] = dot(both_ref[0], in_ref[0, cols, :], 1, 1).astype(bf16)
        for k in range(count):
            part = dot(pick_ref[0, k], result_ref[k * capacity : (k + 1) * capacity], 0, 0)

            @pl.when(step_number == 0)
            def _():
                sums_ref[k, :, cols] = part

            @pl.when(step_number > 0)
            def _():
                sums_ref[k, :, cols] += part

    @pl.when(step_number == steps - 1)
    def _():
        for k in range(count):
            copies, inner = sums_ref[k], inner_sums_ref[k]
            if earlier_refs:
                copies = copies + earlier_refs[k][:, :width].astype(f32)
                inner = inner + earlier_refs[k][:, width:].astype(f32)
            copy_refs[k][:, :width] = copies.astype(bf16)
            copy_refs[k][:, width:] = inner.astype(bf16)


def experts_backward(first, kept, pick, gate_rows, cot_rows, gate, up, in_weight, down_weight):
    experts, count, capacity, tokens = pick.shape
    here, width, hidden = in_weight.shape[0], in_weight.shape[1], down_weight.shape[2]
    rows = count * capacity
    lanes = 128 * -(-2 * experts // 128)
    each = lambda shape: pl.BlockSpec((1,) + shape, lambda e: (first + e,) + (0,) * len(shape))
    near_each = lambda shape: pl.BlockSpec((1,) + shape, lambda e: (e,) + (0,) * len(shape))
    whole = pl.BlockSpec((tokens, width + lanes), lambda e: (0, 0), pipeline_mode=pl.Buffered(1))
    return pl.pallas_call(
        functools.partial(backward_kernel, first, count, len(kept)),
        grid=(here,),
        in_specs=[
            each((count, capacity, tokens)), each((rows, 1)), each((rows, width)),
            each((rows, hidden)), each((rows, hidden)),
            near_each((width, 2 * hidden)), near_each((width, hidden)),
        ] + [pl.BlockSpec(memory_space=pl.ANY)] * len(kept[:1]) + [whole] * len(kept[1:]),
        out_specs=[each((rows, 2 * hidden))] + [whole] * count,
        out_shape=[jax.ShapeDtypeStruct((experts, rows, 2 * hidden), bf16)]
        + [jax.ShapeDtypeStruct((tokens, width + lanes), bf16)] * count,
        scratch_shapes=[
            pltpu.VMEM((rows, chunk_of(width, 1024)), bf16),
            pltpu.VMEM((rows, 1), f32),
            pltpu.VMEM((count, tokens, width), f32),
            pltpu.VMEM((count, tokens, lanes), f32),
        ],
        input_output_aliases={7 + i: i for i in range(len(kept[:1]))},
        compiler_params=KERNEL_PARAMS,
        cost_estimate=SMALL_COST,
        name="experts_backward",
    )(pick, gate_rows, cot_rows, gate, up, in_weight, down_weight, *kept)


def in_grad_kernel(rows_ref, both_ref, earlier_ref, grad_ref):
    width = rows_ref.shape[2]
    step = chunk_of(width, 512)

    @pl.loop(0, width // step)
    def _(j):
        cols = pl.ds(pl.multiple_of(j * step, step), step)
        grad_ref[0, cols, :] = dot(rows_ref[0, :, cols], both_ref[0], 0, 0).astype(bf16)


def experts_in_grad(rows, both, earlier):
    experts, count, width = rows.shape
    each = lambda shape: pl.BlockSpec((1,) + shape, lambda e: (e,) + (0,) * len(shape))
    return pl.pallas_call(
        in_grad_kernel,
        grid=(experts,),
        in_specs=[each(rows.shape[1:]), each(both.shape[1:]), pl.BlockSpec(memory_space=pl.ANY)],
        out_specs=each((width, both.shape[2])),
        out_shape=jax.ShapeDtypeStruct((experts, width, both.shape[2]), bf16),
        compiler_params=KERNEL_PARAMS,
        cost_estimate=SMALL_COST,
        name="experts_in_grad",
    )(rows, both, earlier)


def spread_kernel(split, left_ref, right_ref, *refs):
    groups, parts, cores = split
    out_ref = refs[-1]
    width = right_ref.shape[1]
    rows = out_ref.shape[2] // groups
    each = parts * cores * rows
    for group in range(groups):
        terms = dot(left_ref[:, group * each : (group + 1) * each], right_ref[...], 0, 0).astype(bf16)
        for part in range(parts):
            for core in range(cores):
                start = (part * cores + core) * rows
                place = pl.ds(group * rows, rows)
                out_ref[core, part, place, :width] = terms[start : start + rows]
                if len(refs) > 1:
                    begin = group * each + start
                    out_ref[core, part, place, width:] = refs[0][begin : begin + rows, :]


def spread_product(left, right, beside, split):
    groups, parts, cores = split
    rows = left.shape[1] // (groups * parts * cores)
    width = right.shape[1] + sum(array.shape[1] for array in beside)
    return pl.pallas_call(
        functools.partial(spread_kernel, split),
        out_shape=jax.ShapeDtypeStruct((cores, parts, groups * rows, width), bf16),
        compiler_params=KERNEL_PARAMS,
        cost_estimate=SMALL_COST,
        name="spread_product",
    )(left, right, *beside)


def on_device(
    tokens,
    cotangent,
    expert_ids,
    segment_ids,
    norm_gains,
    w_qkv,
    w_out,
    router,
    expert_in,
    expert_out,
):
    own_low = tokens[0]
    inputs = own_low.astype(f32)
    tok_count, model_width = inputs.shape
    segment = segment_ids[0]
    length = segment.shape[0]
    seq_count = lax.axis_size("seq")
    exp_count = lax.axis_size("exp")
    core_count = lax.axis_size("fsdp")
    own_seq = lax.axis_index("seq")
    own_exp = lax.axis_index("exp")
    rows_dev = w_qkv.shape[0]
    heads_dev = HEADS // seq_count
    head_cols = heads_dev * HEAD_DIM
    experts_total = router.shape[1]
    exp_dev = expert_in.shape[1]

    small = jnp.concatenate([norm_gains, router], axis=1)
    small_cols = small.shape[1]
    ids_room = TOP * tok_count // (seq_count * rows_dev)
    small = jnp.pad(small, ((0, 0), (0, ids_room + -(small_cols + ids_room) % 128)))
    heads_rows = w_qkv.reshape(rows_dev, 3, seq_count, head_cols).transpose(2, 0, 1, 3)
    heads_rows = heads_rows.reshape(seq_count, rows_dev, 3 * head_cols)
    small = jnp.broadcast_to(small[None], (seq_count,) + small.shape)
    heads_seq = exchange(jnp.concatenate([heads_rows, small], axis=2), "seq")
    ids_low = expert_ids[0].astype(bf16).reshape(seq_count, rows_dev, -1)
    first_id = 3 * head_cols + small_cols
    ids_cols = ids_low.shape[2]
    after_ids = heads_seq.shape[2] - first_id - ids_cols
    heads_rows = heads_seq + jnp.pad(ids_low, ((0, 0), (0, 0), (first_id, after_ids)))
    heads_near = gather_near(heads_rows.reshape(seq_count * rows_dev, -1), "exp")
    ids_group = jnp.stack(
        [near[:, first_id : first_id + ids_cols].reshape(tok_count, TOP) for near in heads_near]
    )
    heads_all = order_cores(heads_near, seq_count, "exp", "fsdp")
    heads_weight = heads_all[:, : 3 * head_cols]
    small = heads_all[:, 3 * head_cols : first_id].T
    gains = small[:4].astype(f32)
    router_rows = small[4:]
    all_tokens = jnp.broadcast_to(own_low[None], (seq_count, tok_count, model_width))
    all_tokens = exchange(all_tokens, "seq").reshape(length, model_width)

    out_rows = after(w_out, all_tokens)[None]
    out_rows = exchange(jnp.broadcast_to(out_rows, (seq_count,) + w_out.shape), "seq")
    out_rows = out_rows.reshape(seq_count * rows_dev, model_width)
    out_near = gather_near(after(out_rows, heads_near[-1]), "exp")

    parts = 2 if exp_dev % 2 == 0 else 1
    part_experts = exp_dev // parts
    in_blocks = jnp.transpose(after(expert_in, heads_seq), (1, 0, 2))
    down_blocks = jnp.transpose(after(expert_out, heads_seq), (1, 0, 2))
    in_weights, down_weights = [], []
    for part in range(parts):
        chosen_experts = slice(part * part_experts, (part + 1) * part_experts)
        for blocks, weights in ((in_blocks, in_weights), (down_blocks, down_weights)):
            weights.append(
                lax.all_gather(blocks[chosen_experts], ("seq", "fsdp"), axis=1, tiled=True)
            )

    all_inputs = all_tokens.astype(f32)
    first_inverse = rms_inverse(all_inputs)
    attn_low = (all_inputs * first_inverse * gains[0]).astype(bf16)
    projected = jnp.dot(attn_low, heads_weight, preferred_element_type=f32)
    own_gains = lax.dynamic_slice_in_dim(gains, own_seq * head_cols, head_cols, 1)
    query_pre, key_pre = projected[:, :head_cols], projected[:, head_cols : 2 * head_cols]
    squares = jnp.stack([jnp.sum(query_pre * query_pre, axis=-1), jnp.sum(key_pre * key_pre, axis=-1)])
    squares = sum_all(squares, "seq")
    scales = lax.rsqrt(squares / model_width + epsilon).T
    query_inverse, key_inverse = scales[:, 0:1], scales[:, 1:2]
    turns = rotary_tables(jnp.arange(length, dtype=jnp.int32), HEAD_DIM)
    row_segment, col_segment = segment[:, None], segment[None, :]
    attended, queries, keys, values = attend(
        projected, after(scales, out_near[-1]), own_gains[1:3], turns, row_segment, col_segment, heads_dev
    )
    out_weight = order_cores(out_near, seq_count, "exp", "fsdp")
    merged = lax.all_to_all(attended, "seq", split_axis=0, concat_axis=1, tiled=True)
    branch = jnp.einsum("tc,dc->td", merged, out_weight, preferred_element_type=f32)
    residual = inputs + branch
    mlp_inverse = rms_inverse(residual)
    mlp_low = (residual * mlp_inverse * gains[3]).astype(bf16)

    capacity = tok_count * TOP // experts_total * 9 // 8
    near_experts = own_exp * exp_dev + jnp.arange(exp_dev, dtype=jnp.int32)
    chosen = jnp.any(
        ids_group[:, :, :, None] == near_experts.astype(bf16)[None, None, None, :], axis=2
    )
    earlier = (
        jnp.arange(tok_count)[:, None] > jnp.arange(tok_count)[None, :]
    ).astype(bf16)
    rank = jnp.einsum("tu,sue->est", earlier, chosen.astype(bf16), preferred_element_type=f32)
    rank = jnp.where(jnp.transpose(chosen, (2, 0, 1)), rank, -1.0)
    pick = rank[:, :, None, :] == jnp.arange(capacity, dtype=f32)[None, None, :, None]
    pick_low = pick.astype(bf16)

    mlp_near = gather_near(mlp_low, "exp")
    cot_near = cotangent[0]
    for near in mlp_near[1:]:
        cot_near = after(cot_near, near)
    cot_near = gather_near(cot_near, "exp")
    logits = jnp.stack(
        [jnp.einsum("td,ed->te", near, router_rows, preferred_element_type=f32) for near in mlp_near]
    )
    group_probs = jax.nn.softmax(logits, axis=-1)
    router_probs = group_probs[0]
    near_probs = lax.dynamic_slice_in_dim(group_probs, own_exp * exp_dev, exp_dev, 2)
    near_probs = jnp.transpose(near_probs, (2, 0, 1))
    gate_rows = jnp.sum(jnp.where(pick, near_probs[:, :, None, :], 0.0), axis=-1)
    gate_rows = gate_rows.reshape(exp_dev, exp_count * capacity, 1)
    kept = []
    for part in range(parts):
        kept = experts_forward(
            part * part_experts, kept, pick_low, gate_rows, in_weights[part], down_weights[part], mlp_near
        )
    expert_rows, gate, up, gated = kept[:4]
    mix_near = send_near(kept[4:], "exp")
    output = (residual + add_up(mix_near)).astype(bf16)

    cot_rows, down_grad = experts_down_grad(pick_low, gated, cot_near)
    grad_expert_out = lax.psum_scatter(
        down_grad, ("seq", "fsdp"), scatter_dimension=1, tiled=True
    )
    kept = []
    for part in range(parts):
        kept = experts_backward(
            part * part_experts, kept, pick_low, gate_rows, cot_rows, gate, up,
            in_weights[part], down_weights[part],
        )
    copy_near = send_near(kept[1:], "exp")
    earlier = jnp.stack([block[:8, :128] for block in kept[1:]] + [output[:8, :128]])
    in_grad = experts_in_grad(expert_rows, kept[0], earlier)
    grad_expert_in = lax.psum_scatter(in_grad, ("seq", "fsdp"), scatter_dimension=1, tiled=True)
    copy_near[0] = after(copy_near[0], in_grad)
    mlp_grad_experts = add_up([near[:, :model_width] for near in copy_near])
    prob_pairs = [
        near[:, model_width : model_width + 2 * exp_dev].astype(f32).reshape(tok_count, exp_dev, 2)
        for near in copy_near
    ]
    prob_grad = order([jnp.sum(pair, axis=2) for pair in prob_pairs], "exp", 1, 1)
    prob_grad = prob_grad.reshape(tok_count, experts_total)
    grad_expert_in = jnp.transpose(grad_expert_in, (1, 0, 2)).astype(f32)
    grad_expert_out = jnp.transpose(grad_expert_out, (1, 0, 2)).astype(f32)

    logit_grad = router_probs * (
        prob_grad - jnp.sum(router_probs * prob_grad, axis=-1, keepdims=True)
    )
    router_grad = jnp.dot(logit_grad.T, mlp_low.astype(f32), precision=highest)
    mlp_grad = mlp_grad_experts + jnp.dot(
        logit_grad, router_rows.astype(f32), precision=highest
    )
    residual_norm_grad, mlp_gain_grad = rms_back(mlp_grad, residual, mlp_inverse, gains[3])
    residual_grad = cotangent[0].astype(f32) + residual_norm_grad
    branch_grad = residual_grad.astype(bf16)

    merged_grad = jnp.einsum("td,dc->tc", branch_grad, out_weight, preferred_element_type=f32)
    heads_grad = lax.all_to_all(
        merged_grad.astype(bf16), "seq", split_axis=1, concat_axis=0, tiled=True
    )
    split_sizes = (seq_count, exp_count, core_count)
    out_terms = spread_product(after(branch_grad, merged_grad), merged, [], split_sizes)
    out_terms = scatter_core(out_terms, "fsdp")
    out_terms = scatter(out_terms, "exp").astype(bf16)
    query_grad, key_grad, value_grad = attend_back(
        queries, keys, values, heads_grad, turns, row_segment, col_segment, heads_dev
    )
    query_scaled, key_scaled = query_grad * own_gains[1], key_grad * own_gains[2]
    means = jnp.stack(
        [jnp.sum(query_scaled * query_pre, axis=-1), jnp.sum(key_scaled * key_pre, axis=-1)]
    )
    means = after(sum_all(means, "seq") / model_width, out_terms)
    query_gain_grad = jnp.sum(query_grad * query_pre * query_inverse, axis=0)
    key_gain_grad = jnp.sum(key_grad * key_pre * key_inverse, axis=0)
    query_pre_grad = query_inverse * query_scaled - query_pre * query_inverse**3 * means[0][:, None]
    key_pre_grad = key_inverse * key_scaled - key_pre * key_inverse**3 * means[1][:, None]
    qkv_grad = jnp.concatenate(
        [query_pre_grad.astype(bf16), key_pre_grad.astype(bf16), value_grad],
        axis=1,
    )
    attn_in_part = jnp.einsum("tc,dc->td", qkv_grad, heads_weight, preferred_element_type=f32)
    first_gain_grad = jnp.sum(attn_in_part * all_inputs * first_inverse, axis=0)
    attn_in_grad = scatter(
        attn_in_part.astype(bf16).reshape(seq_count, tok_count, model_width), "seq"
    )
    zero_row = jnp.zeros((model_width,), f32)
    small_terms = jnp.concatenate(
        [
            jnp.stack(
                [
                    first_gain_grad,
                    lax.dynamic_update_slice_in_dim(zero_row, query_gain_grad, own_seq * head_cols, 0),
                    lax.dynamic_update_slice_in_dim(zero_row, key_gain_grad, own_seq * head_cols, 0),
                    mlp_gain_grad,
                ]
            ),
            router_grad,
        ],
        axis=0,
    ).T
    small_terms = jnp.pad(small_terms, ((0, 0), (0, -small_cols % 128)))
    heads_terms = spread_product(attn_low, qkv_grad, [small_terms.astype(bf16)], split_sizes)
    heads_terms = scatter_core(heads_terms, "fsdp")
    heads_terms = scatter(heads_terms, "exp").astype(bf16)
    grad_w_out = scatter(
        after(out_terms, heads_terms).reshape(seq_count, rows_dev, model_width), "seq"
    )
    heads_terms = heads_terms.reshape(seq_count, rows_dev, -1)
    heads_terms = after(after(heads_terms, grad_expert_in), grad_expert_out)
    heads_given, heads_terms = heads_terms, exchange(heads_terms, "seq")
    grad_w_qkv = jnp.concatenate(
        [
            heads_terms[source, :, part * head_cols : (part + 1) * head_cols]
            for part in range(3)
            for source in range(seq_count)
        ],
        axis=1,
    ).astype(f32)
    own_inverse = lax.dynamic_slice_in_dim(first_inverse, own_seq * tok_count, tok_count, 0)
    input_norm_grad, _ = rms_back(after(attn_in_grad, heads_given), inputs, own_inverse, gains[0])
    input_grad = residual_grad + input_norm_grad

    small_grad = jnp.sum(
        heads_terms[:, :, 3 * head_cols : 3 * head_cols + small_cols].astype(f32), axis=0
    )
    return (
        output[None],
        input_grad[None],
        small_grad[:, :4],
        grad_w_qkv,
        grad_w_out,
        small_grad[:, 4:],
        grad_expert_in,
        grad_expert_out,
    )


def solution(mesh):
    in_specs = (
        P(("exp", "fsdp"), "seq", None),
        P(("exp", "fsdp"), "seq", None),
        P(("exp", "fsdp"), "seq", None),
        P(("exp", "fsdp"), None),
        P(("seq", "exp", "fsdp"), None),
        P(("seq", "exp", "fsdp"), None),
        P(("seq", "exp", "fsdp"), None),
        P(("seq", "exp", "fsdp"), None),
        P(("seq", "fsdp"), "exp", None),
        P(("seq", "fsdp"), "exp", None),
    )
    out_specs = (
        P(("exp", "fsdp"), "seq", None),
        P(("exp", "fsdp"), "seq", None),
        P(("seq", "exp", "fsdp"), None),
        P(("seq", "exp", "fsdp"), None),
        P(("seq", "exp", "fsdp"), None),
        P(("seq", "exp", "fsdp"), None),
        P(("seq", "fsdp"), "exp", None),
        P(("seq", "fsdp"), "exp", None),
    )
    return jax.shard_map(
        on_device, mesh=mesh, in_specs=in_specs, out_specs=out_specs, check_vma=False
    )
```

```python
import functools

import jax
import jax.numpy as jnp
from jax import lax
from jax.experimental import pallas as pl
from jax.experimental.pallas import tpu as pltpu
from jax.sharding import PartitionSpec as P

HEADS = 16
HEAD_DIM = 128
FF = 1024
TOP = 8
ATT_BLOCK = 256


epsilon = 1e-05
rotary_base = 10000.0
highest = lax.Precision.HIGHEST
f32 = jnp.float32
bf16 = jnp.bfloat16
VMEM_BYTES = 63 * 1024 * 1024
KERNEL_PARAMS = pltpu.CompilerParams(vmem_limit_bytes=VMEM_BYTES)
SMALL_COST = pl.CostEstimate(flops=1, bytes_accessed=1, transcendentals=0)
DOWN_GRAD_COST = pl.CostEstimate(flops=10**11, bytes_accessed=1, transcendentals=0)
ATTEND_BACK_COST = pl.CostEstimate(flops=250 * 10**9, bytes_accessed=1, transcendentals=0)


def after(value, other):
    first = lax.slice(other, (0,) * other.ndim, (1,) * other.ndim).reshape(())
    return value + (0.0 * first.astype(f32)).astype(value.dtype)


def swap_pairs(count, mask):
    return [(i, i ^ mask) for i in range(count)]


def shift_pairs(count, step):
    return [(i, (i + step) % count) for i in range(count)]


def ring_place(index, count):
    return index & (count - 1) if count & (count - 1) == 0 else lax.rem(index + count, count)


def exchange(stacked, axis, split_axis=0):
    return lax.all_to_all(stacked, axis, split_axis=split_axis, concat_axis=split_axis, tiled=True)


def gather_near(block, axis):
    count = lax.axis_size(axis)
    return [block] + [
        lax.ppermute(block, axis, shift_pairs(count, k)) for k in range(1, count)
    ]


def send_near(blocks, axis):
    count = lax.axis_size(axis)
    return [blocks[0]] + [
        lax.ppermute(blocks[k], axis, shift_pairs(count, -k)) for k in range(1, count)
    ]


def add_up(blocks):
    return sum(block.astype(f32) for block in blocks)


def order(blocks, axis, out_axis=0, sign=-1):
    count = lax.axis_size(axis)
    own = lax.axis_index(axis)
    shape = blocks[0].shape[:out_axis] + (count,) + blocks[0].shape[out_axis:]
    out = jnp.zeros(shape, blocks[0].dtype)
    for k, block in enumerate(blocks):
        place = ring_place(own + sign * k, count)
        out = lax.dynamic_update_index_in_dim(out, block, place, out_axis)
    return out


def split(stacked, axis, in_axis=0, sign=-1):
    count = lax.axis_size(axis)
    own = lax.axis_index(axis)
    return [
        lax.dynamic_index_in_dim(
            stacked, ring_place(own + sign * k, count), in_axis, keepdims=False
        )
        for k in range(count)
    ]


def gather(block, axis, out_axis=0):
    return order(gather_near(block, axis), axis, out_axis)


def scatter(stacked, axis, split_axis=0):
    return add_up(send_near(split(stacked, axis, split_axis), axis))


def sum_all(value, axis):
    count = lax.axis_size(axis)
    return jnp.sum(exchange(jnp.broadcast_to(value[None], (count,) + value.shape), axis), axis=0)


def assemble_kernel(groups, parts, place_ref, *refs):
    sources, out_ref, sems = refs[: len(refs) - 2], refs[-2], refs[-1]
    rows = sources[0].shape[0] // groups
    copies = []
    for k, source in enumerate(sources):
        for group in range(groups):
            target = pl.multiple_of((group * parts + place_ref[k]) * rows, rows)
            copies.append(
                pltpu.make_async_copy(
                    source.at[pl.ds(group * rows, rows)],
                    out_ref.at[pl.ds(target, rows)],
                    sems.at[k, group],
                )
            )
    for copy in copies:
        copy.start()
    for copy in copies:
        copy.wait()


def assemble(blocks, places, groups):
    parts = len(blocks)
    return pl.pallas_call(
        functools.partial(assemble_kernel, groups, parts),
        in_specs=[pl.BlockSpec(memory_space=pltpu.SMEM)]
        + [pl.BlockSpec(memory_space=pltpu.VMEM)] * parts,
        out_specs=pl.BlockSpec(memory_space=pl.ANY),
        out_shape=jax.ShapeDtypeStruct(
            (parts * blocks[0].shape[0], blocks[0].shape[1]), blocks[0].dtype
        ),
        scratch_shapes=[pltpu.SemaphoreType.DMA((parts, groups))],
        compiler_params=KERNEL_PARAMS,
        cost_estimate=SMALL_COST,
        name="assemble",
    )(places, *blocks)


def order_cores(blocks, groups, axis, core_axis):
    count, cores = lax.axis_size(axis), lax.axis_size(core_axis)
    own, own_core = lax.axis_index(axis), lax.axis_index(core_axis)
    if cores == 2:
        blocks = blocks + [lax.ppermute(block, core_axis, swap_pairs(2, 1)) for block in blocks]
        core_places = [own_core, 1 - own_core]
    else:
        every = lax.all_gather(jnp.stack(blocks), core_axis, axis=0)
        blocks = [every[core, k] for core in range(cores) for k in range(count)]
        core_places = list(range(cores))
    places = [
        ring_place(own - k, count) * cores + core for core in core_places for k in range(count)
    ]
    places = jnp.stack([jnp.asarray(place, jnp.int32) for place in places])
    return assemble(blocks, places, groups)


def scatter_core(terms, axis, earlier=()):
    if len(terms) == 1:
        return lax.psum_scatter(terms[0], axis, scatter_dimension=0, tiled=False)
    kept, given = terms
    for array in earlier:
        given = after(given, array)
    received = lax.ppermute(given, axis, swap_pairs(2, 1))
    return (kept.astype(f32) + received.astype(f32)).astype(kept.dtype)


def rms_inverse(values):
    return lax.rsqrt(jnp.mean(values * values, axis=-1, keepdims=True) + epsilon)


def rms_back(gradient, values, inverse, gain_vector):
    scaled = gradient * gain_vector
    gain_grad = jnp.sum(gradient * values * inverse, axis=0)
    value_grad = inverse * scaled - values * inverse**3 * jnp.mean(
        scaled * values, axis=-1, keepdims=True
    )
    return (value_grad, gain_grad)


def rotary_tables(position, head_dim):
    half_dim = head_dim // 2
    exponent = jnp.arange(half_dim, dtype=f32) * (2.0 / head_dim)
    angles = position.astype(f32)[:, None] * (rotary_base ** (-exponent))[None, :]
    cosine, sine_part = jnp.cos(angles), jnp.sin(angles)
    return jnp.stack(
        [
            jnp.concatenate([cosine, cosine], axis=1),
            jnp.concatenate([-sine_part, sine_part], axis=1),
        ]
    )


def dot(one, other, one_axis, other_axis):
    return lax.dot_general(
        one, other, (((one_axis,), (other_axis,)), ((), ())), preferred_element_type=f32
    )


def turn(values, cosines, sines):
    return values * cosines + pltpu.roll(values, HEAD_DIM // 2, 1) * sines


def block_probs(query_rows, keys, query_segment, key_segment, scale):
    scores = dot(query_rows, keys, 1, 1) * scale
    scores = jnp.where(query_segment == key_segment, scores, -jnp.inf)
    terms = jnp.exp(scores - jnp.max(scores, axis=1, keepdims=True))
    return terms / jnp.sum(terms, axis=1, keepdims=True)


def attend_kernel(
    query_ref, key_ref, value_ref, scale_ref, gain_ref, turn_ref, row_seg_ref, col_seg_ref,
    out_ref, query_low_ref, key_low_ref, value_low_ref,
):
    length = query_ref.shape[0]
    cosines, sines = turn_ref[0], turn_ref[1]
    query = query_ref[...] * scale_ref[:, 0:1] * gain_ref[0:1, :]
    key = key_ref[...] * scale_ref[:, 1:2] * gain_ref[1:2, :]
    query_low_ref[...] = turn(query, cosines, sines).astype(bf16)
    key_low_ref[...] = turn(key, cosines, sines).astype(bf16)
    value_low_ref[...] = value_ref[...].astype(bf16)
    for start in range(0, length, ATT_BLOCK):
        stop = start + ATT_BLOCK
        probs = block_probs(
            query_low_ref[start:stop],
            key_low_ref[:stop],
            row_seg_ref[start:stop, 0:1],
            col_seg_ref[0:1, :stop],
            HEAD_DIM ** (-0.5),
        )
        out = dot(probs.astype(bf16), value_low_ref[:stop], 1, 0)
        out_ref[start:stop] = out.astype(bf16)


def attend(projected, scales, gains, turns, row_segment, col_segment, heads):
    length = projected.shape[0]
    column = lambda part: pl.BlockSpec((length, HEAD_DIM), lambda h: (0, part * heads + h))
    whole = lambda shape: pl.BlockSpec(shape, lambda h: (0,) * len(shape))
    out = pl.BlockSpec((length, HEAD_DIM), lambda h: (0, h))
    return pl.pallas_call(
        attend_kernel,
        grid=(heads,),
        in_specs=[
            column(0), column(1), column(2), whole(scales.shape),
            pl.BlockSpec((2, HEAD_DIM), lambda h: (0, h)),
            whole(turns.shape), whole(row_segment.shape), whole(col_segment.shape),
        ],
        out_specs=[out] * 4,
        out_shape=[jax.ShapeDtypeStruct((length, heads * HEAD_DIM), bf16)] * 4,
        compiler_params=KERNEL_PARAMS,
        cost_estimate=SMALL_COST,
        name="attend",
    )(projected, projected, projected, scales, gains, turns, row_segment, col_segment)


def attend_back_kernel(
    query_ref, key_ref, value_ref, grad_ref, query_pre_ref, key_pre_ref, gain_ref, turn_ref,
    row_seg_ref, col_seg_ref, earlier_ref,
    query_out_ref, key_out_ref, value_out_ref, inner_ref, key_sum_ref, value_sum_ref,
):
    length = query_ref.shape[0]
    scale = HEAD_DIM ** (-0.5)
    cosines, sines = turn_ref[0], -turn_ref[1]
    first = pl.program_id(0) == 0
    for start in reversed(range(0, length, ATT_BLOCK)):
        stop = start + ATT_BLOCK
        query_rows, grad_rows, keys = query_ref[start:stop], grad_ref[start:stop], key_ref[:stop]
        probs = block_probs(
            query_rows, keys, row_seg_ref[start:stop, 0:1], col_seg_ref[0:1, :stop], scale
        )
        value_terms = dot(probs.astype(bf16), grad_rows, 0, 0)
        prob_grad = dot(grad_rows, value_ref[:stop], 1, 1)
        inner = jnp.sum(probs * prob_grad, axis=1, keepdims=True)
        score_grad = (probs * (prob_grad - inner)).astype(bf16)
        query_grad = (dot(score_grad, keys, 1, 0) * scale).astype(bf16).astype(f32)
        query_grad = turn(query_grad, cosines[start:stop], sines[start:stop])
        query_out_ref[start:stop] = query_grad
        query_inner = query_grad * gain_ref[0:1, :] * query_pre_ref[start:stop]
        query_inner = jnp.sum(query_inner, axis=1, keepdims=True)
        inner_ref[start:stop, 0:1] = query_inner + jnp.where(first, 0.0, inner_ref[start:stop, 0:1])
        key_terms = dot(score_grad, query_rows, 0, 0)
        if stop == length:
            key_sum_ref[...] = key_terms
            value_sum_ref[...] = value_terms
        else:
            key_sum_ref[:stop] += key_terms
            value_sum_ref[:stop] += value_terms
    key_grad = (key_sum_ref[...] * scale).astype(bf16).astype(f32)
    key_grad = turn(key_grad, cosines, sines)
    key_out_ref[...] = key_grad
    key_inner = jnp.sum(key_grad * gain_ref[1:2, :] * key_pre_ref[...], axis=1, keepdims=True)
    inner_ref[:, 1:2] = key_inner + jnp.where(first, 0.0, inner_ref[:, 1:2])
    value_out_ref[...] = value_sum_ref[...].astype(bf16)


def attend_back(
    queries, keys, values, grads, projected, gains, turns, row_segment, col_segment, earlier, heads
):
    length = queries.shape[0]
    column = pl.BlockSpec((length, HEAD_DIM), lambda h: (0, h))
    whole = lambda shape: pl.BlockSpec(shape, lambda h: (0,) * len(shape))
    shape = (length, heads * HEAD_DIM)
    return pl.pallas_call(
        attend_back_kernel,
        grid=(heads,),
        in_specs=[column] * 4
        + [column, pl.BlockSpec((length, HEAD_DIM), lambda h: (0, heads + h))]
        + [pl.BlockSpec((2, HEAD_DIM), lambda h: (0, h))]
        + [whole(turns.shape), whole(row_segment.shape), whole(col_segment.shape)]
        + [pl.BlockSpec(memory_space=pl.ANY)],
        out_specs=[column] * 3 + [whole((length, 2))],
        out_shape=[
            jax.ShapeDtypeStruct(shape, f32),
            jax.ShapeDtypeStruct(shape, f32),
            jax.ShapeDtypeStruct(shape, bf16),
            jax.ShapeDtypeStruct((length, 2), f32),
        ],
        scratch_shapes=[pltpu.VMEM((length, HEAD_DIM), f32)] * 2,
        compiler_params=KERNEL_PARAMS,
        cost_estimate=ATTEND_BACK_COST,
        name="attend_back",
    )(
        queries, keys, values, grads, projected, projected, gains, turns, row_segment, col_segment, earlier
    )


def interleave_kernel(*refs):
    expert = 0
    for ref in refs[:-1]:
        for k in range(ref.shape[0]):
            refs[-1][:, expert, :] = ref[k].astype(f32)
            expert += 1


def interleave(parts):
    _, rows, width = parts[0].shape
    experts = sum(part.shape[0] for part in parts)
    block = min(rows, 64)
    return pl.pallas_call(
        interleave_kernel,
        grid=(rows // block,),
        in_specs=[
            pl.BlockSpec((part.shape[0], block, width), lambda i: (0, i, 0)) for part in parts
        ],
        out_specs=pl.BlockSpec((block, experts, width), lambda i: (i, 0, 0)),
        out_shape=jax.ShapeDtypeStruct((rows, experts, width), f32),
        compiler_params=KERNEL_PARAMS,
        cost_estimate=SMALL_COST,
        name="interleave",
    )(*parts)


def norm_back_kernel(
    query_grad_ref, key_grad_ref, value_grad_ref, query_pre_ref, key_pre_ref, scale_ref, mean_ref, gain_ref,
    out_ref, gain_grad_ref,
):
    width = query_grad_ref.shape[1]

    @pl.when(pl.program_id(0) == 0)
    def _():
        gain_grad_ref[...] = jnp.zeros_like(gain_grad_ref)

    for part, (grad_ref, pre_ref) in enumerate(
        ((query_grad_ref, query_pre_ref), (key_grad_ref, key_pre_ref))
    ):
        here = slice(part, part + 1)
        grad, scale = grad_ref[...], scale_ref[:, here]
        normal = pre_ref[...] * scale
        gain_grad_ref[here, :] += jnp.sum(grad * normal, axis=0, keepdims=True)
        back = scale * (grad * gain_ref[here, :]) - normal * (scale * scale * mean_ref[:, here])
        out_ref[:, part * width : (part + 1) * width] = back.astype(bf16)
    out_ref[:, 2 * width :] = value_grad_ref[...]


def norm_back(query_grad, key_grad, value_grad, projected, scales, means, gains):
    length, width = query_grad.shape
    block = min(length, 256)
    rows = lambda columns, part: pl.BlockSpec((block, columns), lambda i: (i, part))
    whole = lambda shape: pl.BlockSpec(shape, lambda i: (0,) * len(shape))
    return pl.pallas_call(
        norm_back_kernel,
        grid=(length // block,),
        in_specs=[rows(width, 0)] * 3
        + [rows(width, 0), rows(width, 1), rows(2, 0), rows(2, 0), whole(gains.shape)],
        out_specs=[rows(3 * width, 0), whole(gains.shape)],
        out_shape=[
            jax.ShapeDtypeStruct((length, 3 * width), bf16),
            jax.ShapeDtypeStruct(gains.shape, f32),
        ],
        compiler_params=KERNEL_PARAMS,
        cost_estimate=SMALL_COST,
        name="norm_back",
    )(query_grad, key_grad, value_grad, projected, projected, scales, means, gains)


def chunk_of(width, most):
    return most if width % most == 0 else width


def forward_kernel(count, kept, place_ref, pick_ref, gate_ref, in_ref, down_ref, *refs):
    near_refs, refs = refs[:count], refs[count:]
    earlier_refs, refs = refs[4:kept], refs[kept:]
    rows_ref, gate_out_ref, up_out_ref, gated_ref, mix_ref, result_ref, sums_ref = refs
    step_number, steps = pl.program_id(0), pl.num_programs(0)
    capacity, width = pick_ref.shape[2], rows_ref.shape[2]
    hidden = gated_ref.shape[2]
    for k in range(count):
        rows_ref[0, k * capacity : (k + 1) * capacity] = dot(
            pick_ref[0, k], near_refs[k][...], 1, 0
        ).astype(bf16)
    step = chunk_of(hidden, 512)

    @pl.loop(0, hidden // step)
    def _(j):
        low = pl.ds(pl.multiple_of(j * step, step), step)
        high = pl.ds(pl.multiple_of(hidden + j * step, step), step)
        gate = dot(rows_ref[0], in_ref[0, :, low], 1, 0)
        up = dot(rows_ref[0], in_ref[0, :, high], 1, 0)
        gate_out_ref[0, :, low] = gate.astype(bf16)
        up_out_ref[0, :, low] = up.astype(bf16)
        gated_ref[0, :, low] = (gate * jax.nn.sigmoid(gate) * up * gate_ref[0]).astype(bf16)

    wide = chunk_of(width, 1024)

    @pl.loop(0, width // wide)
    def _(j):
        cols = pl.ds(pl.multiple_of(j * wide, wide), wide)
        result_ref[...] = dot(gated_ref[0], down_ref[0, cols, :], 1, 1).astype(bf16)
        for k in range(count):
            part = dot(pick_ref[0, k], result_ref[k * capacity : (k + 1) * capacity], 0, 0)

            @pl.when(step_number == 0)
            def _():
                sums_ref[k, :, cols] = part

            @pl.when(step_number > 0)
            def _():
                sums_ref[k, :, cols] += part

    @pl.when(step_number == steps - 1)
    def _():
        for k in range(count):
            mix = sums_ref[k]
            if earlier_refs:
                mix = mix + earlier_refs[0][place_ref[k]].astype(f32)
            mix_ref[place_ref[k]] = mix.astype(bf16)


def experts_forward(first, kept, places, pick, gates, in_weight, down_weight, near):
    experts, count, capacity, tokens = pick.shape
    here, width, hidden = in_weight.shape[0], in_weight.shape[1], down_weight.shape[2]
    rows = count * capacity
    each = lambda shape: pl.BlockSpec((1,) + shape, lambda e: (first + e,) + (0,) * len(shape))
    near_each = lambda shape: pl.BlockSpec((1,) + shape, lambda e: (e,) + (0,) * len(shape))
    whole = pl.BlockSpec((tokens, width), lambda e: (0, 0), pipeline_mode=pl.Buffered(1))
    sums = pl.BlockSpec((count, tokens, width), lambda e: (0, 0, 0), pipeline_mode=pl.Buffered(1))
    return pl.pallas_call(
        functools.partial(forward_kernel, count, len(kept)),
        grid=(here,),
        in_specs=[
            pl.BlockSpec(memory_space=pltpu.SMEM),
            each((count, capacity, tokens)), each((rows, 1)),
            near_each((width, 2 * hidden)), near_each((width, hidden)),
        ] + [whole] * count + [pl.BlockSpec(memory_space=pl.ANY)] * len(kept[:4]) + [sums] * len(kept[4:]),
        out_specs=[each((rows, width))] + [each((rows, hidden))] * 3 + [sums],
        out_shape=[jax.ShapeDtypeStruct((experts, rows, width), bf16)]
        + [jax.ShapeDtypeStruct((experts, rows, hidden), bf16)] * 3
        + [jax.ShapeDtypeStruct((count, tokens, width), bf16)],
        scratch_shapes=[
            pltpu.VMEM((rows, chunk_of(width, 1024)), bf16),
            pltpu.VMEM((count, tokens, width), f32),
        ],
        input_output_aliases={5 + count + i: i for i in range(len(kept[:4]))},
        compiler_params=KERNEL_PARAMS,
        cost_estimate=SMALL_COST,
        name="experts_forward",
    )(places, pick, gates, in_weight, down_weight, *near, *kept)


def down_grad_kernel(count, pick_ref, gated_ref, *refs):
    near_refs = refs[:count]
    rows_ref, grad_ref = refs[count:]
    capacity, width = pick_ref.shape[2], rows_ref.shape[2]
    for k in range(count):
        rows_ref[0, k * capacity : (k + 1) * capacity] = dot(
            pick_ref[0, k], near_refs[k][...], 1, 0
        ).astype(bf16)
    step = chunk_of(width, 2048)

    @pl.loop(0, width // step)
    def _(j):
        cols = pl.ds(pl.multiple_of(j * step, step), step)
        grad_ref[0, cols, :] = dot(rows_ref[0, :, cols], gated_ref[0], 0, 0).astype(bf16)


def experts_down_grad(pick, gated, near):
    experts, count, capacity, tokens = pick.shape
    width, hidden = near[0].shape[1], gated.shape[2]
    rows = count * capacity
    each = lambda shape: pl.BlockSpec((1,) + shape, lambda e: (e,) + (0,) * len(shape))
    whole = pl.BlockSpec((tokens, width), lambda e: (0, 0), pipeline_mode=pl.Buffered(1))
    return pl.pallas_call(
        functools.partial(down_grad_kernel, count),
        grid=(experts,),
        in_specs=[each((count, capacity, tokens)), each((rows, hidden))] + [whole] * count,
        out_specs=[each((rows, width)), each((width, hidden))],
        out_shape=[
            jax.ShapeDtypeStruct((experts, rows, width), bf16),
            jax.ShapeDtypeStruct((experts, width, hidden), bf16),
        ],
        compiler_params=KERNEL_PARAMS,
        cost_estimate=DOWN_GRAD_COST,
        name="experts_down_grad",
    )(pick, gated, *near)


def backward_kernel(
    first, count, kept, pick_ref, gate_rows_ref, cot_ref, gate_ref, up_ref, in_ref, down_ref, *refs
):
    earlier_refs, refs = refs[1:kept], refs[kept:]
    both_ref = refs[0]
    copy_refs = refs[1 : 1 + count]
    result_ref, inner_ref, sums_ref, inner_sums_ref = refs[1 + count :]
    step_number, steps = pl.program_id(0), pl.num_programs(0)
    capacity, width = pick_ref.shape[2], cot_ref.shape[2]
    hidden = gate_ref.shape[2]
    lanes = inner_sums_ref.shape[2]
    step = chunk_of(hidden, 512)
    inner_ref[...] = jnp.zeros_like(inner_ref)

    @pl.when(step_number == 0)
    def _():
        inner_sums_ref[...] = jnp.zeros_like(inner_sums_ref)

    @pl.loop(0, hidden // step)
    def _(j):
        low = pl.ds(pl.multiple_of(j * step, step), step)
        high = pl.ds(pl.multiple_of(hidden + j * step, step), step)
        result_grad = dot(cot_ref[0], down_ref[0, :, low], 1, 0)
        gate, up = gate_ref[0, :, low].astype(f32), up_ref[0, :, low].astype(f32)
        sigmoid = jax.nn.sigmoid(gate)
        silu = gate * sigmoid
        inner_ref[...] += jnp.sum(result_grad * silu * up, axis=1, keepdims=True)
        act_grad = result_grad * gate_rows_ref[0]
        both_ref[0, :, low] = (act_grad * up * (sigmoid + silu * (1.0 - sigmoid))).astype(bf16)
        both_ref[0, :, high] = (act_grad * silu).astype(bf16)

    inner_high = inner_ref[...].astype(bf16).astype(f32)
    lane = lax.broadcasted_iota(jnp.int32, (count * capacity, lanes), 1)
    place = 2 * (first + step_number)
    inner_wide = jnp.where(lane == place, inner_high, 0.0)
    inner_wide = jnp.where(lane == place + 1, inner_ref[...] - inner_high, inner_wide)
    inner_wide = inner_wide.astype(bf16)
    for k in range(count):
        inner_sums_ref[k] += dot(pick_ref[0, k], inner_wide[k * capacity : (k + 1) * capacity], 0, 0)
    wide = chunk_of(width, 1024)

    @pl.loop(0, width // wide)
    def _(j):
        cols = pl.ds(pl.multiple_of(j * wide, wide), wide)
        result_ref[...] = dot(both_ref[0], in_ref[0, cols, :], 1, 1).astype(bf16)
        for k in range(count):
            part = dot(pick_ref[0, k], result_ref[k * capacity : (k + 1) * capacity], 0, 0)

            @pl.when(step_number == 0)
            def _():
                sums_ref[k, :, cols] = part

            @pl.when(step_number > 0)
            def _():
                sums_ref[k, :, cols] += part

    @pl.when(step_number == steps - 1)
    def _():
        for k in range(count):
            copies, inner = sums_ref[k], inner_sums_ref[k]
            if earlier_refs:
                copies = copies + earlier_refs[k][:, :width].astype(f32)
                inner = inner + earlier_refs[k][:, width:].astype(f32)
            copy_refs[k][:, :width] = copies.astype(bf16)
            copy_refs[k][:, width:] = inner.astype(bf16)


def experts_backward(first, kept, pick, gate_rows, cot_rows, gate, up, in_weight, down_weight):
    experts, count, capacity, tokens = pick.shape
    here, width, hidden = in_weight.shape[0], in_weight.shape[1], down_weight.shape[2]
    rows = count * capacity
    lanes = 128 * -(-2 * experts // 128)
    each = lambda shape: pl.BlockSpec((1,) + shape, lambda e: (first + e,) + (0,) * len(shape))
    near_each = lambda shape: pl.BlockSpec((1,) + shape, lambda e: (e,) + (0,) * len(shape))
    whole = pl.BlockSpec((tokens, width + lanes), lambda e: (0, 0), pipeline_mode=pl.Buffered(1))
    return pl.pallas_call(
        functools.partial(backward_kernel, first, count, len(kept)),
        grid=(here,),
        in_specs=[
            each((count, capacity, tokens)), each((rows, 1)), each((rows, width)),
            each((rows, hidden)), each((rows, hidden)),
            near_each((width, 2 * hidden)), near_each((width, hidden)),
        ] + [pl.BlockSpec(memory_space=pl.ANY)] * len(kept[:1]) + [whole] * len(kept[1:]),
        out_specs=[each((rows, 2 * hidden))] + [whole] * count,
        out_shape=[jax.ShapeDtypeStruct((experts, rows, 2 * hidden), bf16)]
        + [jax.ShapeDtypeStruct((tokens, width + lanes), bf16)] * count,
        scratch_shapes=[
            pltpu.VMEM((rows, chunk_of(width, 1024)), bf16),
            pltpu.VMEM((rows, 1), f32),
            pltpu.VMEM((count, tokens, width), f32),
            pltpu.VMEM((count, tokens, lanes), f32),
        ],
        input_output_aliases={7 + i: i for i in range(len(kept[:1]))},
        compiler_params=KERNEL_PARAMS,
        cost_estimate=SMALL_COST,
        name="experts_backward",
    )(pick, gate_rows, cot_rows, gate, up, in_weight, down_weight, *kept)


def in_grad_kernel(rows_ref, both_ref, earlier_ref, grad_ref):
    width = rows_ref.shape[2]
    step = chunk_of(width, 512)

    @pl.loop(0, width // step)
    def _(j):
        cols = pl.ds(pl.multiple_of(j * step, step), step)
        grad_ref[0, cols, :] = dot(rows_ref[0, :, cols], both_ref[0], 0, 0).astype(bf16)


def experts_in_grad(rows, both, earlier):
    experts, _, width = rows.shape
    each = lambda shape: pl.BlockSpec((1,) + shape, lambda e: (e,) + (0,) * len(shape))
    return pl.pallas_call(
        in_grad_kernel,
        grid=(experts,),
        in_specs=[each(rows.shape[1:]), each(both.shape[1:]), pl.BlockSpec(memory_space=pl.ANY)],
        out_specs=each((width, both.shape[2])),
        out_shape=jax.ShapeDtypeStruct((experts, width, both.shape[2]), bf16),
        compiler_params=KERNEL_PARAMS,
        cost_estimate=SMALL_COST,
        name="experts_in_grad",
    )(rows, both, earlier)


def spread_kernel(split, outs, own_ref, left_ref, right_ref, *refs):
    groups, parts, cores = split
    extra_refs, out_refs = refs[:-outs], refs[-outs:]
    width = right_ref.shape[1]
    rows = out_refs[0].shape[-2] // groups
    each = parts * cores * rows

    def store(core, place, columns, values):
        if outs == 1:
            out_refs[0][(core,) + place + (columns,)] = values
            return
        for index, ref in enumerate(out_refs):

            @pl.when(own_ref[0] == (core if index == 0 else 1 - core))
            def _():
                ref[place + (columns,)] = values

    for group in range(groups):
        here = slice(group * each, (group + 1) * each)
        terms = dot(left_ref[:, here], right_ref[...], 0, 0)
        low_terms = terms.astype(bf16)
        if extra_refs:
            beside_ref, weight_ref, gain_ref = extra_refs
            sums = jnp.sum(terms * weight_ref[here, :width].astype(f32), axis=1, keepdims=True)
            beside = beside_ref[here, :]
            lane = lax.broadcasted_iota(jnp.int32, beside.shape, 1)
            beside = jnp.where(lane == 0, sums / gain_ref[here, :], beside).astype(bf16)
        for part in range(parts):
            for core in range(cores):
                start = (part * cores + core) * rows
                place = (part, slice(group * rows, (group + 1) * rows))
                store(core, place, slice(0, width), low_terms[start : start + rows])
                if extra_refs:
                    columns = slice(width, width + beside.shape[1])
                    store(core, place, columns, beside[start : start + rows])


def spread_product(left, right, beside, split, own_core):
    groups, parts, cores = split
    rows = left.shape[1] // (groups * parts * cores)
    width = right.shape[1] + (beside[0].shape[1] if beside else 0)
    shape = (parts, groups * rows, width)
    shapes = [shape] * 2 if cores == 2 else [(cores,) + shape]
    arrays = [left, right] + beside
    return pl.pallas_call(
        functools.partial(spread_kernel, split, len(shapes)),
        in_specs=[pl.BlockSpec(memory_space=pltpu.SMEM)]
        + [pl.BlockSpec(memory_space=pltpu.VMEM)] * len(arrays),
        out_shape=[jax.ShapeDtypeStruct(shape, bf16) for shape in shapes],
        compiler_params=KERNEL_PARAMS,
        cost_estimate=SMALL_COST,
        name="spread_product",
    )(jnp.reshape(own_core.astype(jnp.int32), (1,)), *arrays)


def on_device(
    tokens,
    cotangent,
    expert_ids,
    segment_ids,
    norm_gains,
    w_qkv,
    w_out,
    router,
    expert_in,
    expert_out,
):
    own_low = tokens[0]
    inputs = own_low.astype(f32)
    tok_count, model_width = inputs.shape
    segment = segment_ids[0]
    length = segment.shape[0]
    seq_count = lax.axis_size("seq")
    exp_count = lax.axis_size("exp")
    core_count = lax.axis_size("fsdp")
    own_seq = lax.axis_index("seq")
    own_exp = lax.axis_index("exp")
    rows_dev = w_qkv.shape[0]
    heads_dev = HEADS // seq_count
    head_cols = heads_dev * HEAD_DIM
    experts_total = router.shape[1]
    exp_dev = expert_in.shape[1]

    small = jnp.concatenate([norm_gains, router], axis=1)
    small_cols = small.shape[1]
    ids_room = TOP * tok_count // (seq_count * rows_dev)
    small = jnp.pad(small, ((0, 0), (0, ids_room + -(small_cols + ids_room) % 128)))
    heads_rows = w_qkv.reshape(rows_dev, 3, seq_count, head_cols).transpose(2, 0, 1, 3)
    heads_rows = heads_rows.reshape(seq_count, rows_dev, 3 * head_cols)
    small = jnp.broadcast_to(small[None], (seq_count,) + small.shape)
    heads_seq = exchange(jnp.concatenate([heads_rows, small], axis=2), "seq")
    ids_low = expert_ids[0].astype(bf16).reshape(seq_count, rows_dev, -1)
    first_id = 3 * head_cols + small_cols
    ids_cols = ids_low.shape[2]
    after_ids = heads_seq.shape[2] - first_id - ids_cols
    heads_rows = heads_seq + jnp.pad(ids_low, ((0, 0), (0, 0), (first_id, after_ids)))
    heads_near = gather_near(heads_rows.reshape(seq_count * rows_dev, -1), "exp")
    ids_group = jnp.stack(
        [near[:, first_id : first_id + ids_cols].reshape(tok_count, TOP) for near in heads_near]
    )
    heads_all = order_cores(heads_near, seq_count, "exp", "fsdp")
    heads_weight = heads_all[:, : 3 * head_cols]
    small = heads_all[:, 3 * head_cols : first_id].T
    gains = small[:4].astype(f32)
    router_rows = small[4:]
    out_rows = after(w_out, heads_seq)[None]
    out_rows = exchange(jnp.broadcast_to(out_rows, (seq_count,) + w_out.shape), "seq")
    out_rows = out_rows.reshape(seq_count * rows_dev, model_width)
    all_tokens = after(own_low, out_rows)[None]
    all_tokens = jnp.broadcast_to(all_tokens, (seq_count, tok_count, model_width))
    all_tokens = exchange(all_tokens, "seq").reshape(length, model_width)

    out_near = gather_near(after(out_rows, heads_near[-1]), "exp")

    parts = 2 if exp_dev % 2 == 0 else 1
    part_experts = exp_dev // parts
    in_blocks = jnp.transpose(after(expert_in, out_rows), (1, 0, 2))
    down_blocks = jnp.transpose(after(expert_out, out_rows), (1, 0, 2))
    in_weights, down_weights = [], []
    for part in range(parts):
        chosen_experts = slice(part * part_experts, (part + 1) * part_experts)
        for blocks, weights in ((in_blocks, in_weights), (down_blocks, down_weights)):
            weights.append(
                lax.all_gather(blocks[chosen_experts], ("seq", "fsdp"), axis=1, tiled=True)
            )

    all_inputs = all_tokens.astype(f32)
    first_inverse = rms_inverse(all_inputs)
    attn_low = (all_inputs * first_inverse * gains[0]).astype(bf16)
    projected = jnp.dot(attn_low, heads_weight, preferred_element_type=f32)
    own_gains = lax.dynamic_slice_in_dim(gains, own_seq * head_cols, head_cols, 1)
    query_pre, key_pre = projected[:, :head_cols], projected[:, head_cols : 2 * head_cols]
    squares = jnp.stack([jnp.sum(query_pre * query_pre, axis=-1), jnp.sum(key_pre * key_pre, axis=-1)])
    squares = sum_all(squares, "seq")
    scales = lax.rsqrt(squares / model_width + epsilon).T
    turns = rotary_tables(jnp.arange(length, dtype=jnp.int32), HEAD_DIM)
    row_segment, col_segment = segment[:, None], segment[None, :]
    ready = scales
    for near in out_near[1:]:
        ready = after(ready, near)
    attended, queries, keys, values = attend(
        projected, ready, own_gains[1:3], turns, row_segment, col_segment, heads_dev
    )
    out_weight = order_cores(out_near, seq_count, "exp", "fsdp")
    merged = lax.all_to_all(attended, "seq", split_axis=0, concat_axis=1, tiled=True)
    branch = jnp.einsum("tc,dc->td", merged, out_weight, preferred_element_type=f32)
    residual = inputs + branch
    mlp_inverse = rms_inverse(residual)
    mlp_low = (residual * mlp_inverse * gains[3]).astype(bf16)

    capacity = tok_count * TOP // experts_total * 9 // 8
    near_experts = own_exp * exp_dev + jnp.arange(exp_dev, dtype=jnp.int32)
    chosen = jnp.any(
        ids_group[:, :, :, None] == near_experts.astype(bf16)[None, None, None, :], axis=2
    )
    earlier = (
        jnp.arange(tok_count)[:, None] > jnp.arange(tok_count)[None, :]
    ).astype(bf16)
    rank = jnp.einsum("tu,sue->est", earlier, chosen.astype(bf16), preferred_element_type=f32)
    rank = jnp.where(jnp.transpose(chosen, (2, 0, 1)), rank, -1.0)
    pick = rank[:, :, None, :] == jnp.arange(capacity, dtype=f32)[None, None, :, None]
    pick_low = pick.astype(bf16)

    mlp_near = gather_near(mlp_low, "exp")
    cot_near = cotangent[0]
    for near in mlp_near[1:]:
        cot_near = after(cot_near, near)
    cot_near = gather_near(cot_near, "exp")
    logits = jnp.stack(
        [jnp.einsum("td,ed->te", near, router_rows, preferred_element_type=f32) for near in mlp_near]
    )
    group_probs = jax.nn.softmax(logits, axis=-1)
    router_probs = group_probs[0]
    near_probs = lax.dynamic_slice_in_dim(group_probs, own_exp * exp_dev, exp_dev, 2)
    near_probs = jnp.transpose(near_probs, (2, 0, 1))
    gate_rows = jnp.sum(jnp.where(pick, near_probs[:, :, None, :], 0.0), axis=-1)
    gate_rows = gate_rows.reshape(exp_dev, exp_count * capacity, 1)
    places = jnp.stack([ring_place(own_exp - k, exp_count) for k in range(exp_count)])
    kept = []
    for part in range(parts):
        kept = experts_forward(
            part * part_experts, kept, places.astype(jnp.int32), pick_low, gate_rows,
            in_weights[part], down_weights[part], mlp_near,
        )
    expert_rows, gate, up, gated, mix = kept
    output = (residual + jnp.sum(exchange(mix, "exp").astype(f32), axis=0)).astype(bf16)

    cot_rows, down_grad = experts_down_grad(pick_low, gated, cot_near)
    grad_expert_out = lax.psum_scatter(
        down_grad, ("seq", "fsdp"), scatter_dimension=1, tiled=True
    )
    kept = []
    for part in range(parts):
        kept = experts_backward(
            part * part_experts, kept, pick_low, gate_rows, cot_rows, gate, up,
            in_weights[part], down_weights[part],
        )
    copy_near = send_near(kept[1:], "exp")
    before = jnp.stack([block[:16, :128] for block in kept[1:]])
    in_grad = experts_in_grad(expert_rows, kept[0], before)
    grad_expert_in = lax.psum_scatter(in_grad, ("seq", "fsdp"), scatter_dimension=1, tiled=True)
    copy_near[0] = after(after(copy_near[0], in_grad), output)
    mlp_grad_experts = add_up([near[:, :model_width] for near in copy_near])
    prob_pairs = [
        near[:, model_width : model_width + 2 * exp_dev].astype(f32).reshape(tok_count, exp_dev, 2)
        for near in copy_near
    ]
    prob_grad = order([jnp.sum(pair, axis=2) for pair in prob_pairs], "exp", 1, 1)
    prob_grad = prob_grad.reshape(tok_count, experts_total)
    grad_expert_in = interleave([grad_expert_in])
    grad_expert_out = interleave([grad_expert_out])

    logit_grad = router_probs * (
        prob_grad - jnp.sum(router_probs * prob_grad, axis=-1, keepdims=True)
    )
    router_grad = jnp.dot(logit_grad.T, mlp_low.astype(f32), precision=highest)
    logit_high = logit_grad.astype(bf16)
    logit_low = (logit_grad - logit_high.astype(f32)).astype(bf16)
    mlp_grad = mlp_grad_experts + jnp.dot(
        jnp.concatenate([logit_high, logit_low], axis=1),
        jnp.concatenate([router_rows, router_rows], axis=0),
        preferred_element_type=f32,
    )
    residual_norm_grad, mlp_gain_grad = rms_back(mlp_grad, residual, mlp_inverse, gains[3])
    residual_grad = cotangent[0].astype(f32) + residual_norm_grad
    branch_grad = residual_grad.astype(bf16)

    merged_grad = jnp.einsum("td,dc->tc", branch_grad, out_weight, preferred_element_type=f32)
    heads_grad = lax.all_to_all(
        merged_grad.astype(bf16), "seq", split_axis=1, concat_axis=0, tiled=True
    )
    split_sizes = (seq_count, exp_count, core_count)
    out_terms = spread_product(
        branch_grad, merged, [], split_sizes, lax.axis_index("fsdp")
    )
    out_core = scatter_core(out_terms, "fsdp")
    out_sent = send_near(split(out_core, "exp"), "exp")
    out_terms = add_up(out_sent).astype(bf16)
    query_grad, key_grad, value_grad, inner = attend_back(
        queries, keys, values, heads_grad, projected, own_gains[1:3], turns, row_segment, col_segment,
        out_core[0, :16, :128], heads_dev,
    )
    means = sum_all(inner.T, "seq").T / model_width
    qkv_grad, head_gain_grads = norm_back(
        query_grad, key_grad, value_grad, projected, scales, means, own_gains[1:3]
    )
    query_gain_grad, key_gain_grad = head_gain_grads[0], head_gain_grads[1]

    zero_row = jnp.zeros((model_width,), f32)
    small_terms = jnp.concatenate(
        [
            jnp.stack(
                [
                    zero_row,
                    lax.dynamic_update_slice_in_dim(zero_row, query_gain_grad, own_seq * head_cols, 0),
                    lax.dynamic_update_slice_in_dim(zero_row, key_gain_grad, own_seq * head_cols, 0),
                    mlp_gain_grad,
                ]
            ),
            router_grad,
        ],
        axis=0,
    ).T
    small_terms = jnp.pad(small_terms, ((0, 0), (0, -small_cols % 128)))
    beside = [small_terms, heads_all, gains[0][:, None]]
    heads_terms = spread_product(
        attn_low, qkv_grad, beside, split_sizes, lax.axis_index("fsdp")
    )
    heads_terms = scatter_core(heads_terms, "fsdp", out_sent[1:])
    attn_in_part = jnp.einsum(
        "tc,dc->td", after(qkv_grad, heads_terms), heads_weight, preferred_element_type=f32
    )
    attn_in_grad = exchange(
        attn_in_part.astype(bf16).reshape(seq_count, tok_count, model_width), "seq"
    )
    attn_in_grad = jnp.sum(attn_in_grad.astype(f32), axis=0)
    heads_terms = scatter(heads_terms, "exp").astype(bf16)
    terms_cols = heads_terms.shape[1]
    last_terms = jnp.concatenate([heads_terms, out_terms], axis=1)
    last_near = send_near(split(last_terms.reshape(seq_count, rows_dev, -1), "seq"), "seq")
    grad_w_out = add_up([near[:, terms_cols:] for near in last_near])
    small_grad = add_up(
        [near[:, 3 * head_cols : 3 * head_cols + small_cols] for near in last_near]
    )
    heads_terms = order([near[:, : 3 * head_cols] for near in last_near], "seq", 0, 1)
    heads_terms = after(heads_terms, attn_in_grad)
    grad_w_qkv = jnp.concatenate(
        [
            heads_terms[source, :, part * head_cols : (part + 1) * head_cols]
            for part in range(3)
            for source in range(seq_count)
        ],
        axis=1,
    ).astype(f32)

    own_inverse = lax.dynamic_slice_in_dim(first_inverse, own_seq * tok_count, tok_count, 0)
    input_norm_grad, _ = rms_back(attn_in_grad, inputs, own_inverse, gains[0])
    input_grad = residual_grad + input_norm_grad

    return (
        output[None],
        input_grad[None],
        small_grad[:, :4],
        grad_w_qkv,
        grad_w_out,
        small_grad[:, 4:],
        grad_expert_in,
        grad_expert_out,
    )


def solution(mesh):
    in_specs = (
        P(("exp", "fsdp"), "seq", None),
        P(("exp", "fsdp"), "seq", None),
        P(("exp", "fsdp"), "seq", None),
        P(("exp", "fsdp"), None),
        P(("seq", "exp", "fsdp"), None),
        P(("seq", "exp", "fsdp"), None),
        P(("seq", "exp", "fsdp"), None),
        P(("seq", "exp", "fsdp"), None),
        P(("seq", "fsdp"), "exp", None),
        P(("seq", "fsdp"), "exp", None),
    )
    out_specs = (
        P(("exp", "fsdp"), "seq", None),
        P(("exp", "fsdp"), "seq", None),
        P(("seq", "exp", "fsdp"), None),
        P(("seq", "exp", "fsdp"), None),
        P(("seq", "exp", "fsdp"), None),
        P(("seq", "exp", "fsdp"), None),
        P(("seq", "fsdp"), "exp", None),
        P(("seq", "fsdp"), "exp", None),
    )
    return jax.shard_map(
        on_device, mesh=mesh, in_specs=in_specs, out_specs=out_specs, check_vma=False
    )
```

```python
import functools

import jax
import jax.numpy as jnp
from jax import lax
from jax.experimental import pallas as pl
from jax.experimental.pallas import tpu as pltpu
from jax.sharding import PartitionSpec as P

HEADS = 16
HEAD_DIM = 128
FF = 1024
TOP = 8
EARLY = (1,)
ATT_BLOCK = 256


epsilon = 1e-05
rotary_base = 10000.0
highest = lax.Precision.HIGHEST
f32 = jnp.float32
bf16 = jnp.bfloat16
VMEM_BYTES = 63 * 1024 * 1024
KERNEL_PARAMS = pltpu.CompilerParams(vmem_limit_bytes=VMEM_BYTES)
SMALL_COST = pl.CostEstimate(flops=1, bytes_accessed=1, transcendentals=0)
DOWN_GRAD_COST = pl.CostEstimate(flops=10**11, bytes_accessed=1, transcendentals=0)
ATTEND_BACK_COST = pl.CostEstimate(flops=250 * 10**9, bytes_accessed=1, transcendentals=0)


def after(value, other):
    first = lax.slice(other, (0,) * other.ndim, (1,) * other.ndim).reshape(())
    return value + (0.0 * first.astype(f32)).astype(value.dtype)


def swap_pairs(count, mask):
    return [(i, i ^ mask) for i in range(count)]


def shift_pairs(count, step):
    return [(i, (i + step) % count) for i in range(count)]


def ring_place(index, count):
    return index & (count - 1) if count & (count - 1) == 0 else lax.rem(index + count, count)


def exchange(stacked, axis, split_axis=0):
    return lax.all_to_all(stacked, axis, split_axis=split_axis, concat_axis=split_axis, tiled=True)


def gather_near(block, axis):
    count = lax.axis_size(axis)
    return [block] + [
        lax.ppermute(block, axis, shift_pairs(count, k)) for k in range(1, count)
    ]


def send_near(blocks, axis):
    count = lax.axis_size(axis)
    return [blocks[0]] + [
        lax.ppermute(blocks[k], axis, shift_pairs(count, -k)) for k in range(1, count)
    ]


def add_up(blocks):
    return sum(block.astype(f32) for block in blocks)


def order(blocks, axis, out_axis=0, sign=-1):
    count = lax.axis_size(axis)
    own = lax.axis_index(axis)
    shape = blocks[0].shape[:out_axis] + (count,) + blocks[0].shape[out_axis:]
    out = jnp.zeros(shape, blocks[0].dtype)
    for k, block in enumerate(blocks):
        place = ring_place(own + sign * k, count)
        out = lax.dynamic_update_index_in_dim(out, block, place, out_axis)
    return out


def split(stacked, axis, in_axis=0, sign=-1):
    count = lax.axis_size(axis)
    own = lax.axis_index(axis)
    return [
        lax.dynamic_index_in_dim(
            stacked, ring_place(own + sign * k, count), in_axis, keepdims=False
        )
        for k in range(count)
    ]


def gather(block, axis, out_axis=0):
    return order(gather_near(block, axis), axis, out_axis)


def scatter(stacked, axis, split_axis=0):
    return add_up(send_near(split(stacked, axis, split_axis), axis))


def sum_all(value, axis):
    count = lax.axis_size(axis)
    return jnp.sum(exchange(jnp.broadcast_to(value[None], (count,) + value.shape), axis), axis=0)


def assemble_kernel(groups, parts, place_ref, *refs):
    sources, out_ref, sems = refs[: len(refs) - 2], refs[-2], refs[-1]
    rows = sources[0].shape[0] // groups
    copies = []
    for k, source in enumerate(sources):
        for group in range(groups):
            target = pl.multiple_of((group * parts + place_ref[k]) * rows, rows)
            copies.append(
                pltpu.make_async_copy(
                    source.at[pl.ds(group * rows, rows)],
                    out_ref.at[pl.ds(target, rows)],
                    sems.at[k, group],
                )
            )
    for copy in copies:
        copy.start()
    for copy in copies:
        copy.wait()


def assemble(blocks, places, groups):
    parts = len(blocks)
    return pl.pallas_call(
        functools.partial(assemble_kernel, groups, parts),
        in_specs=[pl.BlockSpec(memory_space=pltpu.SMEM)]
        + [pl.BlockSpec(memory_space=pltpu.VMEM)] * parts,
        out_specs=pl.BlockSpec(memory_space=pl.ANY),
        out_shape=jax.ShapeDtypeStruct(
            (parts * blocks[0].shape[0], blocks[0].shape[1]), blocks[0].dtype
        ),
        scratch_shapes=[pltpu.SemaphoreType.DMA((parts, groups))],
        compiler_params=KERNEL_PARAMS,
        cost_estimate=SMALL_COST,
        name="assemble",
    )(places, *blocks)


def order_cores(blocks, groups, axis, core_axis):
    count, cores = lax.axis_size(axis), lax.axis_size(core_axis)
    own, own_core = lax.axis_index(axis), lax.axis_index(core_axis)
    if cores == 2:
        blocks = blocks + [lax.ppermute(block, core_axis, swap_pairs(2, 1)) for block in blocks]
        core_places = [own_core, 1 - own_core]
    else:
        every = lax.all_gather(jnp.stack(blocks), core_axis, axis=0)
        blocks = [every[core, k] for core in range(cores) for k in range(count)]
        core_places = list(range(cores))
    places = [
        ring_place(own - k, count) * cores + core for core in core_places for k in range(count)
    ]
    places = jnp.stack([jnp.asarray(place, jnp.int32) for place in places])
    return assemble(blocks, places, groups)


def scatter_core(terms, axis, earlier=()):
    if len(terms) == 1:
        return lax.psum_scatter(terms[0], axis, scatter_dimension=0, tiled=False)
    kept, given = terms
    for array in earlier:
        given = after(given, array)
    received = lax.ppermute(given, axis, swap_pairs(2, 1))
    return (kept.astype(f32) + received.astype(f32)).astype(kept.dtype)


def rms_inverse(values):
    return lax.rsqrt(jnp.mean(values * values, axis=-1, keepdims=True) + epsilon)


def rms_back(gradient, values, inverse, gain_vector):
    scaled = gradient * gain_vector
    gain_grad = jnp.sum(gradient * values * inverse, axis=0)
    value_grad = inverse * scaled - values * inverse**3 * jnp.mean(
        scaled * values, axis=-1, keepdims=True
    )
    return (value_grad, gain_grad)


def rotary_tables(position, head_dim):
    half_dim = head_dim // 2
    exponent = jnp.arange(half_dim, dtype=f32) * (2.0 / head_dim)
    angles = position.astype(f32)[:, None] * (rotary_base ** (-exponent))[None, :]
    cosine, sine_part = jnp.cos(angles), jnp.sin(angles)
    return jnp.stack(
        [
            jnp.concatenate([cosine, cosine], axis=1),
            jnp.concatenate([-sine_part, sine_part], axis=1),
        ]
    )


def dot(one, other, one_axis, other_axis):
    return lax.dot_general(
        one, other, (((one_axis,), (other_axis,)), ((), ())), preferred_element_type=f32
    )


def turn(values, cosines, sines):
    return values * cosines + pltpu.roll(values, HEAD_DIM // 2, 1) * sines


def block_probs(query_rows, keys, query_segment, key_segment, scale):
    scores = dot(query_rows, keys, 1, 1) * scale
    scores = jnp.where(query_segment == key_segment, scores, -jnp.inf)
    terms = jnp.exp(scores - jnp.max(scores, axis=1, keepdims=True))
    return terms / jnp.sum(terms, axis=1, keepdims=True)


def attend_kernel(
    query_ref, key_ref, value_ref, scale_ref, gain_ref, turn_ref, row_seg_ref, col_seg_ref,
    out_ref, query_low_ref, key_low_ref, value_low_ref,
):
    length = query_ref.shape[0]
    cosines, sines = turn_ref[0], turn_ref[1]
    query = query_ref[...] * scale_ref[:, 0:1] * gain_ref[0:1, :]
    key = key_ref[...] * scale_ref[:, 1:2] * gain_ref[1:2, :]
    query_low_ref[...] = turn(query, cosines, sines).astype(bf16)
    key_low_ref[...] = turn(key, cosines, sines).astype(bf16)
    value_low_ref[...] = value_ref[...].astype(bf16)
    for start in range(0, length, ATT_BLOCK):
        stop = start + ATT_BLOCK
        probs = block_probs(
            query_low_ref[start:stop],
            key_low_ref[:stop],
            row_seg_ref[start:stop, 0:1],
            col_seg_ref[0:1, :stop],
            HEAD_DIM ** (-0.5),
        )
        out = dot(probs.astype(bf16), value_low_ref[:stop], 1, 0)
        out_ref[start:stop] = out.astype(bf16)


def attend(projected, scales, gains, turns, row_segment, col_segment, heads):
    length = projected.shape[0]
    column = lambda part: pl.BlockSpec((length, HEAD_DIM), lambda h: (0, part * heads + h))
    whole = lambda shape: pl.BlockSpec(shape, lambda h: (0,) * len(shape))
    out = pl.BlockSpec((length, HEAD_DIM), lambda h: (0, h))
    return pl.pallas_call(
        attend_kernel,
        grid=(heads,),
        in_specs=[
            column(0), column(1), column(2), whole(scales.shape),
            pl.BlockSpec((2, HEAD_DIM), lambda h: (0, h)),
            whole(turns.shape), whole(row_segment.shape), whole(col_segment.shape),
        ],
        out_specs=[out] * 4,
        out_shape=[jax.ShapeDtypeStruct((length, heads * HEAD_DIM), bf16)] * 4,
        compiler_params=KERNEL_PARAMS,
        cost_estimate=SMALL_COST,
        name="attend",
    )(projected, projected, projected, scales, gains, turns, row_segment, col_segment)


def attend_back_kernel(
    query_ref, key_ref, value_ref, grad_ref, query_pre_ref, key_pre_ref, gain_ref, turn_ref,
    row_seg_ref, col_seg_ref, earlier_ref,
    query_out_ref, key_out_ref, value_out_ref, inner_ref, key_sum_ref, value_sum_ref,
):
    length = query_ref.shape[0]
    scale = HEAD_DIM ** (-0.5)
    cosines, sines = turn_ref[0], -turn_ref[1]
    first = pl.program_id(0) == 0
    for start in reversed(range(0, length, ATT_BLOCK)):
        stop = start + ATT_BLOCK
        query_rows, grad_rows, keys = query_ref[start:stop], grad_ref[start:stop], key_ref[:stop]
        probs = block_probs(
            query_rows, keys, row_seg_ref[start:stop, 0:1], col_seg_ref[0:1, :stop], scale
        )
        value_terms = dot(probs.astype(bf16), grad_rows, 0, 0)
        prob_grad = dot(grad_rows, value_ref[:stop], 1, 1)
        inner = jnp.sum(probs * prob_grad, axis=1, keepdims=True)
        score_grad = (probs * (prob_grad - inner)).astype(bf16)
        query_grad = (dot(score_grad, keys, 1, 0) * scale).astype(bf16).astype(f32)
        query_grad = turn(query_grad, cosines[start:stop], sines[start:stop])
        query_out_ref[start:stop] = query_grad
        query_inner = query_grad * gain_ref[0:1, :] * query_pre_ref[start:stop]
        query_inner = jnp.sum(query_inner, axis=1, keepdims=True)
        inner_ref[start:stop, 0:1] = query_inner + jnp.where(first, 0.0, inner_ref[start:stop, 0:1])
        key_terms = dot(score_grad, query_rows, 0, 0)
        if stop == length:
            key_sum_ref[...] = key_terms
            value_sum_ref[...] = value_terms
        else:
            key_sum_ref[:stop] += key_terms
            value_sum_ref[:stop] += value_terms
    key_grad = (key_sum_ref[...] * scale).astype(bf16).astype(f32)
    key_grad = turn(key_grad, cosines, sines)
    key_out_ref[...] = key_grad
    key_inner = jnp.sum(key_grad * gain_ref[1:2, :] * key_pre_ref[...], axis=1, keepdims=True)
    inner_ref[:, 1:2] = key_inner + jnp.where(first, 0.0, inner_ref[:, 1:2])
    value_out_ref[...] = value_sum_ref[...].astype(bf16)


def attend_back(
    queries, keys, values, grads, projected, gains, turns, row_segment, col_segment, earlier, heads
):
    length = queries.shape[0]
    column = pl.BlockSpec((length, HEAD_DIM), lambda h: (0, h))
    whole = lambda shape: pl.BlockSpec(shape, lambda h: (0,) * len(shape))
    shape = (length, heads * HEAD_DIM)
    return pl.pallas_call(
        attend_back_kernel,
        grid=(heads,),
        in_specs=[column] * 4
        + [column, pl.BlockSpec((length, HEAD_DIM), lambda h: (0, heads + h))]
        + [pl.BlockSpec((2, HEAD_DIM), lambda h: (0, h))]
        + [whole(turns.shape), whole(row_segment.shape), whole(col_segment.shape)]
        + [pl.BlockSpec(memory_space=pl.ANY)],
        out_specs=[column] * 3 + [whole((length, 2))],
        out_shape=[
            jax.ShapeDtypeStruct(shape, f32),
            jax.ShapeDtypeStruct(shape, f32),
            jax.ShapeDtypeStruct(shape, bf16),
            jax.ShapeDtypeStruct((length, 2), f32),
        ],
        scratch_shapes=[pltpu.VMEM((length, HEAD_DIM), f32)] * 2,
        compiler_params=KERNEL_PARAMS,
        cost_estimate=ATTEND_BACK_COST,
        name="attend_back",
    )(
        queries, keys, values, grads, projected, projected, gains, turns, row_segment, col_segment, earlier
    )


def interleave_kernel(*refs):
    expert = 0
    for ref in refs[:-1]:
        for k in range(ref.shape[0]):
            refs[-1][:, expert, :] = ref[k].astype(f32)
            expert += 1


def interleave(parts):
    _, rows, width = parts[0].shape
    experts = sum(part.shape[0] for part in parts)
    block = min(rows, 64)
    return pl.pallas_call(
        interleave_kernel,
        grid=(rows // block,),
        in_specs=[
            pl.BlockSpec((part.shape[0], block, width), lambda i: (0, i, 0)) for part in parts
        ],
        out_specs=pl.BlockSpec((block, experts, width), lambda i: (i, 0, 0)),
        out_shape=jax.ShapeDtypeStruct((rows, experts, width), f32),
        compiler_params=KERNEL_PARAMS,
        cost_estimate=SMALL_COST,
        name="interleave",
    )(*parts)


def norm_back_kernel(
    query_grad_ref, key_grad_ref, value_grad_ref, query_pre_ref, key_pre_ref, scale_ref, mean_ref, gain_ref,
    out_ref, gain_grad_ref,
):
    width = query_grad_ref.shape[1]

    @pl.when(pl.program_id(0) == 0)
    def _():
        gain_grad_ref[...] = jnp.zeros_like(gain_grad_ref)

    for part, (grad_ref, pre_ref) in enumerate(
        ((query_grad_ref, query_pre_ref), (key_grad_ref, key_pre_ref))
    ):
        here = slice(part, part + 1)
        grad, scale = grad_ref[...], scale_ref[:, here]
        normal = pre_ref[...] * scale
        gain_grad_ref[here, :] += jnp.sum(grad * normal, axis=0, keepdims=True)
        back = scale * (grad * gain_ref[here, :]) - normal * (scale * scale * mean_ref[:, here])
        out_ref[:, part * width : (part + 1) * width] = back.astype(bf16)
    out_ref[:, 2 * width :] = value_grad_ref[...]


def norm_back(query_grad, key_grad, value_grad, projected, scales, means, gains):
    length, width = query_grad.shape
    block = min(length, 256)
    rows = lambda columns, part: pl.BlockSpec((block, columns), lambda i: (i, part))
    whole = lambda shape: pl.BlockSpec(shape, lambda i: (0,) * len(shape))
    return pl.pallas_call(
        norm_back_kernel,
        grid=(length // block,),
        in_specs=[rows(width, 0)] * 3
        + [rows(width, 0), rows(width, 1), rows(2, 0), rows(2, 0), whole(gains.shape)],
        out_specs=[rows(3 * width, 0), whole(gains.shape)],
        out_shape=[
            jax.ShapeDtypeStruct((length, 3 * width), bf16),
            jax.ShapeDtypeStruct(gains.shape, f32),
        ],
        compiler_params=KERNEL_PARAMS,
        cost_estimate=SMALL_COST,
        name="norm_back",
    )(query_grad, key_grad, value_grad, projected, projected, scales, means, gains)


def chunk_of(width, most):
    return most if width % most == 0 else width


def route_kernel(experts_total, count, first_ref, router_ref, pick_ref, *refs):
    near_refs, (gate_ref, probs_ref) = refs[:count], refs[count:]
    experts, _, capacity, tokens = pick_ref.shape
    lane = lax.broadcasted_iota(jnp.int32, (tokens, router_ref.shape[0]), 1)
    for k in range(count):
        logits = dot(near_refs[k][...], router_ref[...], 1, 1)
        logits = jnp.where(lane < experts_total, logits, -jnp.inf)
        terms = jnp.exp(logits - jnp.max(logits, axis=1, keepdims=True))
        probs = terms / jnp.sum(terms, axis=1, keepdims=True)
        if k == 0:
            probs_ref[...] = probs
        pairs = jnp.zeros((tokens, router_ref.shape[0]), f32)
        for j in range(experts):
            prob = jnp.sum(jnp.where(lane == first_ref[0] + j, probs, 0.0), axis=1, keepdims=True)
            high = prob.astype(bf16).astype(f32)
            pairs = jnp.where(lane == 2 * j, high, pairs)
            pairs = jnp.where(lane == 2 * j + 1, prob - high, pairs)
        pairs = pairs.astype(bf16)
        for j in range(experts):
            gates = dot(pick_ref[j, k], pairs, 1, 0)
            gate_ref[j, k * capacity : (k + 1) * capacity] = (
                gates[:, 2 * j : 2 * j + 1] + gates[:, 2 * j + 1 : 2 * j + 2]
            )


def route(first, router_rows, pick, near):
    experts, count, capacity, tokens = pick.shape
    experts_total = router_rows.shape[0]
    lanes = 128 * -(-max(experts_total, 2 * experts) // 128)
    router_rows = jnp.pad(router_rows, ((0, lanes - experts_total), (0, 0)))
    vmem = pl.BlockSpec(memory_space=pltpu.VMEM)
    gates, probs = pl.pallas_call(
        functools.partial(route_kernel, experts_total, count),
        in_specs=[pl.BlockSpec(memory_space=pltpu.SMEM)] + [vmem] * (2 + count),
        out_shape=[
            jax.ShapeDtypeStruct((experts, count * capacity, 1), f32),
            jax.ShapeDtypeStruct((tokens, lanes), f32),
        ],
        compiler_params=KERNEL_PARAMS,
        cost_estimate=SMALL_COST,
        name="route",
    )(jnp.reshape(first.astype(jnp.int32), (1,)), router_rows, pick, *near)
    return probs[:, :experts_total], gates


def forward_kernel(count, kept, place_ref, pick_ref, turned_ref, gate_ref, in_ref, down_ref, *refs):
    near_refs, refs = refs[:count], refs[count:]
    earlier_refs, refs = refs[4:kept], refs[kept:]
    rows_ref, gate_out_ref, up_out_ref, gated_ref, mix_ref, result_ref = refs
    step_number, steps = pl.program_id(0), pl.num_programs(0)
    capacity, width = pick_ref.shape[2], rows_ref.shape[2]
    hidden = gated_ref.shape[2]
    for k in range(count):
        rows_ref[0, k * capacity : (k + 1) * capacity] = dot(
            pick_ref[0, k], near_refs[k][...], 1, 0
        ).astype(bf16)
    step = chunk_of(hidden, 512)
    for start in range(0, hidden, step):
        low, high = slice(start, start + step), slice(hidden + start, hidden + start + step)
        gate = dot(rows_ref[0], in_ref[0, :, low], 1, 0)
        up = dot(rows_ref[0], in_ref[0, :, high], 1, 0)
        gate_out_ref[0, :, low] = gate.astype(bf16)
        up_out_ref[0, :, low] = up.astype(bf16)
        gated_ref[0, :, low] = (gate * jax.nn.sigmoid(gate) * up * gate_ref[0]).astype(bf16)
    wide = chunk_of(width, 1024)
    for start in range(0, width, wide):
        cols = slice(start, start + wide)
        result_ref[step_number, :, cols] = dot(gated_ref[0], down_ref[0, cols, :], 1, 1).astype(bf16)

    @pl.when(step_number == steps - 1)
    def _():
        for k in range(count):
            rows = slice(k * capacity, (k + 1) * capacity)
            for start in range(0, width, wide):
                cols = slice(start, start + wide)
                mix = dot(turned_ref[0, k], result_ref[0, rows, cols], 1, 0)
                for expert in range(1, result_ref.shape[0]):
                    mix += dot(turned_ref[expert, k], result_ref[expert, rows, cols], 1, 0)
                if earlier_refs:
                    mix += earlier_refs[0][place_ref[k], :, cols].astype(f32)
                mix_ref[place_ref[k], :, cols] = mix.astype(bf16)


def experts_forward(first, kept, places, pick, turned, gates, in_weight, down_weight, near):
    experts, count, capacity, tokens = pick.shape
    here, width, hidden = in_weight.shape[0], in_weight.shape[1], down_weight.shape[2]
    rows = count * capacity
    each = lambda shape: pl.BlockSpec((1,) + shape, lambda e: (first + e,) + (0,) * len(shape))
    near_each = lambda shape: pl.BlockSpec((1,) + shape, lambda e: (e,) + (0,) * len(shape))
    whole = pl.BlockSpec((tokens, width), lambda e: (0, 0), pipeline_mode=pl.Buffered(1))
    sums = pl.BlockSpec((count, tokens, width), lambda e: (0, 0, 0), pipeline_mode=pl.Buffered(1))
    return pl.pallas_call(
        functools.partial(forward_kernel, count, len(kept)),
        grid=(here,),
        in_specs=[
            pl.BlockSpec(memory_space=pltpu.SMEM),
            each((count, capacity, tokens)),
            pl.BlockSpec(
                (here,) + turned.shape[1:], lambda e: (first // here, 0, 0, 0), pipeline_mode=pl.Buffered(1)
            ),
            each((rows, 1)),
            near_each((width, 2 * hidden)), near_each((width, hidden)),
        ] + [whole] * count + [pl.BlockSpec(memory_space=pl.ANY)] * len(kept[:4]) + [sums] * len(kept[4:]),
        out_specs=[each((rows, width))] + [each((rows, hidden))] * 3 + [sums],
        out_shape=[jax.ShapeDtypeStruct((experts, rows, width), bf16)]
        + [jax.ShapeDtypeStruct((experts, rows, hidden), bf16)] * 3
        + [jax.ShapeDtypeStruct((count, tokens, width), bf16)],
        scratch_shapes=[pltpu.VMEM((here, rows, width), bf16)],
        input_output_aliases={6 + count + i: i for i in range(len(kept[:4]))},
        compiler_params=KERNEL_PARAMS,
        cost_estimate=SMALL_COST,
        name="experts_forward",
    )(places, pick, turned, gates, in_weight, down_weight, *near, *kept)


def down_grad_kernel(count, pick_ref, gated_ref, *refs):
    near_refs = refs[:count]
    rows_ref, grad_ref = refs[count:]
    capacity, width = pick_ref.shape[2], rows_ref.shape[2]
    for k in range(count):
        rows_ref[0, k * capacity : (k + 1) * capacity] = dot(
            pick_ref[0, k], near_refs[k][...], 1, 0
        ).astype(bf16)
    step = chunk_of(width, 2048)

    @pl.loop(0, width // step)
    def _(j):
        cols = pl.ds(pl.multiple_of(j * step, step), step)
        grad_ref[0, cols, :] = dot(rows_ref[0, :, cols], gated_ref[0], 0, 0).astype(bf16)


def experts_down_grad(pick, gated, near):
    experts, count, capacity, tokens = pick.shape
    width, hidden = near[0].shape[1], gated.shape[2]
    rows = count * capacity
    each = lambda shape: pl.BlockSpec((1,) + shape, lambda e: (e,) + (0,) * len(shape))
    whole = pl.BlockSpec((tokens, width), lambda e: (0, 0), pipeline_mode=pl.Buffered(1))
    return pl.pallas_call(
        functools.partial(down_grad_kernel, count),
        grid=(experts,),
        in_specs=[each((count, capacity, tokens)), each((rows, hidden))] + [whole] * count,
        out_specs=[each((rows, width)), each((width, hidden))],
        out_shape=[
            jax.ShapeDtypeStruct((experts, rows, width), bf16),
            jax.ShapeDtypeStruct((experts, width, hidden), bf16),
        ],
        compiler_params=KERNEL_PARAMS,
        cost_estimate=DOWN_GRAD_COST,
        name="experts_down_grad",
    )(pick, gated, *near)


def backward_kernel(
    first, count, kept, turned_ref, gate_rows_ref, cot_ref, gate_ref, up_ref, in_ref, down_ref, *refs
):
    earlier_refs, refs = refs[1:kept], refs[kept:]
    both_ref = refs[0]
    copy_refs = refs[1 : 1 + count]
    result_ref, inner_ref = refs[1 + count :]
    step_number, steps = pl.program_id(0), pl.num_programs(0)
    capacity, width = turned_ref.shape[3], cot_ref.shape[2]
    hidden = gate_ref.shape[2]
    lanes = inner_ref.shape[2]
    step = chunk_of(hidden, 512)
    inner = jnp.zeros((count * capacity, 1), f32)
    for start in range(0, hidden, step):
        low, high = slice(start, start + step), slice(hidden + start, hidden + start + step)
        result_grad = dot(cot_ref[0], down_ref[0, :, low], 1, 0)
        gate, up = gate_ref[0, :, low].astype(f32), up_ref[0, :, low].astype(f32)
        sigmoid = jax.nn.sigmoid(gate)
        silu = gate * sigmoid
        inner += jnp.sum(result_grad * silu * up, axis=1, keepdims=True)
        act_grad = result_grad * gate_rows_ref[0]
        both_ref[0, :, low] = (act_grad * up * (sigmoid + silu * (1.0 - sigmoid))).astype(bf16)
        both_ref[0, :, high] = (act_grad * silu).astype(bf16)
    inner_high = inner.astype(bf16).astype(f32)
    lane = lax.broadcasted_iota(jnp.int32, (count * capacity, lanes), 1)
    place = 2 * (first + step_number)
    inner_wide = jnp.where(lane == place, inner_high, 0.0)
    inner_wide = jnp.where(lane == place + 1, inner - inner_high, inner_wide)
    inner_ref[step_number] = inner_wide.astype(bf16)
    wide = chunk_of(width, 1024)
    for start in range(0, width, wide):
        cols = slice(start, start + wide)
        result_ref[step_number, :, cols] = dot(both_ref[0], in_ref[0, cols, :], 1, 1).astype(bf16)

    @pl.when(step_number == steps - 1)
    def _():
        for k in range(count):
            rows = slice(k * capacity, (k + 1) * capacity)
            pieces = [(result_ref, slice(start, start + wide), start) for start in range(0, width, wide)]
            for ref, cols, start in pieces + [(inner_ref, slice(0, lanes), width)]:
                copies = dot(turned_ref[0, k], ref[0, rows, cols], 1, 0)
                for expert in range(1, result_ref.shape[0]):
                    copies += dot(turned_ref[expert, k], ref[expert, rows, cols], 1, 0)
                target = slice(start, start + cols.stop - cols.start)
                if earlier_refs:
                    copies += earlier_refs[k][:, target].astype(f32)
                copy_refs[k][:, target] = copies.astype(bf16)


def experts_backward(first, kept, turned, gate_rows, cot_rows, gate, up, in_weight, down_weight):
    experts, count, tokens, capacity = turned.shape
    here, width, hidden = in_weight.shape[0], in_weight.shape[1], down_weight.shape[2]
    rows = count * capacity
    lanes = 128 * -(-2 * experts // 128)
    each = lambda shape: pl.BlockSpec((1,) + shape, lambda e: (first + e,) + (0,) * len(shape))
    near_each = lambda shape: pl.BlockSpec((1,) + shape, lambda e: (e,) + (0,) * len(shape))
    whole = pl.BlockSpec((tokens, width + lanes), lambda e: (0, 0), pipeline_mode=pl.Buffered(1))
    return pl.pallas_call(
        functools.partial(backward_kernel, first, count, len(kept)),
        grid=(here,),
        in_specs=[
            pl.BlockSpec(
                (here,) + turned.shape[1:], lambda e: (first // here, 0, 0, 0), pipeline_mode=pl.Buffered(1)
            ),
            each((rows, 1)), each((rows, width)),
            each((rows, hidden)), each((rows, hidden)),
            near_each((width, 2 * hidden)), near_each((width, hidden)),
        ] + [pl.BlockSpec(memory_space=pl.ANY)] * len(kept[:1]) + [whole] * len(kept[1:]),
        out_specs=[each((rows, 2 * hidden))] + [whole] * count,
        out_shape=[jax.ShapeDtypeStruct((experts, rows, 2 * hidden), bf16)]
        + [jax.ShapeDtypeStruct((tokens, width + lanes), bf16)] * count,
        scratch_shapes=[
            pltpu.VMEM((here, rows, width), bf16),
            pltpu.VMEM((here, rows, lanes), bf16),
        ],
        input_output_aliases={7 + i: i for i in range(len(kept[:1]))},
        compiler_params=KERNEL_PARAMS,
        cost_estimate=SMALL_COST,
        name="experts_backward",
    )(turned, gate_rows, cot_rows, gate, up, in_weight, down_weight, *kept)


def in_grad_kernel(rows_ref, both_ref, earlier_ref, grad_ref):
    width = rows_ref.shape[2]
    step = chunk_of(width, 512)

    @pl.loop(0, width // step)
    def _(j):
        cols = pl.ds(pl.multiple_of(j * step, step), step)
        grad_ref[0, cols, :] = dot(rows_ref[0, :, cols], both_ref[0], 0, 0).astype(bf16)


def experts_in_grad(rows, both, earlier):
    experts, _, width = rows.shape
    each = lambda shape: pl.BlockSpec((1,) + shape, lambda e: (e,) + (0,) * len(shape))
    return pl.pallas_call(
        in_grad_kernel,
        grid=(experts,),
        in_specs=[each(rows.shape[1:]), each(both.shape[1:]), pl.BlockSpec(memory_space=pl.ANY)],
        out_specs=each((width, both.shape[2])),
        out_shape=jax.ShapeDtypeStruct((experts, width, both.shape[2]), bf16),
        compiler_params=KERNEL_PARAMS,
        cost_estimate=SMALL_COST,
        name="experts_in_grad",
    )(rows, both, earlier)


def spread_kernel(split, outs, own_ref, left_ref, right_ref, *refs):
    groups, parts, cores = split
    extra_refs, out_refs = refs[:-outs], refs[-outs:]
    width = right_ref.shape[1]
    rows = out_refs[0].shape[-2] // groups
    each = parts * cores * rows

    def store(core, place, columns, values):
        if outs == 1:
            out_refs[0][(core,) + place + (columns,)] = values
            return
        for index, ref in enumerate(out_refs):

            @pl.when(own_ref[0] == (core if index == 0 else 1 - core))
            def _():
                ref[place + (columns,)] = values

    for group in range(groups):
        here = slice(group * each, (group + 1) * each)
        terms = dot(left_ref[:, here], right_ref[...], 0, 0)
        low_terms = terms.astype(bf16)
        if extra_refs:
            beside_ref, weight_ref, gain_ref = extra_refs
            sums = jnp.sum(terms * weight_ref[here, :width].astype(f32), axis=1, keepdims=True)
            beside = beside_ref[here, :]
            lane = lax.broadcasted_iota(jnp.int32, beside.shape, 1)
            beside = jnp.where(lane == 0, sums / gain_ref[here, :], beside).astype(bf16)
        for part in range(parts):
            for core in range(cores):
                start = (part * cores + core) * rows
                place = (part, slice(group * rows, (group + 1) * rows))
                store(core, place, slice(0, width), low_terms[start : start + rows])
                if extra_refs:
                    columns = slice(width, width + beside.shape[1])
                    store(core, place, columns, beside[start : start + rows])


def spread_product(left, right, beside, split, own_core):
    groups, parts, cores = split
    rows = left.shape[1] // (groups * parts * cores)
    width = right.shape[1] + (beside[0].shape[1] if beside else 0)
    shape = (parts, groups * rows, width)
    shapes = [shape] * 2 if cores == 2 else [(cores,) + shape]
    arrays = [left, right] + beside
    return pl.pallas_call(
        functools.partial(spread_kernel, split, len(shapes)),
        in_specs=[pl.BlockSpec(memory_space=pltpu.SMEM)]
        + [pl.BlockSpec(memory_space=pltpu.VMEM)] * len(arrays),
        out_shape=[jax.ShapeDtypeStruct(shape, bf16) for shape in shapes],
        compiler_params=KERNEL_PARAMS,
        cost_estimate=SMALL_COST,
        name="spread_product",
    )(jnp.reshape(own_core.astype(jnp.int32), (1,)), *arrays)


def on_device(
    tokens,
    cotangent,
    expert_ids,
    segment_ids,
    norm_gains,
    w_qkv,
    w_out,
    router,
    expert_in,
    expert_out,
):
    own_low = tokens[0]
    inputs = own_low.astype(f32)
    tok_count, model_width = inputs.shape
    segment = segment_ids[0]
    length = segment.shape[0]
    seq_count = lax.axis_size("seq")
    exp_count = lax.axis_size("exp")
    core_count = lax.axis_size("fsdp")
    own_seq = lax.axis_index("seq")
    own_exp = lax.axis_index("exp")
    rows_dev = w_qkv.shape[0]
    heads_dev = HEADS // seq_count
    head_cols = heads_dev * HEAD_DIM
    experts_total = router.shape[1]
    exp_dev = expert_in.shape[1]

    small = jnp.concatenate([norm_gains, router], axis=1)
    small_cols = small.shape[1]
    ids_room = TOP * tok_count // (seq_count * rows_dev)
    small = jnp.pad(small, ((0, 0), (0, ids_room + -(small_cols + ids_room) % 128)))
    heads_rows = w_qkv.reshape(rows_dev, 3, seq_count, head_cols).transpose(2, 0, 1, 3)
    heads_rows = heads_rows.reshape(seq_count, rows_dev, 3 * head_cols)
    small = jnp.broadcast_to(small[None], (seq_count,) + small.shape)
    heads_seq = exchange(jnp.concatenate([heads_rows, small], axis=2), "seq")
    ids_low = expert_ids[0].astype(bf16).reshape(seq_count, rows_dev, -1)
    first_id = 3 * head_cols + small_cols
    ids_cols = ids_low.shape[2]
    after_ids = heads_seq.shape[2] - first_id - ids_cols
    heads_rows = heads_seq + jnp.pad(ids_low, ((0, 0), (0, 0), (first_id, after_ids)))
    cot_early = {
        k: lax.ppermute(cotangent[0], "exp", shift_pairs(exp_count, k))
        for k in range(1, exp_count)
        if k in EARLY
    }
    heads_near = gather_near(heads_rows.reshape(seq_count * rows_dev, -1), "exp")
    ids_group = jnp.stack(
        [near[:, first_id : first_id + ids_cols].reshape(tok_count, TOP) for near in heads_near]
    )
    heads_all = order_cores(heads_near, seq_count, "exp", "fsdp")
    heads_weight = heads_all[:, : 3 * head_cols]
    small = heads_all[:, 3 * head_cols : first_id].T
    gains = small[:4].astype(f32)
    router_rows = small[4:]
    out_rows = after(w_out, heads_seq)[None]
    out_rows = exchange(jnp.broadcast_to(out_rows, (seq_count,) + w_out.shape), "seq")
    out_rows = out_rows.reshape(seq_count * rows_dev, model_width)
    all_tokens = after(own_low, out_rows)[None]
    all_tokens = jnp.broadcast_to(all_tokens, (seq_count, tok_count, model_width))
    all_tokens = exchange(all_tokens, "seq").reshape(length, model_width)

    out_near = gather_near(after(out_rows, heads_near[-1]), "exp")

    parts = 1
    part_experts = exp_dev // parts
    sent = out_rows
    for near in cot_early.values():
        sent = after(sent[:16, :128], near)
    in_blocks = jnp.transpose(after(expert_in, sent), (1, 0, 2))
    down_blocks = jnp.transpose(after(expert_out, sent), (1, 0, 2))
    in_weights, down_weights = [], []
    for part in range(parts):
        chosen_experts = slice(part * part_experts, (part + 1) * part_experts)
        for blocks, weights in ((in_blocks, in_weights), (down_blocks, down_weights)):
            weights.append(
                lax.all_gather(blocks[chosen_experts], ("seq", "fsdp"), axis=1, tiled=True)
            )

    all_inputs = all_tokens.astype(f32)
    first_inverse = rms_inverse(all_inputs)
    attn_low = (all_inputs * first_inverse * gains[0]).astype(bf16)
    projected = jnp.dot(attn_low, heads_weight, preferred_element_type=f32)
    own_gains = lax.dynamic_slice_in_dim(gains, own_seq * head_cols, head_cols, 1)
    query_pre, key_pre = projected[:, :head_cols], projected[:, head_cols : 2 * head_cols]
    squares = jnp.stack([jnp.sum(query_pre * query_pre, axis=-1), jnp.sum(key_pre * key_pre, axis=-1)])
    squares = sum_all(squares, "seq")
    scales = lax.rsqrt(squares / model_width + epsilon).T
    turns = rotary_tables(jnp.arange(length, dtype=jnp.int32), HEAD_DIM)
    row_segment, col_segment = segment[:, None], segment[None, :]
    ready = scales
    for near in out_near[1:]:
        ready = after(ready, near)
    attended, queries, keys, values = attend(
        projected, ready, own_gains[1:3], turns, row_segment, col_segment, heads_dev
    )
    out_weight = order_cores(out_near, seq_count, "exp", "fsdp")
    merged = lax.all_to_all(attended, "seq", split_axis=0, concat_axis=1, tiled=True)
    branch = jnp.einsum("tc,dc->td", merged, out_weight, preferred_element_type=f32)
    residual = inputs + branch
    mlp_inverse = rms_inverse(residual)
    mlp_low = (residual * mlp_inverse * gains[3]).astype(bf16)

    capacity = tok_count * TOP // experts_total * 9 // 8
    near_experts = own_exp * exp_dev + jnp.arange(exp_dev, dtype=jnp.int32)
    chosen = jnp.any(
        ids_group[:, :, :, None] == near_experts.astype(bf16)[None, None, None, :], axis=2
    )
    earlier = (
        jnp.arange(tok_count)[:, None] > jnp.arange(tok_count)[None, :]
    ).astype(bf16)
    rank = jnp.einsum("tu,sue->est", earlier, chosen.astype(bf16), preferred_element_type=f32)
    rank = jnp.where(jnp.transpose(chosen, (2, 0, 1)), rank, -1.0)
    pick = rank[:, :, None, :] == jnp.arange(capacity, dtype=f32)[None, None, :, None]
    pick_low = pick.astype(bf16)
    turned = rank[:, :, :, None] == jnp.arange(capacity, dtype=f32)[None, None, None, :]
    turned_low = turned.astype(bf16)

    mlp_near = gather_near(mlp_low, "exp")
    late = cotangent[0]
    for near in mlp_near[1:]:
        late = after(late, near)
    cot_near = [cotangent[0]] + [
        cot_early[k] if k in cot_early else lax.ppermute(late, "exp", shift_pairs(exp_count, k))
        for k in range(1, exp_count)
    ]
    router_probs, gate_rows = route(own_exp * exp_dev, router_rows, pick_low, mlp_near)
    places = jnp.stack([ring_place(own_exp - k, exp_count) for k in range(exp_count)])
    kept = []
    for part in range(parts):
        kept = experts_forward(
            part * part_experts, kept, places.astype(jnp.int32), pick_low, turned_low, gate_rows,
            in_weights[part], down_weights[part], mlp_near,
        )
    expert_rows, gate, up, gated, mix = kept
    mix_near = exchange(mix, "exp")
    output = (residual + jnp.sum(mix_near.astype(f32), axis=0)).astype(bf16)

    cot_rows, down_grad = experts_down_grad(pick_low, gated, cot_near)
    grad_expert_out = lax.psum_scatter(
        down_grad, ("seq", "fsdp"), scatter_dimension=1, tiled=True
    )
    kept = []
    for part in range(parts):
        kept = experts_backward(
            part * part_experts, kept, turned_low, gate_rows, cot_rows, gate, up,
            in_weights[part], down_weights[part],
        )
    copy_near = send_near(kept[1:], "exp")
    before = jnp.stack([block[:16, :128] for block in kept[1:]])
    in_grad = experts_in_grad(expert_rows, kept[0], before)
    grad_expert_in = lax.psum_scatter(in_grad, ("seq", "fsdp"), scatter_dimension=1, tiled=True)
    copy_near[0] = after(after(copy_near[0], in_grad), mix_near)
    mlp_grad_experts = add_up([near[:, :model_width] for near in copy_near])
    prob_pairs = [
        near[:, model_width : model_width + 2 * exp_dev].astype(f32).reshape(tok_count, exp_dev, 2)
        for near in copy_near
    ]
    prob_grad = order([jnp.sum(pair, axis=2) for pair in prob_pairs], "exp", 1, 1)
    prob_grad = prob_grad.reshape(tok_count, experts_total)
    grad_expert_in = interleave([grad_expert_in])
    grad_expert_out = interleave([grad_expert_out])

    logit_grad = router_probs * (
        prob_grad - jnp.sum(router_probs * prob_grad, axis=-1, keepdims=True)
    )
    router_grad = jnp.dot(logit_grad.T, mlp_low.astype(f32), precision=highest)
    logit_high = logit_grad.astype(bf16)
    logit_low = (logit_grad - logit_high.astype(f32)).astype(bf16)
    mlp_grad = mlp_grad_experts + jnp.dot(
        jnp.concatenate([logit_high, logit_low], axis=1),
        jnp.concatenate([router_rows, router_rows], axis=0),
        preferred_element_type=f32,
    )
    residual_norm_grad, mlp_gain_grad = rms_back(mlp_grad, residual, mlp_inverse, gains[3])
    residual_grad = cotangent[0].astype(f32) + residual_norm_grad
    branch_grad = residual_grad.astype(bf16)

    merged_grad = jnp.einsum("td,dc->tc", branch_grad, out_weight, preferred_element_type=f32)
    heads_grad = lax.all_to_all(
        merged_grad.astype(bf16), "seq", split_axis=1, concat_axis=0, tiled=True
    )
    split_sizes = (seq_count, exp_count, core_count)
    out_terms = spread_product(
        branch_grad, merged, [], split_sizes, lax.axis_index("fsdp")
    )
    out_core = scatter_core(out_terms, "fsdp")
    out_sent = send_near(split(out_core, "exp"), "exp")
    out_terms = add_up(out_sent).astype(bf16)
    query_grad, key_grad, value_grad, inner = attend_back(
        queries, keys, values, heads_grad, projected, own_gains[1:3], turns, row_segment, col_segment,
        out_core[0, :16, :128], heads_dev,
    )
    means = sum_all(inner.T, "seq").T / model_width
    qkv_grad, head_gain_grads = norm_back(
        query_grad, key_grad, value_grad, projected, scales, means, own_gains[1:3]
    )
    query_gain_grad, key_gain_grad = head_gain_grads[0], head_gain_grads[1]

    zero_row = jnp.zeros((model_width,), f32)
    small_terms = jnp.concatenate(
        [
            jnp.stack(
                [
                    zero_row,
                    lax.dynamic_update_slice_in_dim(zero_row, query_gain_grad, own_seq * head_cols, 0),
                    lax.dynamic_update_slice_in_dim(zero_row, key_gain_grad, own_seq * head_cols, 0),
                    mlp_gain_grad,
                ]
            ),
            router_grad,
        ],
        axis=0,
    ).T
    small_terms = jnp.pad(small_terms, ((0, 0), (0, -small_cols % 128)))
    beside = [small_terms, heads_all, gains[0][:, None]]
    heads_terms = spread_product(
        attn_low, qkv_grad, beside, split_sizes, lax.axis_index("fsdp")
    )
    heads_terms = scatter_core(heads_terms, "fsdp", out_sent[1:])
    attn_in_part = jnp.einsum(
        "tc,dc->td", after(qkv_grad, heads_terms), heads_weight, preferred_element_type=f32
    )
    attn_in_grad = exchange(
        attn_in_part.astype(bf16).reshape(seq_count, tok_count, model_width), "seq"
    )
    attn_in_grad = jnp.sum(attn_in_grad.astype(f32), axis=0)
    heads_terms = scatter(heads_terms, "exp").astype(bf16)
    terms_cols = heads_terms.shape[1]
    last_terms = jnp.concatenate([heads_terms, out_terms], axis=1)
    last_near = send_near(split(last_terms.reshape(seq_count, rows_dev, -1), "seq"), "seq")
    grad_w_out = add_up([near[:, terms_cols:] for near in last_near])
    small_grad = add_up(
        [near[:, 3 * head_cols : 3 * head_cols + small_cols] for near in last_near]
    )
    heads_terms = order([near[:, : 3 * head_cols] for near in last_near], "seq", 0, 1)
    heads_terms = after(heads_terms, attn_in_grad)
    grad_w_qkv = jnp.concatenate(
        [
            heads_terms[source, :, part * head_cols : (part + 1) * head_cols]
            for part in range(3)
            for source in range(seq_count)
        ],
        axis=1,
    ).astype(f32)

    own_inverse = lax.dynamic_slice_in_dim(first_inverse, own_seq * tok_count, tok_count, 0)
    input_norm_grad, _ = rms_back(attn_in_grad, inputs, own_inverse, gains[0])
    input_grad = residual_grad + input_norm_grad

    return (
        output[None],
        input_grad[None],
        small_grad[:, :4],
        grad_w_qkv,
        grad_w_out,
        small_grad[:, 4:],
        grad_expert_in,
        grad_expert_out,
    )


def solution(mesh):
    in_specs = (
        P(("exp", "fsdp"), "seq", None),
        P(("exp", "fsdp"), "seq", None),
        P(("exp", "fsdp"), "seq", None),
        P(("exp", "fsdp"), None),
        P(("seq", "exp", "fsdp"), None),
        P(("seq", "exp", "fsdp"), None),
        P(("seq", "exp", "fsdp"), None),
        P(("seq", "exp", "fsdp"), None),
        P(("seq", "fsdp"), "exp", None),
        P(("seq", "fsdp"), "exp", None),
    )
    out_specs = (
        P(("exp", "fsdp"), "seq", None),
        P(("exp", "fsdp"), "seq", None),
        P(("seq", "exp", "fsdp"), None),
        P(("seq", "exp", "fsdp"), None),
        P(("seq", "exp", "fsdp"), None),
        P(("seq", "exp", "fsdp"), None),
        P(("seq", "fsdp"), "exp", None),
        P(("seq", "fsdp"), "exp", None),
    )
    return jax.shard_map(
        on_device, mesh=mesh, in_specs=in_specs, out_specs=out_specs, check_vma=False
    )
```

```python
import functools

import jax
import jax.numpy as jnp
from jax import lax
from jax.experimental import pallas as pl
from jax.experimental.pallas import tpu as pltpu
from jax.sharding import PartitionSpec as P

HEADS = 16
HEAD_DIM = 128
FF = 1024
TOP = 8
EARLY = (1,)
ATT_BLOCK = 256


epsilon = 1e-05
rotary_base = 10000.0
highest = lax.Precision.HIGHEST
f32 = jnp.float32
bf16 = jnp.bfloat16
VMEM_BYTES = 63 * 1024 * 1024
KERNEL_PARAMS = pltpu.CompilerParams(vmem_limit_bytes=VMEM_BYTES)
SMALL_COST = pl.CostEstimate(flops=1, bytes_accessed=1, transcendentals=0)
DOWN_GRAD_COST = pl.CostEstimate(flops=10**11, bytes_accessed=1, transcendentals=0)
ATTEND_BACK_COST = pl.CostEstimate(flops=310 * 10**9, bytes_accessed=1, transcendentals=0)


def after(value, other):
    first = lax.slice(other, (0,) * other.ndim, (1,) * other.ndim).reshape(())
    return value + (0.0 * first.astype(f32)).astype(value.dtype)


def swap_pairs(count, mask):
    return [(i, i ^ mask) for i in range(count)]


def shift_pairs(count, step):
    return [(i, (i + step) % count) for i in range(count)]


def ring_place(index, count):
    return index & (count - 1) if count & (count - 1) == 0 else lax.rem(index + count, count)


def exchange(stacked, axis, split_axis=0):
    return lax.all_to_all(stacked, axis, split_axis=split_axis, concat_axis=split_axis, tiled=True)


def gather_near(block, axis):
    count = lax.axis_size(axis)
    return [block] + [
        lax.ppermute(block, axis, shift_pairs(count, k)) for k in range(1, count)
    ]


def send_near(blocks, axis):
    count = lax.axis_size(axis)
    return [blocks[0]] + [
        lax.ppermute(blocks[k], axis, shift_pairs(count, -k)) for k in range(1, count)
    ]


def add_up(blocks):
    return sum(block.astype(f32) for block in blocks)


def order(blocks, axis, out_axis=0, sign=-1):
    count = lax.axis_size(axis)
    own = lax.axis_index(axis)
    shape = blocks[0].shape[:out_axis] + (count,) + blocks[0].shape[out_axis:]
    out = jnp.zeros(shape, blocks[0].dtype)
    for k, block in enumerate(blocks):
        place = ring_place(own + sign * k, count)
        out = lax.dynamic_update_index_in_dim(out, block, place, out_axis)
    return out


def split(stacked, axis, in_axis=0, sign=-1):
    count = lax.axis_size(axis)
    own = lax.axis_index(axis)
    return [
        lax.dynamic_index_in_dim(
            stacked, ring_place(own + sign * k, count), in_axis, keepdims=False
        )
        for k in range(count)
    ]


def gather(block, axis, out_axis=0):
    return order(gather_near(block, axis), axis, out_axis)


def scatter(stacked, axis, split_axis=0):
    return add_up(send_near(split(stacked, axis, split_axis), axis))


def sum_all(value, axis):
    count = lax.axis_size(axis)
    return jnp.sum(exchange(jnp.broadcast_to(value[None], (count,) + value.shape), axis), axis=0)


def assemble_kernel(groups, parts, place_ref, *refs):
    sources, out_ref, sems = refs[: len(refs) - 2], refs[-2], refs[-1]
    rows = sources[0].shape[0] // groups
    copies = []
    for k, source in enumerate(sources):
        for group in range(groups):
            target = pl.multiple_of((group * parts + place_ref[k]) * rows, rows)
            copies.append(
                pltpu.make_async_copy(
                    source.at[pl.ds(group * rows, rows)],
                    out_ref.at[pl.ds(target, rows)],
                    sems.at[k, group],
                )
            )
    for copy in copies:
        copy.start()
    for copy in copies:
        copy.wait()


def assemble(blocks, places, groups):
    parts = len(blocks)
    return pl.pallas_call(
        functools.partial(assemble_kernel, groups, parts),
        in_specs=[pl.BlockSpec(memory_space=pltpu.SMEM)]
        + [pl.BlockSpec(memory_space=pltpu.VMEM)] * parts,
        out_specs=pl.BlockSpec(memory_space=pl.ANY),
        out_shape=jax.ShapeDtypeStruct(
            (parts * blocks[0].shape[0], blocks[0].shape[1]), blocks[0].dtype
        ),
        scratch_shapes=[pltpu.SemaphoreType.DMA((parts, groups))],
        compiler_params=KERNEL_PARAMS,
        cost_estimate=SMALL_COST,
        name="assemble",
    )(places, *blocks)


def order_cores(blocks, groups, axis, core_axis):
    count, cores = lax.axis_size(axis), lax.axis_size(core_axis)
    own, own_core = lax.axis_index(axis), lax.axis_index(core_axis)
    if cores == 2:
        blocks = blocks + [lax.ppermute(block, core_axis, swap_pairs(2, 1)) for block in blocks]
        core_places = [own_core, 1 - own_core]
    else:
        every = lax.all_gather(jnp.stack(blocks), core_axis, axis=0)
        blocks = [every[core, k] for core in range(cores) for k in range(count)]
        core_places = list(range(cores))
    places = [
        ring_place(own - k, count) * cores + core for core in core_places for k in range(count)
    ]
    places = jnp.stack([jnp.asarray(place, jnp.int32) for place in places])
    return assemble(blocks, places, groups)


def scatter_core(terms, axis, earlier=()):
    if len(terms) == 1:
        return lax.psum_scatter(terms[0], axis, scatter_dimension=0, tiled=False)
    kept, given = terms
    for array in earlier:
        given = after(given, array)
    received = lax.ppermute(given, axis, swap_pairs(2, 1))
    return (kept.astype(f32) + received.astype(f32)).astype(kept.dtype)


def rms_inverse(values):
    return lax.rsqrt(jnp.mean(values * values, axis=-1, keepdims=True) + epsilon)


def rms_back(gradient, values, inverse, gain_vector):
    scaled = gradient * gain_vector
    gain_grad = jnp.sum(gradient * values * inverse, axis=0)
    value_grad = inverse * scaled - values * inverse**3 * jnp.mean(
        scaled * values, axis=-1, keepdims=True
    )
    return (value_grad, gain_grad)


def rotary_tables(position, head_dim):
    half_dim = head_dim // 2
    exponent = jnp.arange(half_dim, dtype=f32) * (2.0 / head_dim)
    angles = position.astype(f32)[:, None] * (rotary_base ** (-exponent))[None, :]
    cosine, sine_part = jnp.cos(angles), jnp.sin(angles)
    return jnp.stack(
        [
            jnp.concatenate([cosine, cosine], axis=1),
            jnp.concatenate([-sine_part, sine_part], axis=1),
        ]
    )


def dot(one, other, one_axis, other_axis):
    return lax.dot_general(
        one, other, (((one_axis,), (other_axis,)), ((), ())), preferred_element_type=f32
    )


def turn(values, cosines, sines):
    return values * cosines + pltpu.roll(values, HEAD_DIM // 2, 1) * sines


def block_probs(query_rows, keys, query_segment, key_segment, scale):
    scores = dot(query_rows, keys, 1, 1) * scale
    scores = jnp.where(query_segment == key_segment, scores, -jnp.inf)
    terms = jnp.exp(scores - jnp.max(scores, axis=1, keepdims=True))
    return terms / jnp.sum(terms, axis=1, keepdims=True)


def attend_kernel(
    query_ref, key_ref, value_ref, scale_ref, gain_ref, turn_ref, row_seg_ref, col_seg_ref,
    out_ref, query_low_ref, key_low_ref, value_low_ref,
):
    length = query_ref.shape[0]
    cosines, sines = turn_ref[0], turn_ref[1]
    query = query_ref[...] * scale_ref[:, 0:1] * gain_ref[0:1, :]
    key = key_ref[...] * scale_ref[:, 1:2] * gain_ref[1:2, :]
    query_low_ref[...] = turn(query, cosines, sines).astype(bf16)
    key_low_ref[...] = turn(key, cosines, sines).astype(bf16)
    value_low_ref[...] = value_ref[...].astype(bf16)
    for start in range(0, length, ATT_BLOCK):
        stop = start + ATT_BLOCK
        probs = block_probs(
            query_low_ref[start:stop],
            key_low_ref[:stop],
            row_seg_ref[start:stop, 0:1],
            col_seg_ref[0:1, :stop],
            HEAD_DIM ** (-0.5),
        )
        out = dot(probs.astype(bf16), value_low_ref[:stop], 1, 0)
        out_ref[start:stop] = out.astype(bf16)


def attend(projected, scales, gains, turns, row_segment, col_segment, heads):
    length = projected.shape[0]
    column = lambda part: pl.BlockSpec((length, HEAD_DIM), lambda h: (0, part * heads + h))
    whole = lambda shape: pl.BlockSpec(shape, lambda h: (0,) * len(shape))
    out = pl.BlockSpec((length, HEAD_DIM), lambda h: (0, h))
    return pl.pallas_call(
        attend_kernel,
        grid=(heads,),
        in_specs=[
            column(0), column(1), column(2), whole(scales.shape),
            pl.BlockSpec((2, HEAD_DIM), lambda h: (0, h)),
            whole(turns.shape), whole(row_segment.shape), whole(col_segment.shape),
        ],
        out_specs=[out] * 4,
        out_shape=[jax.ShapeDtypeStruct((length, heads * HEAD_DIM), bf16)] * 4,
        compiler_params=KERNEL_PARAMS,
        cost_estimate=SMALL_COST,
        name="attend",
    )(projected, projected, projected, scales, gains, turns, row_segment, col_segment)


def attend_back_kernel(
    query_ref, key_ref, value_ref, grad_ref, query_pre_ref, key_pre_ref, gain_ref, turn_ref,
    row_seg_ref, col_seg_ref, earlier_ref,
    query_out_ref, key_out_ref, value_out_ref, inner_ref, key_sum_ref, value_sum_ref,
):
    length = query_ref.shape[0]
    scale = HEAD_DIM ** (-0.5)
    cosines, sines = turn_ref[0], -turn_ref[1]
    first = pl.program_id(0) == 0
    for start in reversed(range(0, length, ATT_BLOCK)):
        stop = start + ATT_BLOCK
        query_rows, grad_rows, keys = query_ref[start:stop], grad_ref[start:stop], key_ref[:stop]
        probs = block_probs(
            query_rows, keys, row_seg_ref[start:stop, 0:1], col_seg_ref[0:1, :stop], scale
        )
        value_terms = dot(probs.astype(bf16), grad_rows, 0, 0)
        prob_grad = dot(grad_rows, value_ref[:stop], 1, 1)
        inner = jnp.sum(probs * prob_grad, axis=1, keepdims=True)
        score_grad = (probs * (prob_grad - inner)).astype(bf16)
        query_grad = (dot(score_grad, keys, 1, 0) * scale).astype(bf16).astype(f32)
        query_grad = turn(query_grad, cosines[start:stop], sines[start:stop])
        query_out_ref[start:stop] = query_grad
        query_inner = query_grad * gain_ref[0:1, :] * query_pre_ref[start:stop]
        query_inner = jnp.sum(query_inner, axis=1, keepdims=True)
        inner_ref[start:stop, 0:1] = query_inner + jnp.where(first, 0.0, inner_ref[start:stop, 0:1])
        key_terms = dot(score_grad, query_rows, 0, 0)
        if stop == length:
            key_sum_ref[...] = key_terms
            value_sum_ref[...] = value_terms
        else:
            key_sum_ref[:stop] += key_terms
            value_sum_ref[:stop] += value_terms
    key_grad = (key_sum_ref[...] * scale).astype(bf16).astype(f32)
    key_grad = turn(key_grad, cosines, sines)
    key_out_ref[...] = key_grad
    key_inner = jnp.sum(key_grad * gain_ref[1:2, :] * key_pre_ref[...], axis=1, keepdims=True)
    inner_ref[:, 1:2] = key_inner + jnp.where(first, 0.0, inner_ref[:, 1:2])
    value_out_ref[...] = value_sum_ref[...].astype(bf16)


def attend_back(
    queries, keys, values, grads, projected, gains, turns, row_segment, col_segment, earlier, heads
):
    length = queries.shape[0]
    column = pl.BlockSpec((length, HEAD_DIM), lambda h: (0, h))
    whole = lambda shape: pl.BlockSpec(shape, lambda h: (0,) * len(shape))
    shape = (length, heads * HEAD_DIM)
    return pl.pallas_call(
        attend_back_kernel,
        grid=(heads,),
        in_specs=[column] * 4
        + [column, pl.BlockSpec((length, HEAD_DIM), lambda h: (0, heads + h))]
        + [pl.BlockSpec((2, HEAD_DIM), lambda h: (0, h))]
        + [whole(turns.shape), whole(row_segment.shape), whole(col_segment.shape)]
        + [pl.BlockSpec(memory_space=pl.ANY)],
        out_specs=[column] * 3 + [whole((length, 2))],
        out_shape=[
            jax.ShapeDtypeStruct(shape, f32),
            jax.ShapeDtypeStruct(shape, f32),
            jax.ShapeDtypeStruct(shape, bf16),
            jax.ShapeDtypeStruct((length, 2), f32),
        ],
        scratch_shapes=[pltpu.VMEM((length, HEAD_DIM), f32)] * 2,
        compiler_params=KERNEL_PARAMS,
        cost_estimate=ATTEND_BACK_COST,
        name="attend_back",
    )(
        queries, keys, values, grads, projected, projected, gains, turns, row_segment, col_segment, earlier
    )


def interleave_kernel(*refs):
    expert = 0
    for ref in refs[:-1]:
        for k in range(ref.shape[0]):
            refs[-1][:, expert, :] = ref[k].astype(f32)
            expert += 1


def interleave(parts):
    _, rows, width = parts[0].shape
    experts = sum(part.shape[0] for part in parts)
    block = min(rows, 64)
    return pl.pallas_call(
        interleave_kernel,
        grid=(rows // block,),
        in_specs=[
            pl.BlockSpec((part.shape[0], block, width), lambda i: (0, i, 0)) for part in parts
        ],
        out_specs=pl.BlockSpec((block, experts, width), lambda i: (i, 0, 0)),
        out_shape=jax.ShapeDtypeStruct((rows, experts, width), f32),
        compiler_params=KERNEL_PARAMS,
        cost_estimate=SMALL_COST,
        name="interleave",
    )(*parts)


def norm_back_kernel(
    query_grad_ref, key_grad_ref, value_grad_ref, query_pre_ref, key_pre_ref, scale_ref, mean_ref, gain_ref,
    out_ref, gain_grad_ref,
):
    width = query_grad_ref.shape[1]

    @pl.when(pl.program_id(0) == 0)
    def _():
        gain_grad_ref[...] = jnp.zeros_like(gain_grad_ref)

    for part, (grad_ref, pre_ref) in enumerate(
        ((query_grad_ref, query_pre_ref), (key_grad_ref, key_pre_ref))
    ):
        here = slice(part, part + 1)
        grad, scale = grad_ref[...], scale_ref[:, here]
        normal = pre_ref[...] * scale
        gain_grad_ref[here, :] += jnp.sum(grad * normal, axis=0, keepdims=True)
        back = scale * (grad * gain_ref[here, :]) - normal * (scale * scale * mean_ref[:, here])
        out_ref[:, part * width : (part + 1) * width] = back.astype(bf16)
    out_ref[:, 2 * width :] = value_grad_ref[...]


def norm_back(query_grad, key_grad, value_grad, projected, scales, means, gains):
    length, width = query_grad.shape
    block = min(length, 256)
    rows = lambda columns, part: pl.BlockSpec((block, columns), lambda i: (i, part))
    whole = lambda shape: pl.BlockSpec(shape, lambda i: (0,) * len(shape))
    return pl.pallas_call(
        norm_back_kernel,
        grid=(length // block,),
        in_specs=[rows(width, 0)] * 3
        + [rows(width, 0), rows(width, 1), rows(2, 0), rows(2, 0), whole(gains.shape)],
        out_specs=[rows(3 * width, 0), whole(gains.shape)],
        out_shape=[
            jax.ShapeDtypeStruct((length, 3 * width), bf16),
            jax.ShapeDtypeStruct(gains.shape, f32),
        ],
        compiler_params=KERNEL_PARAMS,
        cost_estimate=SMALL_COST,
        name="norm_back",
    )(query_grad, key_grad, value_grad, projected, projected, scales, means, gains)


def chunk_of(width, most):
    return most if width % most == 0 else width


def route_kernel(experts_total, count, first_ref, router_ref, pick_ref, *refs):
    near_refs, (gate_ref, probs_ref) = refs[:count], refs[count:]
    experts, _, capacity, tokens = pick_ref.shape
    lane = lax.broadcasted_iota(jnp.int32, (tokens, router_ref.shape[0]), 1)
    for k in range(count):
        logits = dot(near_refs[k][...], router_ref[...], 1, 1)
        logits = jnp.where(lane < experts_total, logits, -jnp.inf)
        terms = jnp.exp(logits - jnp.max(logits, axis=1, keepdims=True))
        probs = terms / jnp.sum(terms, axis=1, keepdims=True)
        if k == 0:
            probs_ref[...] = probs
        pairs = jnp.zeros((tokens, router_ref.shape[0]), f32)
        for j in range(experts):
            prob = jnp.sum(jnp.where(lane == first_ref[0] + j, probs, 0.0), axis=1, keepdims=True)
            high = prob.astype(bf16).astype(f32)
            pairs = jnp.where(lane == 2 * j, high, pairs)
            pairs = jnp.where(lane == 2 * j + 1, prob - high, pairs)
        pairs = pairs.astype(bf16)
        for j in range(experts):
            gates = dot(pick_ref[j, k], pairs, 1, 0)
            gate_ref[j, k * capacity : (k + 1) * capacity] = (
                gates[:, 2 * j : 2 * j + 1] + gates[:, 2 * j + 1 : 2 * j + 2]
            )


def route(first, router_rows, pick, near):
    experts, count, capacity, tokens = pick.shape
    experts_total = router_rows.shape[0]
    lanes = 128 * -(-max(experts_total, 2 * experts) // 128)
    router_rows = jnp.pad(router_rows, ((0, lanes - experts_total), (0, 0)))
    vmem = pl.BlockSpec(memory_space=pltpu.VMEM)
    gates, probs = pl.pallas_call(
        functools.partial(route_kernel, experts_total, count),
        in_specs=[pl.BlockSpec(memory_space=pltpu.SMEM)] + [vmem] * (2 + count),
        out_shape=[
            jax.ShapeDtypeStruct((experts, count * capacity, 1), f32),
            jax.ShapeDtypeStruct((tokens, lanes), f32),
        ],
        compiler_params=KERNEL_PARAMS,
        cost_estimate=SMALL_COST,
        name="route",
    )(jnp.reshape(first.astype(jnp.int32), (1,)), router_rows, pick, *near)
    return probs[:, :experts_total], gates


def forward_kernel(count, kept, place_ref, pick_ref, turned_ref, gate_ref, in_ref, down_ref, *refs):
    near_refs, refs = refs[:count], refs[count:]
    earlier_refs, refs = refs[4:kept], refs[kept:]
    rows_ref, gate_out_ref, up_out_ref, gated_ref, mix_ref, result_ref = refs
    step_number, steps = pl.program_id(0), pl.num_programs(0)
    capacity, width = pick_ref.shape[2], rows_ref.shape[2]
    hidden = gated_ref.shape[2]
    for k in range(count):
        rows_ref[0, k * capacity : (k + 1) * capacity] = dot(
            pick_ref[0, k], near_refs[k][...], 1, 0
        ).astype(bf16)
    step = chunk_of(hidden, 512)
    for start in range(0, hidden, step):
        low, high = slice(start, start + step), slice(hidden + start, hidden + start + step)
        gate = dot(rows_ref[0], in_ref[0, :, low], 1, 0)
        up = dot(rows_ref[0], in_ref[0, :, high], 1, 0)
        gate_out_ref[0, :, low] = gate.astype(bf16)
        up_out_ref[0, :, low] = up.astype(bf16)
        gated_ref[0, :, low] = (gate * jax.nn.sigmoid(gate) * up * gate_ref[0]).astype(bf16)
    wide = chunk_of(width, 1024)
    for start in range(0, width, wide):
        cols = slice(start, start + wide)
        result_ref[step_number, :, cols] = dot(gated_ref[0], down_ref[0, cols, :], 1, 1).astype(bf16)

    @pl.when(step_number == steps - 1)
    def _():
        for k in range(count):
            rows = slice(k * capacity, (k + 1) * capacity)
            for start in range(0, width, wide):
                cols = slice(start, start + wide)
                mix = dot(turned_ref[0, k], result_ref[0, rows, cols], 1, 0)
                for expert in range(1, result_ref.shape[0]):
                    mix += dot(turned_ref[expert, k], result_ref[expert, rows, cols], 1, 0)
                if earlier_refs:
                    mix += earlier_refs[0][place_ref[k], :, cols].astype(f32)
                mix_ref[place_ref[k], :, cols] = mix.astype(bf16)


def experts_forward(first, kept, places, pick, turned, gates, in_weight, down_weight, near):
    experts, count, capacity, tokens = pick.shape
    here, width, hidden = in_weight.shape[0], in_weight.shape[1], down_weight.shape[2]
    rows = count * capacity
    each = lambda shape: pl.BlockSpec((1,) + shape, lambda e: (first + e,) + (0,) * len(shape))
    near_each = lambda shape: pl.BlockSpec((1,) + shape, lambda e: (e,) + (0,) * len(shape))
    whole = pl.BlockSpec((tokens, width), lambda e: (0, 0), pipeline_mode=pl.Buffered(1))
    sums = pl.BlockSpec((count, tokens, width), lambda e: (0, 0, 0), pipeline_mode=pl.Buffered(1))
    return pl.pallas_call(
        functools.partial(forward_kernel, count, len(kept)),
        grid=(here,),
        in_specs=[
            pl.BlockSpec(memory_space=pltpu.SMEM),
            each((count, capacity, tokens)),
            pl.BlockSpec(
                (here,) + turned.shape[1:], lambda e: (first // here, 0, 0, 0), pipeline_mode=pl.Buffered(1)
            ),
            each((rows, 1)),
            near_each((width, 2 * hidden)), near_each((width, hidden)),
        ] + [whole] * count + [pl.BlockSpec(memory_space=pl.ANY)] * len(kept[:4]) + [sums] * len(kept[4:]),
        out_specs=[each((rows, width))] + [each((rows, hidden))] * 3 + [sums],
        out_shape=[jax.ShapeDtypeStruct((experts, rows, width), bf16)]
        + [jax.ShapeDtypeStruct((experts, rows, hidden), bf16)] * 3
        + [jax.ShapeDtypeStruct((count, tokens, width), bf16)],
        scratch_shapes=[pltpu.VMEM((here, rows, width), bf16)],
        input_output_aliases={6 + count + i: i for i in range(len(kept[:4]))},
        compiler_params=KERNEL_PARAMS,
        cost_estimate=SMALL_COST,
        name="experts_forward",
    )(places, pick, turned, gates, in_weight, down_weight, *near, *kept)


def down_grad_kernel(count, pick_ref, gated_ref, *refs):
    near_refs = refs[:count]
    rows_ref, grad_ref = refs[count:]
    capacity, width = pick_ref.shape[2], rows_ref.shape[2]
    for k in range(count):
        rows_ref[0, k * capacity : (k + 1) * capacity] = dot(
            pick_ref[0, k], near_refs[k][...], 1, 0
        ).astype(bf16)
    step = chunk_of(width, 2048)

    @pl.loop(0, width // step)
    def _(j):
        cols = pl.ds(pl.multiple_of(j * step, step), step)
        grad_ref[0, cols, :] = dot(rows_ref[0, :, cols], gated_ref[0], 0, 0).astype(bf16)


def experts_down_grad(pick, gated, near):
    experts, count, capacity, tokens = pick.shape
    width, hidden = near[0].shape[1], gated.shape[2]
    rows = count * capacity
    each = lambda shape: pl.BlockSpec((1,) + shape, lambda e: (e,) + (0,) * len(shape))
    whole = pl.BlockSpec((tokens, width), lambda e: (0, 0), pipeline_mode=pl.Buffered(1))
    return pl.pallas_call(
        functools.partial(down_grad_kernel, count),
        grid=(experts,),
        in_specs=[each((count, capacity, tokens)), each((rows, hidden))] + [whole] * count,
        out_specs=[each((rows, width)), each((width, hidden))],
        out_shape=[
            jax.ShapeDtypeStruct((experts, rows, width), bf16),
            jax.ShapeDtypeStruct((experts, width, hidden), bf16),
        ],
        compiler_params=KERNEL_PARAMS,
        cost_estimate=DOWN_GRAD_COST,
        name="experts_down_grad",
    )(pick, gated, *near)


def backward_kernel(
    first, count, kept, turned_ref, gate_rows_ref, cot_ref, gate_ref, up_ref, in_ref, down_ref, *refs
):
    earlier_refs, refs = refs[1:kept], refs[kept:]
    both_ref = refs[0]
    copy_refs = refs[1 : 1 + count]
    result_ref, inner_ref = refs[1 + count :]
    step_number, steps = pl.program_id(0), pl.num_programs(0)
    capacity, width = turned_ref.shape[3], cot_ref.shape[2]
    hidden = gate_ref.shape[2]
    lanes = inner_ref.shape[2]
    step = chunk_of(hidden, 512)
    inner = jnp.zeros((count * capacity, 1), f32)
    for start in range(0, hidden, step):
        low, high = slice(start, start + step), slice(hidden + start, hidden + start + step)
        result_grad = dot(cot_ref[0], down_ref[0, :, low], 1, 0)
        gate, up = gate_ref[0, :, low].astype(f32), up_ref[0, :, low].astype(f32)
        sigmoid = jax.nn.sigmoid(gate)
        silu = gate * sigmoid
        inner += jnp.sum(result_grad * silu * up, axis=1, keepdims=True)
        act_grad = result_grad * gate_rows_ref[0]
        both_ref[0, :, low] = (act_grad * up * (sigmoid + silu * (1.0 - sigmoid))).astype(bf16)
        both_ref[0, :, high] = (act_grad * silu).astype(bf16)
    inner_high = inner.astype(bf16).astype(f32)
    lane = lax.broadcasted_iota(jnp.int32, (count * capacity, lanes), 1)
    place = 2 * (first + step_number)
    inner_wide = jnp.where(lane == place, inner_high, 0.0)
    inner_wide = jnp.where(lane == place + 1, inner - inner_high, inner_wide)
    inner_ref[step_number] = inner_wide.astype(bf16)
    wide = chunk_of(width, 1024)
    for start in range(0, width, wide):
        cols = slice(start, start + wide)
        result_ref[step_number, :, cols] = dot(both_ref[0], in_ref[0, cols, :], 1, 1).astype(bf16)

    @pl.when(step_number == steps - 1)
    def _():
        for k in range(count):
            rows = slice(k * capacity, (k + 1) * capacity)
            pieces = [(result_ref, slice(start, start + wide), start) for start in range(0, width, wide)]
            for ref, cols, start in pieces + [(inner_ref, slice(0, lanes), width)]:
                copies = dot(turned_ref[0, k], ref[0, rows, cols], 1, 0)
                for expert in range(1, result_ref.shape[0]):
                    copies += dot(turned_ref[expert, k], ref[expert, rows, cols], 1, 0)
                target = slice(start, start + cols.stop - cols.start)
                if earlier_refs:
                    copies += earlier_refs[k][:, target].astype(f32)
                copy_refs[k][:, target] = copies.astype(bf16)


def experts_backward(first, kept, turned, gate_rows, cot_rows, gate, up, in_weight, down_weight):
    experts, count, tokens, capacity = turned.shape
    here, width, hidden = in_weight.shape[0], in_weight.shape[1], down_weight.shape[2]
    rows = count * capacity
    lanes = 128 * -(-2 * experts // 128)
    each = lambda shape: pl.BlockSpec((1,) + shape, lambda e: (first + e,) + (0,) * len(shape))
    near_each = lambda shape: pl.BlockSpec((1,) + shape, lambda e: (e,) + (0,) * len(shape))
    whole = pl.BlockSpec((tokens, width + lanes), lambda e: (0, 0), pipeline_mode=pl.Buffered(1))
    return pl.pallas_call(
        functools.partial(backward_kernel, first, count, len(kept)),
        grid=(here,),
        in_specs=[
            pl.BlockSpec(
                (here,) + turned.shape[1:], lambda e: (first // here, 0, 0, 0), pipeline_mode=pl.Buffered(1)
            ),
            each((rows, 1)), each((rows, width)),
            each((rows, hidden)), each((rows, hidden)),
            near_each((width, 2 * hidden)), near_each((width, hidden)),
        ] + [pl.BlockSpec(memory_space=pl.ANY)] * len(kept[:1]) + [whole] * len(kept[1:]),
        out_specs=[each((rows, 2 * hidden))] + [whole] * count,
        out_shape=[jax.ShapeDtypeStruct((experts, rows, 2 * hidden), bf16)]
        + [jax.ShapeDtypeStruct((tokens, width + lanes), bf16)] * count,
        scratch_shapes=[
            pltpu.VMEM((here, rows, width), bf16),
            pltpu.VMEM((here, rows, lanes), bf16),
        ],
        input_output_aliases={7 + i: i for i in range(len(kept[:1]))},
        compiler_params=KERNEL_PARAMS,
        cost_estimate=SMALL_COST,
        name="experts_backward",
    )(turned, gate_rows, cot_rows, gate, up, in_weight, down_weight, *kept)


def in_grad_kernel(rows_ref, both_ref, earlier_ref, grad_ref):
    width = rows_ref.shape[2]
    step = chunk_of(width, 512)

    @pl.loop(0, width // step)
    def _(j):
        cols = pl.ds(pl.multiple_of(j * step, step), step)
        grad_ref[0, cols, :] = dot(rows_ref[0, :, cols], both_ref[0], 0, 0).astype(bf16)


def experts_in_grad(rows, both, earlier):
    experts, _, width = rows.shape
    each = lambda shape: pl.BlockSpec((1,) + shape, lambda e: (e,) + (0,) * len(shape))
    return pl.pallas_call(
        in_grad_kernel,
        grid=(experts,),
        in_specs=[each(rows.shape[1:]), each(both.shape[1:]), pl.BlockSpec(memory_space=pl.ANY)],
        out_specs=each((width, both.shape[2])),
        out_shape=jax.ShapeDtypeStruct((experts, width, both.shape[2]), bf16),
        compiler_params=KERNEL_PARAMS,
        cost_estimate=SMALL_COST,
        name="experts_in_grad",
    )(rows, both, earlier)


def spread_kernel(split, outs, own_ref, left_ref, right_ref, *refs):
    groups, parts, cores = split
    extra_refs, out_refs = refs[:-outs], refs[-outs:]
    width = right_ref.shape[1]
    rows = out_refs[0].shape[-2] // groups
    each = parts * cores * rows

    def store(core, place, columns, values):
        if outs == 1:
            out_refs[0][(core,) + place + (columns,)] = values
            return
        for index, ref in enumerate(out_refs):

            @pl.when(own_ref[0] == (core if index == 0 else 1 - core))
            def _():
                ref[place + (columns,)] = values

    for group in range(groups):
        here = slice(group * each, (group + 1) * each)
        terms = dot(left_ref[:, here], right_ref[...], 0, 0)
        low_terms = terms.astype(bf16)
        if extra_refs:
            beside_ref, weight_ref, gain_ref = extra_refs
            sums = jnp.sum(terms * weight_ref[here, :width].astype(f32), axis=1, keepdims=True)
            beside = beside_ref[here, :]
            lane = lax.broadcasted_iota(jnp.int32, beside.shape, 1)
            beside = jnp.where(lane == 0, sums / gain_ref[here, :], beside).astype(bf16)
        for part in range(parts):
            for core in range(cores):
                start = (part * cores + core) * rows
                place = (part, slice(group * rows, (group + 1) * rows))
                store(core, place, slice(0, width), low_terms[start : start + rows])
                if extra_refs:
                    columns = slice(width, width + beside.shape[1])
                    store(core, place, columns, beside[start : start + rows])


def spread_product(left, right, beside, split, own_core):
    groups, parts, cores = split
    rows = left.shape[1] // (groups * parts * cores)
    width = right.shape[1] + (beside[0].shape[1] if beside else 0)
    shape = (parts, groups * rows, width)
    shapes = [shape] * 2 if cores == 2 else [(cores,) + shape]
    arrays = [left, right] + beside
    return pl.pallas_call(
        functools.partial(spread_kernel, split, len(shapes)),
        in_specs=[pl.BlockSpec(memory_space=pltpu.SMEM)]
        + [pl.BlockSpec(memory_space=pltpu.VMEM)] * len(arrays),
        out_shape=[jax.ShapeDtypeStruct(shape, bf16) for shape in shapes],
        compiler_params=KERNEL_PARAMS,
        cost_estimate=SMALL_COST,
        name="spread_product",
    )(jnp.reshape(own_core.astype(jnp.int32), (1,)), *arrays)


def on_device(
    tokens,
    cotangent,
    expert_ids,
    segment_ids,
    norm_gains,
    w_qkv,
    w_out,
    router,
    expert_in,
    expert_out,
):
    own_low = tokens[0]
    inputs = own_low.astype(f32)
    tok_count, model_width = inputs.shape
    segment = segment_ids[0]
    length = segment.shape[0]
    seq_count = lax.axis_size("seq")
    exp_count = lax.axis_size("exp")
    core_count = lax.axis_size("fsdp")
    own_seq = lax.axis_index("seq")
    own_exp = lax.axis_index("exp")
    rows_dev = w_qkv.shape[0]
    heads_dev = HEADS // seq_count
    head_cols = heads_dev * HEAD_DIM
    experts_total = router.shape[1]
    exp_dev = expert_in.shape[1]

    small = jnp.concatenate([norm_gains, router], axis=1)
    small_cols = small.shape[1]
    ids_room = TOP * tok_count // (seq_count * rows_dev)
    small = jnp.pad(small, ((0, 0), (0, ids_room + -(small_cols + ids_room) % 128)))
    heads_rows = w_qkv.reshape(rows_dev, 3, seq_count, head_cols).transpose(2, 0, 1, 3)
    heads_rows = heads_rows.reshape(seq_count, rows_dev, 3 * head_cols)
    small = jnp.broadcast_to(small[None], (seq_count,) + small.shape)
    heads_seq = exchange(jnp.concatenate([heads_rows, small], axis=2), "seq")
    ids_low = expert_ids[0].astype(bf16).reshape(seq_count, rows_dev, -1)
    first_id = 3 * head_cols + small_cols
    ids_cols = ids_low.shape[2]
    after_ids = heads_seq.shape[2] - first_id - ids_cols
    heads_rows = heads_seq + jnp.pad(ids_low, ((0, 0), (0, 0), (first_id, after_ids)))
    cot_early = {
        k: lax.ppermute(cotangent[0], "exp", shift_pairs(exp_count, k))
        for k in range(1, exp_count)
        if k in EARLY
    }
    heads_near = gather_near(heads_rows.reshape(seq_count * rows_dev, -1), "exp")
    ids_group = jnp.stack(
        [near[:, first_id : first_id + ids_cols].reshape(tok_count, TOP) for near in heads_near]
    )
    heads_all = order_cores(heads_near, seq_count, "exp", "fsdp")
    heads_weight = heads_all[:, : 3 * head_cols]
    small = heads_all[:, 3 * head_cols : first_id].T
    gains = small[:4].astype(f32)
    router_rows = small[4:]
    out_rows = after(w_out, heads_seq)[None]
    out_rows = exchange(jnp.broadcast_to(out_rows, (seq_count,) + w_out.shape), "seq")
    out_rows = out_rows.reshape(seq_count * rows_dev, model_width)
    all_tokens = after(own_low, out_rows)[None]
    all_tokens = jnp.broadcast_to(all_tokens, (seq_count, tok_count, model_width))
    all_tokens = exchange(all_tokens, "seq").reshape(length, model_width)

    out_near = gather_near(after(out_rows, heads_near[-1]), "exp")

    parts = 1
    part_experts = exp_dev // parts
    sent = out_rows
    for near in cot_early.values():
        sent = after(sent[:16, :128], near)
    in_blocks = jnp.transpose(after(expert_in, sent), (1, 0, 2))
    down_blocks = jnp.transpose(after(expert_out, sent), (1, 0, 2))
    in_weights, down_weights = [], []
    for part in range(parts):
        chosen_experts = slice(part * part_experts, (part + 1) * part_experts)
        for blocks, weights in ((in_blocks, in_weights), (down_blocks, down_weights)):
            weights.append(
                lax.all_gather(blocks[chosen_experts], ("seq", "fsdp"), axis=1, tiled=True)
            )

    all_inputs = all_tokens.astype(f32)
    first_inverse = rms_inverse(all_inputs)
    attn_low = (all_inputs * first_inverse * gains[0]).astype(bf16)
    projected = jnp.dot(attn_low, heads_weight, preferred_element_type=f32)
    own_gains = lax.dynamic_slice_in_dim(gains, own_seq * head_cols, head_cols, 1)
    query_pre, key_pre = projected[:, :head_cols], projected[:, head_cols : 2 * head_cols]
    squares = jnp.stack([jnp.sum(query_pre * query_pre, axis=-1), jnp.sum(key_pre * key_pre, axis=-1)])
    squares = sum_all(squares, "seq")
    scales = lax.rsqrt(squares / model_width + epsilon).T
    turns = rotary_tables(jnp.arange(length, dtype=jnp.int32), HEAD_DIM)
    row_segment, col_segment = segment[:, None], segment[None, :]
    ready = scales
    for near in out_near[1:]:
        ready = after(ready, near)
    attended, queries, keys, values = attend(
        projected, ready, own_gains[1:3], turns, row_segment, col_segment, heads_dev
    )
    out_weight = order_cores(out_near, seq_count, "exp", "fsdp")
    merged = lax.all_to_all(attended, "seq", split_axis=0, concat_axis=1, tiled=True)
    branch = jnp.einsum("tc,dc->td", merged, out_weight, preferred_element_type=f32)
    residual = inputs + branch
    mlp_inverse = rms_inverse(residual)
    mlp_low = (residual * mlp_inverse * gains[3]).astype(bf16)

    capacity = tok_count * TOP // experts_total * 9 // 8
    near_experts = own_exp * exp_dev + jnp.arange(exp_dev, dtype=jnp.int32)
    chosen = jnp.any(
        ids_group[:, :, :, None] == near_experts.astype(bf16)[None, None, None, :], axis=2
    )
    earlier = (
        jnp.arange(tok_count)[:, None] > jnp.arange(tok_count)[None, :]
    ).astype(bf16)
    rank = jnp.einsum("tu,sue->est", earlier, chosen.astype(bf16), preferred_element_type=f32)
    rank = jnp.where(jnp.transpose(chosen, (2, 0, 1)), rank, -1.0)
    pick = rank[:, :, None, :] == jnp.arange(capacity, dtype=f32)[None, None, :, None]
    pick_low = pick.astype(bf16)
    turned = rank[:, :, :, None] == jnp.arange(capacity, dtype=f32)[None, None, None, :]
    turned_low = turned.astype(bf16)

    mlp_near = gather_near(mlp_low, "exp")
    late = cotangent[0]
    for near in mlp_near[1:]:
        late = after(late, near)
    cot_near = [cotangent[0]] + [
        cot_early[k] if k in cot_early else lax.ppermute(late, "exp", shift_pairs(exp_count, k))
        for k in range(1, exp_count)
    ]
    router_probs, gate_rows = route(own_exp * exp_dev, router_rows, pick_low, mlp_near)
    places = jnp.stack([ring_place(own_exp - k, exp_count) for k in range(exp_count)])
    kept = []
    for part in range(parts):
        kept = experts_forward(
            part * part_experts, kept, places.astype(jnp.int32), pick_low, turned_low, gate_rows,
            in_weights[part], down_weights[part], mlp_near,
        )
    expert_rows, gate, up, gated, mix = kept
    mix_near = exchange(mix, "exp")
    output = (residual + jnp.sum(mix_near.astype(f32), axis=0)).astype(bf16)

    cot_rows, down_grad = experts_down_grad(pick_low, gated, cot_near)
    grad_expert_out = lax.psum_scatter(
        down_grad, ("seq", "fsdp"), scatter_dimension=1, tiled=True
    )
    kept = []
    for part in range(parts):
        kept = experts_backward(
            part * part_experts, kept, turned_low, gate_rows, cot_rows, gate, up,
            in_weights[part], down_weights[part],
        )
    copy_near = send_near(kept[1:], "exp")
    before = jnp.stack([block[:16, :128] for block in kept[1:]])
    in_grad = experts_in_grad(expert_rows, kept[0], before)
    grad_expert_in = lax.psum_scatter(in_grad, ("seq", "fsdp"), scatter_dimension=1, tiled=True)
    copy_near[0] = after(after(copy_near[0], in_grad), mix_near)
    mlp_grad_experts = add_up([near[:, :model_width] for near in copy_near])
    prob_pairs = [
        near[:, model_width : model_width + 2 * exp_dev].astype(f32).reshape(tok_count, exp_dev, 2)
        for near in copy_near
    ]
    prob_grad = order([jnp.sum(pair, axis=2) for pair in prob_pairs], "exp", 1, 1)
    prob_grad = prob_grad.reshape(tok_count, experts_total)
    grad_expert_in = interleave([grad_expert_in])
    grad_expert_out = interleave([grad_expert_out])

    logit_grad = router_probs * (
        prob_grad - jnp.sum(router_probs * prob_grad, axis=-1, keepdims=True)
    )
    router_grad = jnp.dot(logit_grad.T, mlp_low.astype(f32), precision=highest)
    logit_high = logit_grad.astype(bf16)
    logit_low = (logit_grad - logit_high.astype(f32)).astype(bf16)
    mlp_grad = mlp_grad_experts + jnp.dot(
        jnp.concatenate([logit_high, logit_low], axis=1),
        jnp.concatenate([router_rows, router_rows], axis=0),
        preferred_element_type=f32,
    )
    residual_norm_grad, mlp_gain_grad = rms_back(mlp_grad, residual, mlp_inverse, gains[3])
    residual_grad = cotangent[0].astype(f32) + residual_norm_grad
    branch_grad = residual_grad.astype(bf16)

    merged_grad = jnp.einsum("td,dc->tc", branch_grad, out_weight, preferred_element_type=f32)
    heads_grad = lax.all_to_all(
        merged_grad.astype(bf16), "seq", split_axis=1, concat_axis=0, tiled=True
    )
    split_sizes = (seq_count, exp_count, core_count)
    out_terms = spread_product(
        branch_grad, merged, [], split_sizes, lax.axis_index("fsdp")
    )
    out_core = scatter_core(out_terms, "fsdp")
    out_sent = send_near(split(out_core, "exp"), "exp")
    out_terms = add_up(out_sent).astype(bf16)
    query_grad, key_grad, value_grad, inner = attend_back(
        queries, keys, values, heads_grad, projected, own_gains[1:3], turns, row_segment, col_segment,
        out_core[0, :16, :128], heads_dev,
    )
    means = sum_all(inner.T, "seq").T / model_width
    qkv_grad, head_gain_grads = norm_back(
        query_grad, key_grad, value_grad, projected, scales, means, own_gains[1:3]
    )
    query_gain_grad, key_gain_grad = head_gain_grads[0], head_gain_grads[1]

    zero_row = jnp.zeros((model_width,), f32)
    small_terms = jnp.concatenate(
        [
            jnp.stack(
                [
                    zero_row,
                    lax.dynamic_update_slice_in_dim(zero_row, query_gain_grad, own_seq * head_cols, 0),
                    lax.dynamic_update_slice_in_dim(zero_row, key_gain_grad, own_seq * head_cols, 0),
                    mlp_gain_grad,
                ]
            ),
            router_grad,
        ],
        axis=0,
    ).T
    small_terms = jnp.pad(small_terms, ((0, 0), (0, -small_cols % 128)))
    beside = [small_terms, heads_all, gains[0][:, None]]
    heads_terms = spread_product(
        attn_low, qkv_grad, beside, split_sizes, lax.axis_index("fsdp")
    )
    heads_terms = scatter_core(heads_terms, "fsdp", out_sent[1:])
    attn_in_part = jnp.einsum(
        "tc,dc->td", after(qkv_grad, heads_terms), heads_weight, preferred_element_type=f32
    )
    attn_in_grad = exchange(
        attn_in_part.astype(bf16).reshape(seq_count, tok_count, model_width), "seq"
    )
    attn_in_grad = jnp.sum(attn_in_grad.astype(f32), axis=0)
    heads_blocks = split(heads_terms, "exp")
    heads_blocks[0] = after(after(heads_blocks[0], grad_expert_in), grad_expert_out)
    heads_terms = add_up(send_near(heads_blocks, "exp")).astype(bf16)
    terms_cols = heads_terms.shape[1]
    last_terms = jnp.concatenate([heads_terms, out_terms], axis=1)
    last_near = send_near(split(last_terms.reshape(seq_count, rows_dev, -1), "seq"), "seq")
    grad_w_out = add_up([near[:, terms_cols:] for near in last_near])
    small_grad = add_up(
        [near[:, 3 * head_cols : 3 * head_cols + small_cols] for near in last_near]
    )
    heads_terms = order([near[:, : 3 * head_cols] for near in last_near], "seq", 0, 1)
    heads_terms = after(heads_terms, attn_in_grad)
    grad_w_qkv = jnp.concatenate(
        [
            heads_terms[source, :, part * head_cols : (part + 1) * head_cols]
            for part in range(3)
            for source in range(seq_count)
        ],
        axis=1,
    ).astype(f32)

    own_inverse = lax.dynamic_slice_in_dim(first_inverse, own_seq * tok_count, tok_count, 0)
    input_norm_grad, _ = rms_back(attn_in_grad, inputs, own_inverse, gains[0])
    input_grad = residual_grad + input_norm_grad

    return (
        output[None],
        input_grad[None],
        small_grad[:, :4],
        grad_w_qkv,
        grad_w_out,
        small_grad[:, 4:],
        grad_expert_in,
        grad_expert_out,
    )


def solution(mesh):
    in_specs = (
        P(("exp", "fsdp"), "seq", None),
        P(("exp", "fsdp"), "seq", None),
        P(("exp", "fsdp"), "seq", None),
        P(("exp", "fsdp"), None),
        P(("seq", "exp", "fsdp"), None),
        P(("seq", "exp", "fsdp"), None),
        P(("seq", "exp", "fsdp"), None),
        P(("seq", "exp", "fsdp"), None),
        P(("seq", "fsdp"), "exp", None),
        P(("seq", "fsdp"), "exp", None),
    )
    out_specs = (
        P(("exp", "fsdp"), "seq", None),
        P(("exp", "fsdp"), "seq", None),
        P(("seq", "exp", "fsdp"), None),
        P(("seq", "exp", "fsdp"), None),
        P(("seq", "exp", "fsdp"), None),
        P(("seq", "exp", "fsdp"), None),
        P(("seq", "fsdp"), "exp", None),
        P(("seq", "fsdp"), "exp", None),
    )
    return jax.shard_map(
        on_device, mesh=mesh, in_specs=in_specs, out_specs=out_specs, check_vma=False
    )
```
